32 devices in a mesh: section: 2 (over x), dp: 16 (over z, y, core).
Axes of the slice: x: 2, y: 2, z: 4, core: 2. Of those that a mesh axis runs over, the one named last changes fastest.
Arguments:
- patches: bfloat16 [16384, 768], P('dp'), may hold values from -6 to 6
- targets: bfloat16 [16384, 768], P('dp'), may hold values from -6 to 6
- code_ids: int32 [16384], P('dp'), may hold values from 0 to 3199
- codebook: bfloat16 [3200, 768], P('dp'), may hold values from -6 to 6
- norm_gains: float32 [2, 2, 768], P('section'), may hold values from 0.25 to 1.75
- norm_shifts: float32 [2, 2, 768], P('section'), may hold values from -4 to 4
- w_qkv: bfloat16 [2, 768, 2304], P('section'), may hold values from -0.21875 to 0.21875
- w_out: bfloat16 [2, 768, 768], P('section'), may hold values from -0.875 to 0.875
- out_bias: float32 [2, 768], P('section'), may hold values from -4 to 4
- w_up: bfloat16 [2, 768, 3072], P('section'), may hold values from -0.21875 to 0.21875
- up_bias: float32 [2, 3072], P('section'), may hold values from -6 to 6
- w_down: bfloat16 [2, 3072, 768], P('section'), may hold values from -0.109375 to 0.109375
- down_bias: float32 [2, 768], P('section'), may hold values from -4 to 4
Outputs:
- block_out: bfloat16 [2, 16384, 768], P('section', 'dp')
- input_grad: float32 [2, 16384, 768], P('section', 'dp')
- g_norm_gains: float32 [2, 2, 768], P('section')
- g_norm_shifts: float32 [2, 2, 768], P('section')
- g_qkv: float32 [2, 768, 2304], P('section', 'dp')
- g_out: float32 [2, 768, 768], P('section', 'dp')
- g_out_bias: float32 [2, 768], P('section')
- g_up: float32 [2, 768, 3072], P('section', 'dp')
- g_up_bias: float32 [2, 3072], P('section')
- g_down: float32 [2, 3072, 768], P('section', 'dp')
- g_down_bias: float32 [2, 768], P('section')
- histogram: int32 [3200], P('dp')
- stats: float32 [3], replicated
The draws below stay inside these ranges and needn't reach their ends.
Inputs may be any that keep to these rules, and one draw needn't show every extreme that they name: `code_ids`: each patch's chosen codebook row.
All inputs are finite; a program needn't handle non-finite values.
Results may differ from the reference program's by a relative error of at most 0.011.
Values may be sent and summed in bfloat16 or wider, within the bound.
A program may use at most 256 MiB of HBM per device.

```python
import math
import jax
import jax.numpy as jnp
import numpy as np
from jax import lax

D = 768
HEADS = 12
HD = 64
FF = 3072
SEQ = 256
TOKENS = 16384
VOCAB = 3200


def plant(drawn, rng, low, top_value):
    shape = drawn.shape
    place = [jax.random.randint(jax.random.fold_in(rng, axis), (), 0, shape[axis]) for axis in range(len(shape))]
    drawn = drawn.at[tuple(place)].set(low)
    longest = shape.index(max(shape))
    place[longest] = (place[longest] + 1) % shape[longest]
    return drawn.at[tuple(place)].set(top_value)


def raised(array, key, source, target, parts, factor):
    owner, partner = [(jnp.arange(array.shape[dim]) // (array.shape[dim] // parts)).reshape([-1 if axis == dim else 1 for axis in range(array.ndim)]) for dim in (source, target)]
    chosen = jax.random.permutation(key, parts)[partner]
    strong = (owner == chosen) | (owner == (partner + parts // 2) % parts)
    return jnp.where(strong, factor * array, array)


def block_scale(key, extent, split, low, largest):
    def one(position, shards_of):
        draws = jax.random.uniform(jax.random.fold_in(jax.random.fold_in(key, 6), position), (shards_of,), jnp.float32, low / len(split), largest / len(split))
        return jnp.repeat(jnp.exp(draws), extent[position] // shards_of).reshape((-1,) + (1,) * (len(extent) - position - 1))

    loudness = one(*split[0])
    for cut in split[1:]:
        loudness = loudness * one(*cut)
    return loudness


def rank_bounds(amount, skew):
    weights = [(1 << 20) // math.isqrt(grade ** skew) + 1 for grade in range(1, amount + 1)]
    spread = 1 + sum(weights) // (1 << 30)
    return np.cumsum(np.array([max(1, weight // spread) for weight in weights]))


def ranked(stream_key, extent, number_of, slope):
    table = rank_bounds(number_of, slope)
    pick = jax.random.randint(jax.random.fold_in(stream_key, 1), extent, 0, int(table[number_of - 1]))
    standing = jnp.searchsorted(jnp.asarray(table, jnp.int32), pick, side="right")
    return jax.random.permutation(jax.random.fold_in(stream_key, 2), number_of)[standing].astype(jnp.int32)


def normal_values(stream_key, dims, spread, most, cuts=(), dtype=jnp.bfloat16):
    level = block_scale(stream_key, dims, cuts, -0.22, 0.18) if cuts else 1.0
    result = jax.random.normal(stream_key, dims, jnp.float32) * spread * level
    return jnp.minimum(jnp.maximum(result, -most), most).astype(dtype)


def bell_draw_with(key, shape, scale, bound, split, heavy, held_as=jnp.bfloat16):
    array = scale * jax.random.normal(key, shape, jnp.float32)
    if split:
        array = array * block_scale(key, shape, split, -0.22, 0.18)
    return jnp.clip(raised(array, jax.random.fold_in(key, 3), *heavy), -bound, bound).astype(held_as)


def setup_inputs(seed: int = 0) -> dict:
    key_list = jax.random.split(jax.random.key(seed), 14)
    return {
        "patches": bell_draw_with(key_list[0], (TOKENS, D), 1.0, 6.0, ((0, 16),), (0, 1, 16, 2.0)),
        "targets": normal_values(key_list[1], (TOKENS, D), 1.0, 6.0, ((0, 16),)),
        "code_ids": plant(ranked(key_list[2], (TOKENS,), VOCAB, 2), jax.random.fold_in(key_list[2], 3), 0, VOCAB - 1).astype(jnp.int32),
        "codebook": normal_values(key_list[3], (VOCAB, D), 1.0, 6.0, ((0, 16),)),
        "norm_gains": jnp.clip(1.0 + 0.15 * jax.random.normal(key_list[4], (2, 2, D), jnp.float32), 0.25, 1.75),
        "norm_shifts": normal_values(key_list[5], (2, 2, D), 0.3, 4.0, ((0, 2),), jnp.float32),
        "w_qkv": normal_values(key_list[6], (2, D, 3 * D), D ** -0.5, 0.21875, ((0, 2),)),
        "w_out": normal_values(key_list[7], (2, D, D), (D // 16) ** -0.5, 0.875, ((0, 2),)),
        "out_bias": normal_values(key_list[8], (2, D), 0.3, 4.0, ((0, 2),), jnp.float32),
        "w_up": normal_values(key_list[9], (2, D, FF), D ** -0.5, 0.21875, ((0, 2),)),
        "up_bias": normal_values(key_list[10], (2, FF), 0.5, 6.0, ((0, 2),), jnp.float32),
        "w_down": normal_values(key_list[11], (2, FF, D), FF ** -0.5, 0.109375, ((0, 2),)),
        "down_bias": normal_values(key_list[12], (2, D), 0.3, 4.0, ((0, 2),), jnp.float32),
    }


@jax.custom_vjp
def low(v):
    return lax.optimization_barrier(v.astype(jnp.bfloat16)).astype(jnp.float32)

@jax.custom_vjp
def low_back(v):
    return v

def low_keep(v):
    return (low(v), None)

def low_pass(kept, grad):
    return (grad,)

def back_keep(v):
    return (v, None)

def back_low(kept, grad):
    return (low(grad),)
low.defvjp(low_keep, low_pass)
low_back.defvjp(back_keep, back_low)
COMMIT_WEIGHT = 0.25
EPSILON = 1e-06
HIGHEST = lax.Precision.HIGHEST

def product(left, right):
    return jnp.dot(left, right, precision=HIGHEST)

def normed(rows_in, gain_row, shift_row):
    average = lax.optimization_barrier(jnp.mean(rows_in, axis=-1, keepdims=True))
    centered = rows_in - average
    variance = lax.optimization_barrier(jnp.mean(centered * centered, axis=-1, keepdims=True))
    return centered * lax.rsqrt(variance + EPSILON) * gain_row + shift_row

def attend_one(triple):
    queries, key_rows, value_rows = triple
    scores = low_back(jnp.einsum('qhd,khd->hqk', queries, key_rows, precision=HIGHEST) * HD ** (-0.5))
    peak_score = lax.optimization_barrier(jnp.max(scores, axis=-1, keepdims=True))
    exponent = jnp.exp(scores - peak_score)
    shares = low(exponent / lax.optimization_barrier(jnp.sum(exponent, axis=-1, keepdims=True)))
    return jnp.einsum('hqk,khd->qhd', shares, value_rows, precision=HIGHEST)

def residual_block(rows_in, gain_rows, shift_rows, w_qkv, w_out, out_bias, w_up, up_bias, w_down, down_bias):
    row_count = rows_in.shape[0]
    normal_a = low(normed(rows_in, gain_rows[0], shift_rows[0]))
    projected = low_back(low(product(normal_a, w_qkv)))
    projected = projected.reshape(row_count // SEQ, SEQ, 3, HEADS, HD)
    attended = lax.map(jax.checkpoint(attend_one), (projected[:, :, 0], projected[:, :, 1], projected[:, :, 2]))
    attended = low_back(low(attended.reshape(row_count, HEADS * HD)))
    hidden_one = rows_in + low_back(product(attended, w_out)) + out_bias
    normal_b = low(normed(hidden_one, gain_rows[1], shift_rows[1]))
    preact = low_back(product(normal_b, w_up) + up_bias)
    activated = low(0.5 * preact * (1.0 + lax.erf(preact * 0.5 ** 0.5)))
    return hidden_one + low_back(product(activated, w_down)) + down_bias

def section_params(float_params, index):
    return tuple((param[index] for param in float_params))

def reference(patches, targets, code_ids, codebook, norm_gains, norm_shifts, w_qkv, w_out, out_bias, w_up, up_bias, w_down, down_bias):
    float_params = tuple((param.astype(jnp.float32) for param in (norm_gains, norm_shifts, w_qkv, w_out, out_bias, w_up, up_bias, w_down, down_bias)))
    inputs = patches.astype(jnp.float32)
    target_rows = targets.astype(jnp.float32)
    chosen = jnp.take(codebook, code_ids, axis=0).astype(jnp.float32)
    fixed_code = residual_block(inputs, *section_params(float_params, 0))

    def objective(inputs, probe, params):
        encoded = residual_block(inputs, *section_params(params, 0))
        quantized = low_back(low(encoded + (chosen - fixed_code))) + probe
        decoded = residual_block(quantized, *section_params(params, 1))
        recon_sum = jnp.sum((decoded - target_rows) ** 2)
        commit_sum = jnp.sum((encoded - chosen) ** 2)
        return (0.5 * recon_sum + 0.5 * COMMIT_WEIGHT * commit_sum, (encoded, decoded, recon_sum + COMMIT_WEIGHT * commit_sum))
    loss_value, pullback, extras = jax.vjp(objective, inputs, jnp.zeros_like(inputs), float_params, has_aux=True)
    encoded, decoded, both_sums = extras
    grad_inputs, grad_probe, grad_params = pullback(jnp.ones((), jnp.float32))
    counts = jnp.zeros((VOCAB,), jnp.float32).at[code_ids].add(1.0)
    shares = counts / TOKENS
    nonzero_share = jnp.where(counts > 0, shares, 1.0)
    entropy = -jnp.sum(shares * jnp.log(nonzero_share))
    usage = jnp.sum((counts > 0).astype(jnp.float32)) / VOCAB
    stats = jnp.stack([both_sums / (TOKENS * D), usage, jnp.exp(entropy) / VOCAB])
    block_out = jnp.stack([encoded, decoded]).astype(jnp.bfloat16)
    input_grad = jnp.stack([grad_inputs, grad_probe])
    return (block_out, input_grad, grad_params[0], grad_params[1], grad_params[2], grad_params[3], grad_params[4], grad_params[5], grad_params[6], grad_params[7], grad_params[8], counts.astype(jnp.int32), stats)
```

```python
import functools

import jax
import jax.numpy as jnp
from jax import lax
from jax.experimental import pallas as pl
from jax.experimental.pallas import tpu as pltpu
from jax.sharding import PartitionSpec as P

SEQ = 256
D = 768
HD = 64
HEADS = 12
FF = 3072
FF_PIECE = 768
QKV = 3 * D
L_O, L_A, L_M, L_ALL = D, 2 * D, 3 * D, 3 * D + FF
D_GH, D_QKV, D_GB, D_ALL = FF, FF + D, FF + D + QKV, FF + D + QKV + D
V_COUNT, V_LOSS, V_ROWS = 10, 15, 16
COUNT_ROWS = V_LOSS - V_COUNT

COMMIT_WEIGHT = 0.25
EPSILON = 1e-06
SQRT_HALF = 0.5**0.5
INV_ROOT_TAU = 0.3989422804014327
HEAD_SCALE = HD**-0.5
MESH = pl.DeviceIdType.MESH
BF, F32 = jnp.bfloat16, jnp.float32
VMEM_BYTES = 60 << 20


def matmul_nn(left, right):
    return jnp.dot(left, right, preferred_element_type=F32)


def matmul_nt(left, right):
    return lax.dot_general(left, right, (((1,), (1,)), ((), ())), preferred_element_type=F32)


def matmul_tn(left, right):
    return lax.dot_general(left, right, (((0,), (0,)), ((), ())), preferred_element_type=F32)


def layer_norm(rows_in):
    centered = rows_in - jnp.mean(rows_in, axis=-1, keepdims=True)
    inv_std = lax.rsqrt(jnp.mean(centered * centered, axis=-1, keepdims=True) + EPSILON)
    return centered * inv_std, inv_std


def norm_back(incoming, scaled, inv_std, gain_row):
    x = incoming * gain_row
    return inv_std * (
        x
        - jnp.mean(x, axis=-1, keepdims=True)
        - scaled * jnp.mean(x * scaled, axis=-1, keepdims=True)
    )


def column_sum(x):
    return jnp.sum(x, axis=0, keepdims=True)


def head_masks():
    low = lax.broadcasted_iota(jnp.int32, (SEQ, 2 * HD), 1) < HD
    return (lambda t: jnp.where(low, t, 0)), (lambda t: jnp.where(low, 0, t))


def forward_image(x_ref, weights, l_ref, qkv_ref, pt_ref, slope_ref, h1_ref, out_ref, outb_ref, vt_ref, ot_ref):
    gains, shifts, w_qkv, w_out, out_bias, w_up, up_bias, w_down, down_bias = weights
    h = x_ref[...].astype(F32)
    s1, _ = layer_norm(h)
    a = (s1 * gains[0:1, :] + shifts[0:1, :]).astype(BF)
    l_ref[:, L_A:L_M] = a
    for j in range(3):
        qkv_ref[:, j * D : (j + 1) * D] = matmul_nn(a, w_qkv[:, j * D : (j + 1) * D]).astype(BF)
    vt_ref[...] = qkv_ref[:, 2 * D : 3 * D].T
    masks = head_masks()
    for pair in range(HEADS // 2):
        q = qkv_ref[:, pair * 128 : (pair + 1) * 128]
        k = qkv_ref[:, D + pair * 128 : D + (pair + 1) * 128]
        for half in range(2):
            head = 2 * pair + half
            st = matmul_nt(masks[half](k), q)
            e = jnp.exp((st - jnp.max(st, axis=0, keepdims=True)) * HEAD_SCALE)
            pt = (e * (1.0 / column_sum(e))).astype(BF)
            pt_ref[head] = pt
            span = slice(head * HD, (head + 1) * HD)
            ot_ref[span, :] = matmul_nn(vt_ref[span, :], pt).astype(BF)
    o = ot_ref[...].T
    l_ref[:, L_O:L_A] = o
    h1 = h + matmul_nn(o, w_out[...]) + out_bias[...]
    h1_ref[...] = h1
    s2, _ = layer_norm(h1)
    b = (s2 * gains[1:2, :] + shifts[1:2, :]).astype(BF)
    l_ref[:, 0:L_O] = b
    result = h1 + down_bias[...]
    for j in range(FF // FF_PIECE):
        span = slice(j * FF_PIECE, (j + 1) * FF_PIECE)
        u = matmul_nn(b, w_up[:, span]) + up_bias[:, span]
        half_curve = 0.5 + 0.5 * lax.erf(u * SQRT_HALF)
        m = (u * half_curve).astype(BF)
        l_ref[:, L_M + j * FF_PIECE : L_M + (j + 1) * FF_PIECE] = m
        slope = half_curve + u * jnp.exp(-0.5 * u * u) * INV_ROOT_TAU
        slope_ref[:, span] = slope.astype(slope_ref.dtype)
        result = result + matmul_nn(m, w_down[span, :])
    out_ref[...] = result
    outb_ref[...] = result.astype(BF)


def backward_image(
    scale, out_ref, other_ref, arrived_ref, x_ref, weights, qkv_ref, pt_ref, slope_ref, h1_ref,
    d_ref, vec_ref, dh_ref, dhb_ref, kt_ref, qt_ref,
):
    gains, shifts, w_qkv, w_out, out_bias, w_up, up_bias, w_down, down_bias = weights
    diff = out_ref[...] - other_ref[...].astype(F32)
    vec_ref[V_LOSS : V_LOSS + 1, :] = column_sum(diff * diff) * scale
    vec_ref[V_COUNT:V_LOSS, :] = jnp.zeros((COUNT_ROWS, D), F32)
    g = diff * scale + arrived_ref[...].astype(F32)
    gb = g.astype(BF)
    d_ref[:, D_GB:D_ALL] = gb
    vec_ref[9:10, :] = column_sum(g)
    db = jnp.zeros((SEQ, D), F32)
    for j in range(FF // FF_PIECE):
        span = slice(j * FF_PIECE, (j + 1) * FF_PIECE)
        du = (matmul_nt(gb, w_down[span, :]) * slope_ref[:, span].astype(F32)).astype(BF)
        d_ref[:, span] = du
        vec_ref[5 + j : 6 + j, :] = column_sum(du.astype(F32))
        db = db + matmul_nt(du, w_up[:, span])
    s2, inv2 = layer_norm(h1_ref[...])
    vec_ref[1:2, :] = column_sum(db * s2)
    vec_ref[3:4, :] = column_sum(db)
    dh1 = g + norm_back(db, s2, inv2, gains[1:2, :])
    vec_ref[4:5, :] = column_sum(dh1)
    gh = dh1.astype(BF)
    d_ref[:, D_GH:D_QKV] = gh
    do = matmul_nt(gh, w_out[...]).astype(BF)
    kt_ref[...] = qkv_ref[:, D : 2 * D].T
    masks = head_masks()
    for pair in range(HEADS // 2):
        lanes = slice(pair * 128, (pair + 1) * 128)
        q = qkv_ref[:, lanes]
        v = qkv_ref[:, 2 * D + pair * 128 : 2 * D + (pair + 1) * 128]
        do_pair = do[:, lanes]
        dk = dv = 0.0
        for half in range(2):
            head = 2 * pair + half
            pt = pt_ref[head]
            ptf = pt.astype(F32)
            dv = dv + matmul_nn(pt, masks[half](do_pair))
            dpt = matmul_nt(masks[half](v), do_pair)
            dst = (ptf * (dpt - column_sum(dpt * ptf))).astype(BF)
            dk = dk + matmul_nn(dst, masks[half](q))
            span = slice(head * HD, (head + 1) * HD)
            qt_ref[span, :] = (matmul_nn(kt_ref[span, :], dst) * HEAD_SCALE).astype(BF)
        base = D_QKV + D + pair * 128
        d_ref[:, base : base + 128] = (dk * HEAD_SCALE).astype(BF)
        d_ref[:, base + D : base + D + 128] = dv.astype(BF)
    d_ref[:, D_QKV : D_QKV + D] = qt_ref[...].T
    da = matmul_nt(d_ref[:, D_QKV:D_GB], w_qkv[...])
    s1, inv1 = layer_norm(x_ref[...].astype(F32))
    vec_ref[0:1, :] = column_sum(da * s1)
    vec_ref[2:3, :] = column_sum(da)
    dh = dh1 + norm_back(da, s1, inv1, gains[0:1, :])
    dh_ref[...] = dh
    dhb_ref[...] = dh.astype(BF)


WEIGHT_SHAPES = ((2, D), (2, D), (D, QKV), (D, D), (1, D), (D, FF), (1, FF), (FF, D), (1, D))


def weight_specs():
    def whole(shape):
        return pl.BlockSpec(shape, lambda *_: (0, 0), pipeline_mode=pl.Buffered(1))

    return [whole(shape) for shape in WEIGHT_SHAPES]


def block_forward(x, weights):
    rows = x.shape[0]
    images = rows // SEQ

    def row_block(width):
        return pl.BlockSpec((SEQ, width), lambda i: (i, 0))

    def body(x_ref, *refs):
        forward_image(x_ref, refs[:9], *refs[9:])

    def shape(width, dtype):
        return jax.ShapeDtypeStruct((rows, width), dtype)

    return pl.pallas_call(
        body,
        grid=(images,),
        in_specs=[row_block(D)] + weight_specs(),
        out_specs=[
            row_block(L_ALL),
            row_block(QKV),
            pl.BlockSpec((HEADS, SEQ, SEQ), lambda i: (i, 0, 0)),
            row_block(FF),
            row_block(D),
            row_block(D),
            row_block(D),
        ],
        out_shape=[
            shape(L_ALL, BF),
            shape(QKV, BF),
            jax.ShapeDtypeStruct((images * HEADS, SEQ, SEQ), BF),
            shape(FF, BF),
            shape(D, F32),
            shape(D, F32),
            shape(D, BF),
        ],
        scratch_shapes=[pltpu.VMEM((D, SEQ), BF), pltpu.VMEM((D, SEQ), BF)],
        compiler_params=pltpu.CompilerParams(vmem_limit_bytes=VMEM_BYTES),
        name="block_forward",
    )(x, *weights)


def block_backward(which, flags, result, other, arrived, x, weights, qkv, pt, slope, h1, vec, d, dh):
    rows = x.shape[0]

    def row_block(width):
        return pl.BlockSpec((SEQ, width), lambda i, which_ref: (which_ref[0], 0))

    def whole(height, width):
        return pl.BlockSpec((height, width), lambda i, which_ref: (0, 0))

    def body(which_ref, flags_ref, out_ref, other_ref, arrived_ref, x_ref, *refs):
        weight_refs = refs[:9]
        qkv_ref, pt_ref, slope_ref, h1_ref, vec_in = refs[9:14]
        d_ref, dh_ref, vec_out, dhb_ref, kt_ref, qt_ref = refs[-6:]
        backward_image(
            flags_ref[0], out_ref, other_ref, arrived_ref, x_ref, weight_refs, qkv_ref, pt_ref,
            slope_ref, h1_ref, d_ref, vec_out, dh_ref, dhb_ref, kt_ref, qt_ref,
        )
        vec_out[...] = vec_in[...] + vec_out[...] * flags_ref[1]

    keep = [] if d is None else [d, dh]
    first_kept = 2 + 4 + 9 + 5
    return pl.pallas_call(
        body,
        grid_spec=pltpu.PrefetchScalarGridSpec(
            num_scalar_prefetch=1,
            grid=(1,),
            in_specs=[pl.BlockSpec(memory_space=pltpu.SMEM), row_block(D), row_block(D), whole(SEQ, D), row_block(D)]
            + weight_specs()
            + [
                row_block(QKV),
                pl.BlockSpec((HEADS, SEQ, SEQ), lambda i, which_ref: (which_ref[0], 0, 0)),
                row_block(FF),
                row_block(D),
                whole(V_ROWS, D),
            ]
            + [pl.BlockSpec(memory_space=pl.ANY)] * len(keep),
            out_specs=[row_block(D_ALL), row_block(D), whole(V_ROWS, D), whole(SEQ, D)],
            scratch_shapes=[pltpu.VMEM((D, SEQ), BF), pltpu.VMEM((D, SEQ), BF)],
        ),
        out_shape=[
            jax.ShapeDtypeStruct((rows, D_ALL), BF),
            jax.ShapeDtypeStruct((rows, D), F32),
            jax.ShapeDtypeStruct((V_ROWS, D), F32),
            jax.ShapeDtypeStruct((SEQ, D), BF),
        ],
        input_output_aliases={first_kept: 0, first_kept + 1: 1} if keep else {},
        compiler_params=pltpu.CompilerParams(vmem_limit_bytes=VMEM_BYTES),
        name="block_backward",
    )(which, flags, result, other, arrived, x, *weights, qkv, pt, slope, h1, vec, *keep)


UNITS = 36
PART = D // 16
COLS = 256
LAG_Y, LAG_Z, LAG_OUT = 1, 3, 5
PIECE = 384


def reduce_kernel(
    l_ref, d_ref, vec_ref, qkv_out, out_out, up_out, down_out, vec_out, side_out,
    lt, lbuf, dbuf, acc_y, acc_z, acc_o, tx_c, rx_c, tx_y, rx_y, tx_z, rx_z, vec_tx, vec_c, vec_y, vec_z,
    lsem, dsem, sc, rc, sy, ry, sz, rz, sv, rv,
):
    sec, dp = lax.axis_index("section"), lax.axis_index("dp")
    core, y, z = dp % 2, (dp // 2) % 2, dp // 4
    across = (sec, dp + 1 - 2 * core)
    along_y = (sec, dp + 2 - 4 * y)
    along_z = [(sec, (z + k) % 4 * 4 + y * 2 + core) for k in (1, 2, 3)]
    beside = (1 - sec, dp)
    barrier = pltpu.get_barrier_semaphore()
    for target in [across, along_y, beside] + along_z:
        pl.semaphore_signal(barrier, inc=1, device_id=target, device_id_type=MESH)
    pl.semaphore_wait(barrier, 6)

    def remote(src, dst, send, recv, target):
        return pltpu.make_async_remote_copy(src, dst, send, recv, device_id=target, device_id_type=MESH)

    def spot(g):
        return ((g % 2 + core) % 2) * 8 + (((g // 2) % 2 + y) % 2) * 4 + (g // 4 - z + 4) % 4

    def aligned(x, n):
        return pl.multiple_of(x, n)

    def load_left(i):
        return pltpu.make_async_copy(l_ref.at[:, pl.ds(aligned(i * PIECE, PIECE), PIECE)], lbuf.at[i % 2], lsem.at[i % 2])

    def load_right(u):
        d = jnp.where(u < 24, u, 24 + u % 3)
        return pltpu.make_async_copy(d_ref.at[:, pl.ds(aligned(d * COLS, COLS), COLS)], dbuf.at[u % 2], dsem.at[u % 2])

    def prepare(i):
        load_left(i).wait()

        @pl.when(i < 13)
        def _():
            load_left(i + 1).start()

        turned = lbuf[i % 2].T

        @pl.when(i < 6)
        def _():
            for k in range(8):
                place = spot((i % 2) * 8 + k) * PART
                lt[i // 2, pl.ds(aligned(place, PART), PART), :] = turned[k * PART : (k + 1) * PART]

        @pl.when(i >= 6)
        def _():
            for k in range(8):
                place = spot((i - 6) * 2 + k // 4) * PART
                lt[3 + k % 4, pl.ds(aligned(place, PART), PART), :] = turned[k * PART : (k + 1) * PART]

    def send_core(u):
        return remote(tx_c.at[u], rx_c.at[u], sc.at[u], rc.at[u], across)

    def send_y(u):
        return remote(tx_y.at[u], rx_y.at[u], sy.at[u], ry.at[u], along_y)

    def send_z(u, k):
        return remote(tx_z.at[u, k], rx_z.at[u, k], sz.at[u, k], rz.at[u, k], along_z[k])

    vec_core = remote(vec_ref, vec_c, sv.at[0], rv.at[0], across)
    vec_along_y = remote(vec_tx, vec_y, sv.at[1], rv.at[1], along_y)
    vec_along_z = [remote(vec_z.at[z], vec_z.at[z], sv.at[2 + k], rv.at[2 + k], along_z[k]) for k in range(3)]
    vec_beside = remote(vec_out.at[8:16], side_out, sv.at[5], rv.at[5], beside)

    load_left(0).start()
    load_right(0).start()
    prepare(0)
    prepare(1)
    vec_core.start()

    def step(i, carry):
        @pl.when(i < UNITS)
        def _():
            u = i

            @pl.when(u + 1 < UNITS)
            def _():
                load_right(u + 1).start()

            load_right(u).wait()
            l = jnp.where(u < 12, 0, jnp.where(u < 15, 1, jnp.where(u < 24, 2, 3 + (u - 24) // 3)))
            product = matmul_nn(lt[l], dbuf[u % 2])
            acc_y[u % 2] = product[: 8 * PART]
            tx_c[u] = product[8 * PART :].astype(BF)
            send_core(u).start()

        @pl.when((i >= LAG_Y) & (i < UNITS + LAG_Y))
        def _():
            u = i - LAG_Y
            send_core(u).wait()
            t = acc_y[u % 2] + rx_c[u].astype(F32)
            acc_z[u % 4] = t[: 4 * PART]
            tx_y[u] = t[4 * PART :].astype(BF)
            send_y(u).start()

        @pl.when((i >= LAG_Z) & (i < UNITS + LAG_Z))
        def _():
            u = i - LAG_Z
            send_y(u).wait()
            t = acc_z[u % 4] + rx_y[u].astype(F32)
            acc_o[u % 4] = t[:PART]
            for k in range(3):
                tx_z[u, k] = t[PART * (k + 1) : PART * (k + 2)].astype(BF)
                send_z(u, k).start()

        @pl.when(i >= LAG_OUT)
        def _():
            u = i - LAG_OUT
            t = acc_o[u % 4]
            for k in range(3):
                send_z(u, k).wait()
                t = t + rx_z[u, k].astype(F32)

            def lanes(n):
                return pl.ds(aligned(n * COLS, COLS), COLS)

            @pl.when(u < 12)
            def _():
                up_out[:, lanes(u)] = t

            @pl.when((u >= 12) & (u < 15))
            def _():
                out_out[:, lanes(u - 12)] = t

            @pl.when((u >= 15) & (u < 24))
            def _():
                qkv_out[:, lanes(u - 15)] = t

            @pl.when(u >= 24)
            def _():
                down_out[pl.ds(aligned((u - 24) // 3 * PART, PART), PART), lanes(u % 3)] = t

        @pl.when(i < 12)
        def _():
            prepare(i + 2)

        @pl.when(i == 3)
        def _():
            vec_core.wait()
            vec_tx[...] = vec_ref[...] + vec_c[...]
            vec_along_y.start()

        @pl.when(i == 8)
        def _():
            vec_along_y.wait()
            vec_z[z] = vec_tx[...] + vec_y[...]
            for copy in vec_along_z:
                copy.start()

        @pl.when(i == 14)
        def _():
            for copy in vec_along_z:
                copy.wait()
            vec_out[...] = (vec_z[0] + vec_z[1]) + (vec_z[2] + vec_z[3])
            vec_beside.start()

        return carry

    lax.fori_loop(0, UNITS + LAG_OUT, step, 0)
    vec_beside.wait()


def reduce_weights(l, d, vec):
    dma = pltpu.SemaphoreType.DMA
    vm = pltpu.VMEM
    return pl.pallas_call(
        reduce_kernel,
        out_shape=[
            jax.ShapeDtypeStruct((PART, QKV), F32),
            jax.ShapeDtypeStruct((PART, D), F32),
            jax.ShapeDtypeStruct((PART, FF), F32),
            jax.ShapeDtypeStruct((4 * PART, D), F32),
            jax.ShapeDtypeStruct((V_ROWS, D), F32),
            jax.ShapeDtypeStruct((8, D), F32),
        ],
        in_specs=[pl.BlockSpec(memory_space=pl.ANY)] * 2 + [pl.BlockSpec(memory_space=pltpu.VMEM)],
        out_specs=[pl.BlockSpec(memory_space=pltpu.VMEM)] * 6,
        scratch_shapes=[
            vm((7, D, 4 * SEQ), BF), vm((2, 4 * SEQ, PIECE), BF), vm((2, 4 * SEQ, COLS), BF),
            vm((2, 8 * PART, COLS), F32), vm((4, 4 * PART, COLS), F32), vm((4, PART, COLS), F32),
            vm((UNITS, 8 * PART, COLS), BF), vm((UNITS, 8 * PART, COLS), BF),
            vm((UNITS, 4 * PART, COLS), BF), vm((UNITS, 4 * PART, COLS), BF),
            vm((UNITS, 3, PART, COLS), BF), vm((UNITS, 3, PART, COLS), BF),
            vm((V_ROWS, D), F32), vm((V_ROWS, D), F32), vm((V_ROWS, D), F32), vm((4, V_ROWS, D), F32),
            dma((2,)), dma((2,)), dma((UNITS,)), dma((UNITS,)), dma((UNITS,)), dma((UNITS,)),
            dma((UNITS, 3)), dma((UNITS, 3)), dma((6,)), dma((6,)),
        ],
        compiler_params=pltpu.CompilerParams(collective_id=1, has_side_effects=True, vmem_limit_bytes=VMEM_BYTES),
        name="weight_grad_reduce",
    )(l, d, vec)


def count_shares(counts, total_count):
    shares = counts / total_count
    nonzero_share = jnp.where(counts > 0, shares, 1.0)
    return -jnp.sum(shares * jnp.log(nonzero_share)), jnp.sum((counts > 0).astype(F32))


def on_device(
    patches, targets, code_ids, codebook, norm_gains, norm_shifts, w_qkv, w_out, out_bias, w_up, up_bias, w_down, down_bias
):
    section = lax.axis_index("section")
    leading = section == 0
    dp_size = lax.axis_size("dp")
    dp = lax.axis_index("dp")
    weights = (
        norm_gains[0], norm_shifts[0], w_qkv[0], w_out[0], out_bias, w_up[0], up_bias, w_down[0], down_bias
    )
    rows, width = patches.shape
    images = rows // SEQ
    vocab_local = codebook.shape[0]
    vocab_all = vocab_local * dp_size
    total_tokens = rows * dp_size

    shard_rows = lax.all_gather(codebook, "dp", axis=0, tiled=True)
    chosen = jnp.take(shard_rows, jnp.clip(code_ids, 0, vocab_all - 1), axis=0)

    l, qkv, pt, slope, h1, result, result_bf = block_forward(jnp.where(leading, patches, chosen), weights)

    other = jnp.where(leading, chosen, targets)
    d = dh = None
    vec = jnp.zeros((V_ROWS, D), F32)
    arrived = jnp.zeros((SEQ, D), BF)
    x = jnp.where(leading, patches, chosen)
    for moment in range(images + 1):
        which = jnp.clip(moment - 1 + section, 0, images - 1).astype(jnp.int32)[None]
        active = jnp.where(leading, moment >= 1, moment < images).astype(F32)
        flags = jnp.stack([jnp.where(leading, COMMIT_WEIGHT, 1.0).astype(F32), active])
        d, dh, vec, outgoing = block_backward(
            which, flags, result, other, arrived, x, weights, qkv, pt, slope, h1, vec, d, dh
        )
        if moment < images:
            arrived = lax.ppermute(outgoing, "section", [(1, 0)])

    vocab_iota = lax.broadcasted_iota(jnp.int32, (1, vocab_all), 1)
    counts = jnp.sum((code_ids[:, None] == vocab_iota).astype(F32), axis=0)
    small = dp_size == 16 and vocab_all <= COUNT_ROWS * D and rows == 4 * SEQ
    if small:
        spread = jnp.pad(counts, (0, COUNT_ROWS * D - vocab_all)).reshape(COUNT_ROWS, D)
        vec = lax.dynamic_update_slice(vec, spread, (V_COUNT, 0))
        g_qkv, g_out, g_up, g_down, vec, side = reduce_weights(l, d, vec)
        counts = vec[V_COUNT:V_LOSS].reshape(-1)[:vocab_all]
        loss_all = jnp.sum(vec[V_LOSS]) + jnp.sum(side[V_LOSS - 8])
        entropy_all, used_all = count_shares(counts, total_tokens)
        hist_local = lax.dynamic_slice(counts, (dp * vocab_local,), (vocab_local,))
    else:
        pairs = (
            (l[:, L_A:L_M], d[:, D_QKV:D_GB]),
            (l[:, L_O:L_A], d[:, D_GH:D_QKV]),
            (l[:, :L_O], d[:, :D_GH]),
            (l[:, L_M:], d[:, D_GB:]),
        )
        g_qkv, g_out, g_up, g_down = (
            lax.psum_scatter(matmul_tn(left, right), "dp", scatter_dimension=0, tiled=True) for left, right in pairs
        )
        hist_local = lax.psum_scatter(counts, "dp", scatter_dimension=0, tiled=True)
        entropy_part, used_part = count_shares(hist_local, total_tokens)
        vec = lax.psum(vec, "dp")
        entropy_all, used_all = lax.psum((entropy_part, used_part), "dp")
        loss_all = lax.psum(jnp.sum(vec[V_LOSS]), "section")
    stats = jnp.stack([loss_all / (total_tokens * width), used_all / vocab_all, jnp.exp(entropy_all) / vocab_all])
    return (
        result_bf[None],
        dh[None],
        vec[None, 0:2],
        vec[None, 2:4],
        g_qkv[None],
        g_out[None],
        vec[None, 4],
        g_up[None],
        vec[5:9].reshape(1, FF),
        g_down[None],
        vec[None, 9],
        hist_local.astype(jnp.int32),
        stats,
    )


def solution(mesh):
    return jax.shard_map(
        on_device,
        mesh=mesh,
        in_specs=(
            P("dp", None),
            P("dp", None),
            P("dp"),
            P("dp", None),
            P("section", None, None),
            P("section", None, None),
            P("section", None, None),
            P("section", None, None),
            P("section", None),
            P("section", None, None),
            P("section", None),
            P("section", None, None),
            P("section", None),
        ),
        out_specs=(
            P("section", "dp", None),
            P("section", "dp", None),
            P("section", None, None),
            P("section", None, None),
            P("section", "dp", None),
            P("section", "dp", None),
            P("section", None),
            P("section", "dp", None),
            P("section", None),
            P("section", "dp", None),
            P("section", None),
            P("dp"),
            P(),
        ),
        check_vma=False,
    )
```

```python
import functools

import jax
import jax.numpy as jnp
from jax import lax
from jax.experimental import pallas as pl
from jax.experimental.pallas import tpu as pltpu
from jax.sharding import PartitionSpec as P

SEQ = 256
D = 768
HD = 64
HEADS = 12
FF = 3072
FF_PIECE = 768
QKV = 3 * D
L_O, L_A, L_M, L_ALL = D, 2 * D, 3 * D, 3 * D + FF
D_GH, D_QKV, D_GB, D_ALL = FF, FF + D, FF + D + QKV, FF + D + QKV + D
V_LOSS, V_ROWS, V_COLS = 15, 16, D + 256

COMMIT_WEIGHT = 0.25
EPSILON = 1e-06
SQRT_HALF = 0.5**0.5
INV_ROOT_TAU = 0.3989422804014327
LOG2_E = 1.4426950408889634
HEAD_SCALE = HD**-0.5
MESH = pl.DeviceIdType.MESH
BF, F32 = jnp.bfloat16, jnp.float32
VMEM_BYTES = 60 << 20


def matmul_nn(left, right):
    return jnp.dot(left, right, preferred_element_type=F32)


def matmul_nt(left, right):
    return lax.dot_general(left, right, (((1,), (1,)), ((), ())), preferred_element_type=F32)


def matmul_tn(left, right):
    return lax.dot_general(left, right, (((0,), (0,)), ((), ())), preferred_element_type=F32)


def layer_norm(rows_in):
    centered = rows_in - jnp.mean(rows_in, axis=-1, keepdims=True)
    inv_std = lax.rsqrt(jnp.mean(centered * centered, axis=-1, keepdims=True) + EPSILON)
    return centered * inv_std, inv_std


def norm_back(incoming, scaled, inv_std, gain_row):
    x = incoming * gain_row
    return inv_std * (
        x
        - jnp.mean(x, axis=-1, keepdims=True)
        - scaled * jnp.mean(x * scaled, axis=-1, keepdims=True)
    )


def column_sum(x):
    return jnp.sum(x, axis=0, keepdims=True)


def head_masks():
    low = lax.broadcasted_iota(jnp.int32, (1, 2 * HD), 1) < HD
    ones = low.astype(F32)
    return ones.astype(BF), (1.0 - ones).astype(BF)


def head_pair(ref, base, head):
    return ref[:, base + head // 2 * 128 : base + (head // 2 + 1) * 128]


def forward_image(x_ref, weights, l_ref, qkv_ref, pt_ref, slope_ref, h1_ref, out_ref, outb_ref, vt_ref, ot_ref):
    gains, shifts, w_qkv, w_out, out_bias, w_up, up_bias, w_down, down_bias = weights
    h = x_ref[...].astype(F32)
    s1, _ = layer_norm(h)
    a = (s1 * gains[0:1, :] + shifts[0:1, :]).astype(BF)
    l_ref[:, L_A:L_M] = a
    for j in range(3):
        qkv_ref[:, j * D : (j + 1) * D] = matmul_nn(a, w_qkv[:, j * D : (j + 1) * D]).astype(BF)
    vt_ref[...] = qkv_ref[:, 2 * D : 3 * D].T
    masks = head_masks()
    scores = [
        matmul_nt(head_pair(qkv_ref, D, head) * masks[head % 2], head_pair(qkv_ref, 0, head)) for head in range(HEADS)
    ]
    for head in range(HEADS):
        st = scores[head]
        e = jnp.exp2((st - jnp.max(st, axis=0, keepdims=True)) * (HEAD_SCALE * LOG2_E))
        pt_ref[head] = (e * (1.0 / column_sum(e))).astype(BF)
    for head in range(HEADS):
        span = slice(head * HD, (head + 1) * HD)
        ot_ref[span, :] = matmul_nn(vt_ref[span, :], pt_ref[head]).astype(BF)
    o = ot_ref[...].T
    l_ref[:, L_O:L_A] = o
    h1 = h + matmul_nn(o, w_out[...]) + out_bias[...]
    h1_ref[...] = h1
    s2, _ = layer_norm(h1)
    b = (s2 * gains[1:2, :] + shifts[1:2, :]).astype(BF)
    l_ref[:, 0:L_O] = b
    result = h1 + down_bias[...]
    for j in range(FF // FF_PIECE):
        span = slice(j * FF_PIECE, (j + 1) * FF_PIECE)
        u = matmul_nn(b, w_up[:, span]) + up_bias[:, span]
        half_curve = 0.5 + 0.5 * lax.erf(u * SQRT_HALF)
        m = (u * half_curve).astype(BF)
        l_ref[:, L_M + j * FF_PIECE : L_M + (j + 1) * FF_PIECE] = m
        slope = half_curve + u * jnp.exp(-0.5 * u * u) * INV_ROOT_TAU
        slope_ref[:, span] = slope.astype(slope_ref.dtype)
        result = result + matmul_nn(m, w_down[span, :])
    out_ref[...] = result
    outb_ref[...] = result.astype(BF)


def backward_image(
    scale, out_ref, other_ref, arrived_ref, x_ref, weights, qkv_ref, pt_ref, slope_ref, h1_ref,
    d_ref, vec_ref, dh_ref, dhb_ref, kt_ref, qt_ref,
):
    gains, shifts, w_qkv, w_out, out_bias, w_up, up_bias, w_down, down_bias = weights
    diff = out_ref[...] - other_ref[...].astype(F32)

    def add(row, value):
        vec_ref[row : row + 1, :D] += column_sum(value)

    add(V_LOSS, diff * diff * scale)
    g = diff * scale + arrived_ref[...].astype(F32)
    gb = g.astype(BF)
    d_ref[:, D_GB:D_ALL] = gb
    add(9, g)
    db = jnp.zeros((SEQ, D), F32)
    for j in range(FF // FF_PIECE):
        span = slice(j * FF_PIECE, (j + 1) * FF_PIECE)
        du = (matmul_nt(gb, w_down[span, :]) * slope_ref[:, span].astype(F32)).astype(BF)
        d_ref[:, span] = du
        add(5 + j, du.astype(F32))
        db = db + matmul_nt(du, w_up[:, span])
    s2, inv2 = layer_norm(h1_ref[...])
    add(1, db * s2)
    add(3, db)
    dh1 = g + norm_back(db, s2, inv2, gains[1:2, :])
    add(4, dh1)
    gh = dh1.astype(BF)
    d_ref[:, D_GH:D_QKV] = gh
    do = matmul_nt(gh, w_out[...]).astype(BF)
    kt_ref[...] = qkv_ref[:, D : 2 * D].T
    masks = head_masks()

    def do_pair(head):
        return do[:, head // 2 * 128 : (head // 2 + 1) * 128]

    dpts = [matmul_nt(head_pair(qkv_ref, 2 * D, head) * masks[head % 2], do_pair(head)) for head in range(HEADS)]

    def both(parts, pair, make):
        return matmul_nn(
            jnp.concatenate(parts[2 * pair : 2 * pair + 2], axis=1),
            jnp.concatenate([make(2 * pair) * masks[0], make(2 * pair) * masks[1]], axis=0),
        )

    base = D_QKV + D
    for pair in range(HEADS // 2):
        dv = both([pt_ref[head] for head in range(HEADS)], pair, do_pair)
        d_ref[:, base + D + pair * 128 : base + D + (pair + 1) * 128] = dv.astype(BF)
    dsts = []
    for head in range(HEADS):
        ptf = pt_ref[head].astype(F32)
        dsts.append((ptf * (dpts[head] - column_sum(dpts[head] * ptf))).astype(BF))
    for pair in range(HEADS // 2):
        dk = both(dsts, pair, lambda head: head_pair(qkv_ref, 0, head))
        d_ref[:, base + pair * 128 : base + (pair + 1) * 128] = (dk * HEAD_SCALE).astype(BF)
    for head in range(HEADS):
        span = slice(head * HD, (head + 1) * HD)
        qt_ref[span, :] = (matmul_nn(kt_ref[span, :], dsts[head]) * HEAD_SCALE).astype(BF)
    d_ref[:, D_QKV : D_QKV + D] = qt_ref[...].T
    da = matmul_nt(d_ref[:, D_QKV:D_GB], w_qkv[...])
    s1, inv1 = layer_norm(x_ref[...].astype(F32))
    add(0, da * s1)
    add(2, da)
    dh = dh1 + norm_back(da, s1, inv1, gains[0:1, :])
    dh_ref[...] = dh
    dhb_ref[...] = dh.astype(BF)


WEIGHT_SHAPES = ((2, D), (2, D), (D, QKV), (D, D), (1, D), (D, FF), (1, FF), (FF, D), (1, D))


def weight_specs():
    def whole(shape):
        return pl.BlockSpec(shape, lambda *_: (0, 0), pipeline_mode=pl.Buffered(1))

    return [whole(shape) for shape in WEIGHT_SHAPES]


def block_forward(x, weights):
    rows = x.shape[0]
    images = rows // SEQ

    def row_block(width):
        return pl.BlockSpec((SEQ, width), lambda i: (i, 0))

    def body(x_ref, *refs):
        forward_image(x_ref, refs[:9], *refs[9:])

    def shape(width, dtype):
        return jax.ShapeDtypeStruct((rows, width), dtype)

    return pl.pallas_call(
        body,
        grid=(images,),
        in_specs=[row_block(D)] + weight_specs(),
        out_specs=[
            row_block(L_ALL),
            row_block(QKV),
            pl.BlockSpec((HEADS, SEQ, SEQ), lambda i: (i, 0, 0)),
            row_block(FF),
            row_block(D),
            row_block(D),
            row_block(D),
        ],
        out_shape=[
            shape(L_ALL, BF),
            shape(QKV, BF),
            jax.ShapeDtypeStruct((images * HEADS, SEQ, SEQ), BF),
            shape(FF, BF),
            shape(D, F32),
            shape(D, F32),
            shape(D, BF),
        ],
        scratch_shapes=[pltpu.VMEM((D, SEQ), BF), pltpu.VMEM((D, SEQ), BF)],
        compiler_params=pltpu.CompilerParams(vmem_limit_bytes=VMEM_BYTES),
        name="block_forward",
    )(x, *weights)


def block_backward(which, flags, result, other, arrived, x, weights, qkv, pt, slope, h1, vec, d, dh):
    rows = x.shape[0]

    def row_block(width):
        return pl.BlockSpec((SEQ, width), lambda i, which_ref: (which_ref[0], 0))

    def whole(height, width):
        return pl.BlockSpec((height, width), lambda i, which_ref: (0, 0))

    def body(which_ref, flags_ref, out_ref, other_ref, arrived_ref, x_ref, *refs):
        weight_refs = refs[:9]
        qkv_ref, pt_ref, slope_ref, h1_ref, vec_in = refs[9:14]
        d_ref, dh_ref, vec_out, dhb_ref, kt_ref, qt_ref = refs[-6:]
        vec_out[...] = jnp.zeros_like(vec_out)
        backward_image(
            flags_ref[0], out_ref, other_ref, arrived_ref, x_ref, weight_refs, qkv_ref, pt_ref,
            slope_ref, h1_ref, d_ref, vec_out, dh_ref, dhb_ref, kt_ref, qt_ref,
        )
        vec_out[...] = vec_in[...] + vec_out[...] * flags_ref[1]

    keep = [] if d is None else [d, dh]
    first_kept = 2 + 4 + 9 + 5
    return pl.pallas_call(
        body,
        grid_spec=pltpu.PrefetchScalarGridSpec(
            num_scalar_prefetch=1,
            grid=(1,),
            in_specs=[pl.BlockSpec(memory_space=pltpu.SMEM), row_block(D), row_block(D), whole(SEQ, D), row_block(D)]
            + weight_specs()
            + [
                row_block(QKV),
                pl.BlockSpec((HEADS, SEQ, SEQ), lambda i, which_ref: (which_ref[0], 0, 0)),
                row_block(FF),
                row_block(D),
                whole(V_ROWS, V_COLS),
            ]
            + [pl.BlockSpec(memory_space=pl.ANY)] * len(keep),
            out_specs=[row_block(D_ALL), row_block(D), whole(V_ROWS, V_COLS), whole(SEQ, D)],
            scratch_shapes=[pltpu.VMEM((D, SEQ), BF), pltpu.VMEM((D, SEQ), BF)],
        ),
        out_shape=[
            jax.ShapeDtypeStruct((rows, D_ALL), BF),
            jax.ShapeDtypeStruct((rows, D), F32),
            jax.ShapeDtypeStruct((V_ROWS, V_COLS), F32),
            jax.ShapeDtypeStruct((SEQ, D), BF),
        ],
        input_output_aliases={first_kept: 0, first_kept + 1: 1} if keep else {},
        compiler_params=pltpu.CompilerParams(vmem_limit_bytes=VMEM_BYTES),
        name="block_backward",
    )(which, flags, result, other, arrived, x, *weights, qkv, pt, slope, h1, vec, *keep)


IMAGES = 4
SHARD = 208


def blocks_kernel(
    patches_ref, targets_ref, ids_ref, codebook_ref, gains, shifts, w_qkv_ref, w_out_ref, out_bias, w_up_ref, up_bias,
    w_down_ref, down_bias, result_ref, dh_ref, l_ref, d_ref, vec_ref,
    w_qkv, w_out, w_up, w_down, shards, ids_col, x_buf, other_buf, arrived, outgoing,
    qkv, pt, slope, h1, result, l_buf, d_buf, result_buf, dh_buf, vt, ot,
    w_sem, in_sem, out_sem, sz, rz, sy, ry, sc, rc, sx, rx,
):
    section, dp = lax.axis_index("section"), lax.axis_index("dp")
    core, y, z = dp % 2, (dp // 2) % 2, dp // 4
    across = (section, dp + 1 - 2 * core)
    along_y = (section, dp + 2 - 4 * y)
    along_z = [(section, (z + k) % 4 * 4 + y * 2 + core) for k in (1, 2, 3)]
    beside = (1 - section, dp)

    big = ((w_qkv_ref, w_qkv), (w_out_ref, w_out), (w_up_ref, w_up), (w_down_ref, w_down))
    loads = [pltpu.make_async_copy(src, dst, w_sem.at[i]) for i, (src, dst) in enumerate(big)]
    for load in loads:
        load.start()
    patch_load = pltpu.make_async_copy(patches_ref, x_buf, in_sem)
    target_load = pltpu.make_async_copy(targets_ref, other_buf, in_sem)

    @pl.when(section == 0)
    def _():
        patch_load.start()

    @pl.when(section == 1)
    def _():
        target_load.start()
        arrived[...] = jnp.zeros_like(arrived)

    rows_here = codebook_ref.shape[0]
    shards[dp] = jnp.zeros((SHARD, D), BF)
    shards[dp, :rows_here] = codebook_ref[...]

    barrier = pltpu.get_barrier_semaphore()
    for target in [across, along_y, beside] + along_z:
        pl.semaphore_signal(barrier, inc=1, device_id=target, device_id_type=MESH)
    pl.semaphore_wait(barrier, 6)

    def move(place, send, recv, target):
        return pltpu.make_async_remote_copy(
            shards.at[place], shards.at[place], send, recv, device_id=target, device_id_type=MESH
        )

    near = [(z - k + 4) % 4 * 4 + y * 2 + core for k in range(4)]
    far = [(z - k + 4) % 4 * 4 + (1 - y) * 2 + core for k in range(4)]

    def send_z(k):
        return move(dp, sz.at[k - 1], rz.at[k - 1], along_z[k - 1])

    def got_z(k):
        return move(near[k], sz.at[k - 1], rz.at[k - 1], along_z[k - 1])

    def send_y(k):
        return move(near[k], sy.at[k], ry.at[k], along_y)

    def got_y(k):
        return move(far[k], sy.at[k], ry.at[k], along_y)

    def send_core(k):
        return move(near[k] if k < 4 else far[k - 4], sc.at[k], rc.at[k], across)

    def got_core(k):
        place = near[k] if k < 4 else far[k - 4]
        return move(place + 1 - 2 * core, sc.at[k], rc.at[k], across)

    send_z(1).start()
    send_y(0).start()
    send_z(2).start()
    send_z(3).start()
    send_core(0).start()

    vec_ref[...] = jnp.zeros_like(vec_ref)
    ids_col[...] = jnp.broadcast_to(ids_ref[...], (128, IMAGES * SEQ)).T
    lane = lax.broadcasted_iota(jnp.int32, (IMAGES * SEQ, 128), 1)

    def pick(place, dest, first):
        rel = ids_col[...] - place * rows_here
        low = (rel == lane).astype(F32)
        high = ((rel - 128 == lane) & (lane < rows_here - 128)).astype(F32)
        one_hot = jnp.concatenate([low, high], axis=1)
        vec_ref[pl.ds(place, 1), D:] = column_sum(one_hot)
        one_hot = one_hot[:, :SHARD].astype(BF)
        for i in range(IMAGES):
            rows = matmul_nn(one_hot[i * SEQ : (i + 1) * SEQ], shards[place]).astype(BF)
            dest[i] = rows if first else dest[i] + rows

    def gather(dest):
        pick(dp, dest, True)
        for step in ("c0", "z1", "c1", "y0", "c4", "z2", "c2", "y1", "c5", "z3", "c3", "y2", "c6", "y3", "c7"):
            k = int(step[1])
            if step[0] == "z":
                got_z(k).wait_recv()
                send_y(k).start()
                send_core(k).start()
                place = near[k]
            elif step[0] == "y":
                got_y(k).wait_recv()
                send_core(4 + k).start()
                place = far[k]
            else:
                got_core(k).wait_recv()
                place = (near[k] if k < 4 else far[k - 4]) + 1 - 2 * core
            pick(place, dest, False)

    @pl.when(section == 0)
    def _():
        gather(other_buf)
        patch_load.wait()

    @pl.when(section == 1)
    def _():
        gather(x_buf)
        target_load.wait()

    for k in range(1, 4):
        send_z(k).wait_send()
    for k in range(4):
        send_y(k).wait_send()
    for k in range(8):
        send_core(k).wait_send()
    for load in loads:
        load.wait()

    weights = (gains, shifts, w_qkv, w_out, out_bias, w_up, up_bias, w_down, down_bias)
    scale = jnp.where(section == 0, COMMIT_WEIGHT, 1.0)

    def rows_of(ref, image):
        return ref.at[pl.ds(pl.multiple_of(image * SEQ, SEQ), SEQ)]

    def stores(image, forward):
        pairs = ((l_buf, l_ref), (result_buf, result_ref)) if forward else ((d_buf, d_ref), (dh_buf, dh_ref))
        first = 0 if forward else 2
        return [
            pltpu.make_async_copy(src, rows_of(dst, image), out_sem.at[first + i]) for i, (src, dst) in enumerate(pairs)
        ]

    def cross(image):
        return pltpu.make_async_remote_copy(
            outgoing.at[image], arrived.at[image], sx.at[image], rx.at[image], device_id=beside, device_id_type=MESH
        )

    def step(i, carry):
        even = i % 2 == 0
        ahead = jnp.where(section == 1, even, (i == 0) | ((i % 2 == 1) & (i < 7)))

        @pl.when(ahead)
        def _():
            image = (i + 1) // 2
            slot = image % 2

            @pl.when(image > 0)
            def _():
                for copy in stores(image - 1, True):
                    copy.wait()

            forward_image(
                x_buf.at[image], weights, l_buf, qkv.at[slot], pt.at[slot], slope.at[slot], h1.at[slot],
                result.at[slot], result_buf, vt, ot,
            )
            for copy in stores(image, True):
                copy.start()

        @pl.when(jnp.logical_not(ahead))
        def _():
            image = (i - 1) // 2
            slot = image % 2

            @pl.when(image > 0)
            def _():
                for copy in stores(image - 1, False):
                    copy.wait()

            @pl.when(section == 0)
            def _():
                cross(image).wait_recv()

            backward_image(
                scale, result.at[slot], other_buf.at[image], arrived.at[image], x_buf.at[image], weights,
                qkv.at[slot], pt.at[slot], slope.at[slot], h1.at[slot], d_buf, vec_ref, dh_buf, outgoing.at[image], vt, ot,
            )

            @pl.when(section == 1)
            def _():
                cross(image).start()

            for copy in stores(image, False):
                copy.start()

        return carry

    lax.fori_loop(0, 2 * IMAGES, step, 0)
    for forward in (True, False):
        for copy in stores(IMAGES - 1, forward):
            copy.wait()

    @pl.when(section == 1)
    def _():
        for image in range(IMAGES):
            cross(image).wait_send()


def run_blocks(patches, targets, ids, codebook, weights):
    dma = pltpu.SemaphoreType.DMA
    vm = pltpu.VMEM
    rows = IMAGES * SEQ
    inside, outside = pl.BlockSpec(memory_space=pltpu.VMEM), pl.BlockSpec(memory_space=pl.ANY)
    weight_places = [inside, inside, outside, outside, inside, outside, inside, outside, inside]
    return pl.pallas_call(
        blocks_kernel,
        out_shape=[
            jax.ShapeDtypeStruct((rows, D), BF),
            jax.ShapeDtypeStruct((rows, D), F32),
            jax.ShapeDtypeStruct((rows, L_ALL), BF),
            jax.ShapeDtypeStruct((rows, D_ALL), BF),
            jax.ShapeDtypeStruct((V_ROWS, V_COLS), F32),
        ],
        in_specs=[outside, outside, inside, inside] + weight_places,
        out_specs=[outside] * 4 + [inside],
        scratch_shapes=[
            vm((D, QKV), BF), vm((D, D), BF), vm((D, FF), BF), vm((FF, D), BF),
            vm((16, SHARD, D), BF), vm((rows, 128), jnp.int32),
            vm((IMAGES, SEQ, D), BF), vm((IMAGES, SEQ, D), BF), vm((IMAGES, SEQ, D), BF), vm((IMAGES, SEQ, D), BF),
            vm((2, SEQ, QKV), BF), vm((2, HEADS, SEQ, SEQ), BF), vm((2, SEQ, FF), BF), vm((2, SEQ, D), F32),
            vm((2, SEQ, D), F32), vm((SEQ, L_ALL), BF), vm((SEQ, D_ALL), BF), vm((SEQ, D), BF), vm((SEQ, D), F32),
            vm((D, SEQ), BF), vm((D, SEQ), BF),
            dma((4,)), dma(()), dma((4,)), dma((3,)), dma((3,)), dma((4,)), dma((4,)), dma((8,)), dma((8,)),
            dma((IMAGES,)), dma((IMAGES,)),
        ],
        compiler_params=pltpu.CompilerParams(collective_id=2, has_side_effects=True, vmem_limit_bytes=VMEM_BYTES),
        name="blocks",
    )(patches.reshape(IMAGES, SEQ, D), targets.reshape(IMAGES, SEQ, D), ids.reshape(1, rows), codebook, *weights)


UNITS = 36
PART = D // 16
COLS = 256
LAG_Y, LAG_Z, LAG_OUT = 1, 3, 5
PIECE = 384


def reduce_kernel(
    vocab, l_ref, d_ref, vec_ref, qkv_out, out_out, up_out, down_out, vec_out, hist_out, stats_out,
    lt, lbuf, dbuf, acc_y, acc_z, acc_o, tx_c, rx_c, tx_y, rx_y, tx_z, rx_z, vec_tx, vec_c, vec_y, vec_z, side,
    lsem, dsem, sc, rc, sy, ry, sz, rz, sv, rv,
):
    sec, dp = lax.axis_index("section"), lax.axis_index("dp")
    core, y, z = dp % 2, (dp // 2) % 2, dp // 4
    across = (sec, dp + 1 - 2 * core)
    along_y = (sec, dp + 2 - 4 * y)
    along_z = [(sec, (z + k) % 4 * 4 + y * 2 + core) for k in (1, 2, 3)]
    beside = (1 - sec, dp)
    barrier = pltpu.get_barrier_semaphore()
    for target in [across, along_y, beside] + along_z:
        pl.semaphore_signal(barrier, inc=1, device_id=target, device_id_type=MESH)
    pl.semaphore_wait(barrier, 6)

    def remote(src, dst, send, recv, target):
        return pltpu.make_async_remote_copy(src, dst, send, recv, device_id=target, device_id_type=MESH)

    def spot(g):
        return ((g % 2 + core) % 2) * 8 + (((g // 2) % 2 + y) % 2) * 4 + (g // 4 - z + 4) % 4

    def aligned(x, n):
        return pl.multiple_of(x, n)

    def load_left(i):
        return pltpu.make_async_copy(l_ref.at[:, pl.ds(aligned(i * PIECE, PIECE), PIECE)], lbuf.at[i % 2], lsem.at[i % 2])

    def load_right(u):
        d = jnp.where(u < 24, u, 24 + u % 3)
        return pltpu.make_async_copy(d_ref.at[:, pl.ds(aligned(d * COLS, COLS), COLS)], dbuf.at[u % 2], dsem.at[u % 2])

    def prepare(i):
        load_left(i).wait()

        @pl.when(i < 13)
        def _():
            load_left(i + 1).start()

        turned = lbuf[i % 2].T

        @pl.when(i < 6)
        def _():
            for k in range(8):
                place = spot((i % 2) * 8 + k) * PART
                lt[i // 2, pl.ds(aligned(place, PART), PART), :] = turned[k * PART : (k + 1) * PART]

        @pl.when(i >= 6)
        def _():
            for k in range(8):
                place = spot((i - 6) * 2 + k // 4) * PART
                lt[3 + k % 4, pl.ds(aligned(place, PART), PART), :] = turned[k * PART : (k + 1) * PART]

    def send_core(u):
        return remote(tx_c.at[u], rx_c.at[u], sc.at[u], rc.at[u], across)

    def send_y(u):
        return remote(tx_y.at[u], rx_y.at[u], sy.at[u], ry.at[u], along_y)

    def send_z(u, k):
        return remote(tx_z.at[u, k], rx_z.at[u, k], sz.at[u, k], rz.at[u, k], along_z[k])

    vec_core = remote(vec_ref, vec_c, sv.at[0], rv.at[0], across)
    vec_along_y = remote(vec_tx, vec_y, sv.at[1], rv.at[1], along_y)
    vec_along_z = [remote(vec_z.at[z], vec_z.at[z], sv.at[2 + k], rv.at[2 + k], along_z[k]) for k in range(3)]
    vec_beside = remote(vec_out.at[8:16], side, sv.at[5], rv.at[5], beside)

    load_left(0).start()
    load_right(0).start()
    prepare(0)
    prepare(1)
    vec_core.start()

    def step(i, carry):
        @pl.when(i < UNITS)
        def _():
            u = i

            @pl.when(u + 1 < UNITS)
            def _():
                load_right(u + 1).start()

            load_right(u).wait()
            l = jnp.where(u < 12, 0, jnp.where(u < 15, 1, jnp.where(u < 24, 2, 3 + (u - 24) // 3)))
            product = matmul_nn(lt[l], dbuf[u % 2])
            acc_y[u % 2] = product[: 8 * PART]
            tx_c[u] = product[8 * PART :].astype(BF)
            send_core(u).start()

        @pl.when((i >= LAG_Y) & (i < UNITS + LAG_Y))
        def _():
            u = i - LAG_Y
            send_core(u).wait()
            t = acc_y[u % 2] + rx_c[u].astype(F32)
            acc_z[u % 4] = t[: 4 * PART]
            tx_y[u] = t[4 * PART :].astype(BF)
            send_y(u).start()

        @pl.when((i >= LAG_Z) & (i < UNITS + LAG_Z))
        def _():
            u = i - LAG_Z
            send_y(u).wait()
            t = acc_z[u % 4] + rx_y[u].astype(F32)
            acc_o[u % 4] = t[:PART]
            for k in range(3):
                tx_z[u, k] = t[PART * (k + 1) : PART * (k + 2)].astype(BF)
                send_z(u, k).start()

        @pl.when(i >= LAG_OUT)
        def _():
            u = i - LAG_OUT
            t = acc_o[u % 4]
            for k in range(3):
                send_z(u, k).wait()
                t = t + rx_z[u, k].astype(F32)

            def lanes(n):
                return pl.ds(aligned(n * COLS, COLS), COLS)

            @pl.when(u < 12)
            def _():
                up_out[:, lanes(u)] = t

            @pl.when((u >= 12) & (u < 15))
            def _():
                out_out[:, lanes(u - 12)] = t

            @pl.when((u >= 15) & (u < 24))
            def _():
                qkv_out[:, lanes(u - 15)] = t

            @pl.when(u >= 24)
            def _():
                down_out[pl.ds(aligned((u - 24) // 3 * PART, PART), PART), lanes(u % 3)] = t

        @pl.when(i < 12)
        def _():
            prepare(i + 2)

        @pl.when(i == 3)
        def _():
            vec_core.wait()
            vec_tx[...] = vec_ref[...] + vec_c[...]
            vec_along_y.start()

        @pl.when(i == 8)
        def _():
            vec_along_y.wait()
            vec_z[z] = vec_tx[...] + vec_y[...]
            for copy in vec_along_z:
                copy.start()

        @pl.when(i == 14)
        def _():
            for copy in vec_along_z:
                copy.wait()
            vec_out[...] = (vec_z[0] + vec_z[1]) + (vec_z[2] + vec_z[3])
            vec_beside.start()

        return carry

    lax.fori_loop(0, UNITS + LAG_OUT, step, 0)
    vec_beside.wait()

    def total(value):
        return jnp.sum(jnp.sum(value, axis=1, keepdims=True), axis=0, keepdims=True)

    tokens = 16 * l_ref.shape[0]
    counts = vec_out[:, D:]
    shares = counts * (1.0 / tokens)
    entropy = -total(shares * jnp.log(jnp.where(counts > 0, shares, 1.0)))
    used = total((counts > 0).astype(F32))
    loss = total(vec_out[V_LOSS : V_LOSS + 1, :D]) + total(side[V_LOSS - 8 : V_LOSS - 7, :D])
    lane = lax.broadcasted_iota(jnp.int32, (8, 128), 1)
    last = jnp.where(lane == 1, used / vocab, jnp.exp(entropy) / vocab)
    stats_out[...] = jnp.where(lane == 0, loss / (tokens * D), last)
    hist_out[...] = vec_out[pl.ds(dp, 1), D:].astype(jnp.int32)


def reduce_weights(l, d, vec, vocab):
    dma = pltpu.SemaphoreType.DMA
    vm = pltpu.VMEM
    return pl.pallas_call(
        functools.partial(reduce_kernel, vocab),
        out_shape=[
            jax.ShapeDtypeStruct((PART, QKV), F32),
            jax.ShapeDtypeStruct((PART, D), F32),
            jax.ShapeDtypeStruct((PART, FF), F32),
            jax.ShapeDtypeStruct((4 * PART, D), F32),
            jax.ShapeDtypeStruct((V_ROWS, V_COLS), F32),
            jax.ShapeDtypeStruct((1, V_COLS - D), jnp.int32),
            jax.ShapeDtypeStruct((8, 128), F32),
        ],
        in_specs=[pl.BlockSpec(memory_space=pl.ANY)] * 2 + [pl.BlockSpec(memory_space=pltpu.VMEM)],
        out_specs=[pl.BlockSpec(memory_space=pltpu.VMEM)] * 7,
        scratch_shapes=[
            vm((7, D, 4 * SEQ), BF), vm((2, 4 * SEQ, PIECE), BF), vm((2, 4 * SEQ, COLS), BF),
            vm((2, 8 * PART, COLS), F32), vm((4, 4 * PART, COLS), F32), vm((4, PART, COLS), F32),
            vm((UNITS, 8 * PART, COLS), BF), vm((UNITS, 8 * PART, COLS), BF),
            vm((UNITS, 4 * PART, COLS), BF), vm((UNITS, 4 * PART, COLS), BF),
            vm((UNITS, 3, PART, COLS), BF), vm((UNITS, 3, PART, COLS), BF),
            vm((V_ROWS, V_COLS), F32), vm((V_ROWS, V_COLS), F32), vm((V_ROWS, V_COLS), F32), vm((4, V_ROWS, V_COLS), F32),
            vm((8, V_COLS), F32),
            dma((2,)), dma((2,)), dma((UNITS,)), dma((UNITS,)), dma((UNITS,)), dma((UNITS,)),
            dma((UNITS, 3)), dma((UNITS, 3)), dma((6,)), dma((6,)),
        ],
        compiler_params=pltpu.CompilerParams(collective_id=1, has_side_effects=True, vmem_limit_bytes=VMEM_BYTES),
        name="weight_grad_reduce",
    )(l, d, vec)


def count_shares(counts, total_count):
    shares = counts / total_count
    nonzero_share = jnp.where(counts > 0, shares, 1.0)
    return -jnp.sum(shares * jnp.log(nonzero_share)), jnp.sum((counts > 0).astype(F32))


def on_device(
    patches, targets, code_ids, codebook, norm_gains, norm_shifts, w_qkv, w_out, out_bias, w_up, up_bias, w_down, down_bias
):
    section = lax.axis_index("section")
    leading = section == 0
    dp_size = lax.axis_size("dp")
    dp = lax.axis_index("dp")
    weights = (
        norm_gains[0], norm_shifts[0], w_qkv[0], w_out[0], out_bias, w_up[0], up_bias, w_down[0], down_bias
    )
    rows, width = patches.shape
    images = rows // SEQ
    vocab_local = codebook.shape[0]
    vocab_all = vocab_local * dp_size
    total_tokens = rows * dp_size

    small = dp_size == 16 and vocab_local <= SHARD and rows == IMAGES * SEQ
    if small:
        result_bf, dh, l, d, vec = run_blocks(patches, targets, code_ids, codebook, weights)
        g_qkv, g_out, g_up, g_down, vec, hist, stats = reduce_weights(l, d, vec, vocab_all)
        hist_local = hist[0, :vocab_local]
        stats = stats[0, :3]
    else:
        shard_rows = lax.all_gather(codebook, "dp", axis=0, tiled=True)
        chosen = jnp.take(shard_rows, jnp.clip(code_ids, 0, vocab_all - 1), axis=0)
        x = jnp.where(leading, patches, chosen)
        l, qkv, pt, slope, h1, result, result_bf = block_forward(x, weights)
        other = jnp.where(leading, chosen, targets)
        d = dh = None
        vec = jnp.zeros((V_ROWS, V_COLS), F32)
        arrived = jnp.zeros((SEQ, D), BF)
        for moment in range(images + 1):
            which = jnp.clip(moment - 1 + section, 0, images - 1).astype(jnp.int32)[None]
            active = jnp.where(leading, moment >= 1, moment < images).astype(F32)
            flags = jnp.stack([jnp.where(leading, COMMIT_WEIGHT, 1.0).astype(F32), active])
            d, dh, vec, outgoing = block_backward(
                which, flags, result, other, arrived, x, weights, qkv, pt, slope, h1, vec, d, dh
            )
            if moment < images:
                arrived = lax.ppermute(outgoing, "section", [(1, 0)])
        pairs = (
            (l[:, L_A:L_M], d[:, D_QKV:D_GB]),
            (l[:, L_O:L_A], d[:, D_GH:D_QKV]),
            (l[:, :L_O], d[:, :D_GH]),
            (l[:, L_M:], d[:, D_GB:]),
        )
        g_qkv, g_out, g_up, g_down = (
            lax.psum_scatter(matmul_tn(left, right), "dp", scatter_dimension=0, tiled=True) for left, right in pairs
        )
        vocab_iota = lax.broadcasted_iota(jnp.int32, (1, vocab_all), 1)
        counts = jnp.sum((code_ids[:, None] == vocab_iota).astype(F32), axis=0)
        hist_local = lax.psum_scatter(counts, "dp", scatter_dimension=0, tiled=True)
        entropy_part, used_part = count_shares(hist_local, total_tokens)
        hist_local = hist_local.astype(jnp.int32)
        vec = lax.psum(vec, "dp")
        entropy_all, used_all = lax.psum((entropy_part, used_part), "dp")
        loss_all = lax.psum(jnp.sum(vec[V_LOSS, :D]), "section")
        stats = jnp.stack(
            [loss_all / (total_tokens * width), used_all / vocab_all, jnp.exp(entropy_all) / vocab_all]
        )
    return (
        result_bf[None],
        dh[None],
        vec[None, 0:2, :D],
        vec[None, 2:4, :D],
        g_qkv[None],
        g_out[None],
        vec[None, 4, :D],
        g_up[None],
        vec[5:9, :D].reshape(1, FF),
        g_down[None],
        vec[None, 9, :D],
        hist_local,
        stats,
    )


def solution(mesh):
    return jax.shard_map(
        on_device,
        mesh=mesh,
        in_specs=(
            P("dp", None),
            P("dp", None),
            P("dp"),
            P("dp", None),
            P("section", None, None),
            P("section", None, None),
            P("section", None, None),
            P("section", None, None),
            P("section", None),
            P("section", None, None),
            P("section", None),
            P("section", None, None),
            P("section", None),
        ),
        out_specs=(
            P("section", "dp", None),
            P("section", "dp", None),
            P("section", None, None),
            P("section", None, None),
            P("section", "dp", None),
            P("section", "dp", None),
            P("section", None),
            P("section", "dp", None),
            P("section", None),
            P("section", "dp", None),
            P("section", None),
            P("dp"),
            P(),
        ),
        check_vma=False,
    )
```

```python
import functools

import jax
import jax.numpy as jnp
from jax import lax
from jax.experimental import pallas as pl
from jax.experimental.pallas import tpu as pltpu
from jax.sharding import PartitionSpec as P

SEQ = 256
D = 768
HD = 64
HEADS = 12
FF = 3072
FF_PIECE = 768
QKV = 3 * D
L_O, L_A, L_M, L_ALL = D, 2 * D, 3 * D, 3 * D + FF
D_GH, D_QKV, D_GB, D_ALL = FF, FF + D, FF + D + QKV, FF + D + QKV + D
V_SIDE, V_LOSS, V_ROWS, V_COLS = 14, 15, 16, D + 256

COMMIT_WEIGHT = 0.25
EPSILON = 1e-06
SQRT_HALF = 0.5**0.5
INV_ROOT_TAU = 0.3989422804014327
LOG2_E = 1.4426950408889634
HEAD_SCALE = HD**-0.5
MESH = pl.DeviceIdType.MESH
BF, F32 = jnp.bfloat16, jnp.float32
VMEM_BYTES = 60 << 20


def matmul_nn(left, right):
    return jnp.dot(left, right, preferred_element_type=F32)


def matmul_nt(left, right):
    return lax.dot_general(left, right, (((1,), (1,)), ((), ())), preferred_element_type=F32)


def matmul_tn(left, right):
    return lax.dot_general(left, right, (((0,), (0,)), ((), ())), preferred_element_type=F32)


def layer_norm(rows_in):
    centered = rows_in - jnp.mean(rows_in, axis=-1, keepdims=True)
    inv_std = lax.rsqrt(jnp.mean(centered * centered, axis=-1, keepdims=True) + EPSILON)
    return centered * inv_std, inv_std


def norm_back(incoming, scaled, inv_std, gain_row):
    x = incoming * gain_row
    return inv_std * (
        x
        - jnp.mean(x, axis=-1, keepdims=True)
        - scaled * jnp.mean(x * scaled, axis=-1, keepdims=True)
    )


def column_sum(x):
    return jnp.sum(x, axis=0, keepdims=True)


def head_masks():
    low = lax.broadcasted_iota(jnp.int32, (1, 2 * HD), 1) < HD
    ones = low.astype(F32)
    return ones.astype(BF), (1.0 - ones).astype(BF)


def head_pair(ref, base, head):
    return ref[:, base + head // 2 * 128 : base + (head // 2 + 1) * 128]


def forward_image(x_ref, weights, l_ref, qkv_ref, pt_ref, slope_ref, h1_ref, out_ref, outb_ref, vt_ref, ot_ref):
    gains, shifts, w_qkv, w_out, out_bias, w_up, up_bias, w_down, down_bias = weights
    h = x_ref[...].astype(F32)
    s1, _ = layer_norm(h)
    a = (s1 * gains[0:1, :] + shifts[0:1, :]).astype(BF)
    l_ref[:, L_A:L_M] = a
    for j in range(3):
        qkv_ref[:, j * D : (j + 1) * D] = matmul_nn(a, w_qkv[:, j * D : (j + 1) * D]).astype(BF)
    vt_ref[...] = qkv_ref[:, 2 * D : 3 * D].T
    masks = head_masks()
    scores = [
        matmul_nt(head_pair(qkv_ref, D, head) * masks[head % 2], head_pair(qkv_ref, 0, head)) for head in range(HEADS)
    ]
    for head in range(HEADS):
        st = scores[head]
        e = jnp.exp2((st - jnp.max(st, axis=0, keepdims=True)) * (HEAD_SCALE * LOG2_E))
        pt_ref[head] = (e * (1.0 / column_sum(e))).astype(BF)
    for head in range(HEADS):
        span = slice(head * HD, (head + 1) * HD)
        ot_ref[span, :] = matmul_nn(vt_ref[span, :], pt_ref[head]).astype(BF)
    o = ot_ref[...].T
    l_ref[:, L_O:L_A] = o
    h1 = h + matmul_nn(o, w_out[...]) + out_bias[...]
    h1_ref[...] = h1
    s2, _ = layer_norm(h1)
    b = (s2 * gains[1:2, :] + shifts[1:2, :]).astype(BF)
    l_ref[:, 0:L_O] = b
    result = h1 + down_bias[...]
    for j in range(FF // FF_PIECE):
        span = slice(j * FF_PIECE, (j + 1) * FF_PIECE)
        u = matmul_nn(b, w_up[:, span]) + up_bias[:, span]
        half_curve = 0.5 + 0.5 * lax.erf(u * SQRT_HALF)
        m = (u * half_curve).astype(BF)
        l_ref[:, L_M + j * FF_PIECE : L_M + (j + 1) * FF_PIECE] = m
        slope = half_curve + u * jnp.exp(-0.5 * u * u) * INV_ROOT_TAU
        slope_ref[:, span] = slope.astype(slope_ref.dtype)
        result = result + matmul_nn(m, w_down[span, :])
    out_ref[...] = result
    outb_ref[...] = result.astype(BF)


def backward_image(
    scale, receives, out_ref, other_ref, arrived_ref, x_ref, weights, qkv_ref, pt_ref, slope_ref, h1_ref,
    d_ref, vec_ref, dh_ref, dhb_ref, kt_ref, qt_ref,
):
    gains, shifts, w_qkv, w_out, out_bias, w_up, up_bias, w_down, down_bias = weights
    diff = out_ref[...] - other_ref[...].astype(F32)

    def add(row, value):
        vec_ref[row : row + 1, :D] += column_sum(value)

    g = diff * scale + jnp.where(receives, arrived_ref[...].astype(F32), 0.0)
    gb = g.astype(BF)
    d_ref[:, D_GB:D_ALL] = gb
    add(9, g)
    db = jnp.zeros((SEQ, D), F32)
    for j in range(FF // FF_PIECE):
        span = slice(j * FF_PIECE, (j + 1) * FF_PIECE)
        du = (matmul_nt(gb, w_down[span, :]) * slope_ref[:, span].astype(F32)).astype(BF)
        d_ref[:, span] = du
        add(5 + j, du.astype(F32))
        db = db + matmul_nt(du, w_up[:, span])
    s2, inv2 = layer_norm(h1_ref[...])
    add(1, db * s2)
    add(3, db)
    dh1 = g + norm_back(db, s2, inv2, gains[1:2, :])
    add(4, dh1)
    gh = dh1.astype(BF)
    d_ref[:, D_GH:D_QKV] = gh
    do = matmul_nt(gh, w_out[...]).astype(BF)
    kt_ref[...] = qkv_ref[:, D : 2 * D].T
    masks = head_masks()

    def do_pair(head):
        return do[:, head // 2 * 128 : (head // 2 + 1) * 128]

    dpts = [matmul_nt(head_pair(qkv_ref, 2 * D, head) * masks[head % 2], do_pair(head)) for head in range(HEADS)]

    def both(parts, pair, make):
        return matmul_nn(
            jnp.concatenate(parts[2 * pair : 2 * pair + 2], axis=1),
            jnp.concatenate([make(2 * pair) * masks[0], make(2 * pair) * masks[1]], axis=0),
        )

    base = D_QKV + D
    for pair in range(HEADS // 2):
        dv = both([pt_ref[head] for head in range(HEADS)], pair, do_pair)
        d_ref[:, base + D + pair * 128 : base + D + (pair + 1) * 128] = dv.astype(BF)
    dsts = []
    for head in range(HEADS):
        ptf = pt_ref[head].astype(F32)
        dsts.append((ptf * (dpts[head] - column_sum(dpts[head] * ptf))).astype(BF))
    for pair in range(HEADS // 2):
        dk = both(dsts, pair, lambda head: head_pair(qkv_ref, 0, head))
        d_ref[:, base + pair * 128 : base + (pair + 1) * 128] = (dk * HEAD_SCALE).astype(BF)
    for head in range(HEADS):
        span = slice(head * HD, (head + 1) * HD)
        qt_ref[span, :] = (matmul_nn(kt_ref[span, :], dsts[head]) * HEAD_SCALE).astype(BF)
    d_ref[:, D_QKV : D_QKV + D] = qt_ref[...].T
    da = matmul_nt(d_ref[:, D_QKV:D_GB], w_qkv[...])
    s1, inv1 = layer_norm(x_ref[...].astype(F32))
    add(0, da * s1)
    add(2, da)
    dh = dh1 + norm_back(da, s1, inv1, gains[0:1, :])
    dh_ref[...] = dh
    dhb_ref[...] = dh.astype(BF)


WEIGHT_SHAPES = ((2, D), (2, D), (D, QKV), (D, D), (1, D), (D, FF), (1, FF), (FF, D), (1, D))


def weight_specs():
    def whole(shape):
        return pl.BlockSpec(shape, lambda *_: (0, 0), pipeline_mode=pl.Buffered(1))

    return [whole(shape) for shape in WEIGHT_SHAPES]


def block_forward(x, weights):
    rows = x.shape[0]
    images = rows // SEQ

    def row_block(width):
        return pl.BlockSpec((SEQ, width), lambda i: (i, 0))

    def body(x_ref, *refs):
        forward_image(x_ref, refs[:9], *refs[9:])

    def shape(width, dtype):
        return jax.ShapeDtypeStruct((rows, width), dtype)

    return pl.pallas_call(
        body,
        grid=(images,),
        in_specs=[row_block(D)] + weight_specs(),
        out_specs=[
            row_block(L_ALL),
            row_block(QKV),
            pl.BlockSpec((HEADS, SEQ, SEQ), lambda i: (i, 0, 0)),
            row_block(FF),
            row_block(D),
            row_block(D),
            row_block(D),
        ],
        out_shape=[
            shape(L_ALL, BF),
            shape(QKV, BF),
            jax.ShapeDtypeStruct((images * HEADS, SEQ, SEQ), BF),
            shape(FF, BF),
            shape(D, F32),
            shape(D, F32),
            shape(D, BF),
        ],
        scratch_shapes=[pltpu.VMEM((D, SEQ), BF), pltpu.VMEM((D, SEQ), BF)],
        compiler_params=pltpu.CompilerParams(vmem_limit_bytes=VMEM_BYTES),
        name="block_forward",
    )(x, *weights)


def block_backward(which, flags, result, other, arrived, x, weights, qkv, pt, slope, h1, vec, d, dh):
    rows = x.shape[0]

    def row_block(width):
        return pl.BlockSpec((SEQ, width), lambda i, which_ref: (which_ref[0], 0))

    def whole(height, width):
        return pl.BlockSpec((height, width), lambda i, which_ref: (0, 0))

    def body(which_ref, flags_ref, out_ref, other_ref, arrived_ref, x_ref, *refs):
        weight_refs = refs[:9]
        qkv_ref, pt_ref, slope_ref, h1_ref, vec_in = refs[9:14]
        d_ref, dh_ref, vec_out, dhb_ref, kt_ref, qt_ref = refs[-6:]
        vec_out[...] = jnp.zeros_like(vec_out)
        backward_image(
            flags_ref[0], flags_ref[2] > 0, out_ref, other_ref, arrived_ref, x_ref, weight_refs, qkv_ref, pt_ref,
            slope_ref, h1_ref, d_ref, vec_out, dh_ref, dhb_ref, kt_ref, qt_ref,
        )
        diff = out_ref[...] - other_ref[...].astype(F32)
        vec_out[V_LOSS : V_LOSS + 1, :D] = column_sum(diff * diff * flags_ref[0])
        vec_out[...] = vec_in[...] + vec_out[...] * flags_ref[1]

    keep = [] if d is None else [d, dh]
    first_kept = 2 + 4 + 9 + 5
    return pl.pallas_call(
        body,
        grid_spec=pltpu.PrefetchScalarGridSpec(
            num_scalar_prefetch=1,
            grid=(1,),
            in_specs=[pl.BlockSpec(memory_space=pltpu.SMEM), row_block(D), row_block(D), whole(SEQ, D), row_block(D)]
            + weight_specs()
            + [
                row_block(QKV),
                pl.BlockSpec((HEADS, SEQ, SEQ), lambda i, which_ref: (which_ref[0], 0, 0)),
                row_block(FF),
                row_block(D),
                whole(V_ROWS, V_COLS),
            ]
            + [pl.BlockSpec(memory_space=pl.ANY)] * len(keep),
            out_specs=[row_block(D_ALL), row_block(D), whole(V_ROWS, V_COLS), whole(SEQ, D)],
            scratch_shapes=[pltpu.VMEM((D, SEQ), BF), pltpu.VMEM((D, SEQ), BF)],
        ),
        out_shape=[
            jax.ShapeDtypeStruct((rows, D_ALL), BF),
            jax.ShapeDtypeStruct((rows, D), F32),
            jax.ShapeDtypeStruct((V_ROWS, V_COLS), F32),
            jax.ShapeDtypeStruct((SEQ, D), BF),
        ],
        input_output_aliases={first_kept: 0, first_kept + 1: 1} if keep else {},
        compiler_params=pltpu.CompilerParams(vmem_limit_bytes=VMEM_BYTES),
        name="block_backward",
    )(which, flags, result, other, arrived, x, *weights, qkv, pt, slope, h1, vec, *keep)


IMAGES = 4
SHARD = 208
SLICES = 3
SLICE = D // SLICES


def blocks_kernel(
    patches_ref, targets_ref, ids_ref, codebook_ref, gains, shifts, w_qkv_ref, w_out_ref, out_bias, w_up_ref, up_bias,
    w_down_ref, down_bias, result_ref, dh_ref, l_ref, d_ref, vec_ref,
    w_qkv, w_out, w_up, w_down, shards, ids_col, rows_buf, crossing, loss_buf, loss_side,
    qkv, pt, slope, h1, result, l_buf, d_buf, result_buf, dh_buf, vt, ot,
    w_sem, in_sem, out_sem, r_in, s_z, s_y, s_x, s_c, r_c, s_loss, r_loss, sx, rx,
):
    section, dp = lax.axis_index("section"), lax.axis_index("dp")
    core, y, z = dp % 2, (dp // 2) % 2, dp // 4
    across = (section, dp + 1 - 2 * core)
    along_y = (section, dp + 2 - 4 * y)
    along_z = [(section, (z + k) % 4 * 4 + y * 2 + core) for k in (1, 2, 3)]
    beside = (1 - section, dp)

    big = ((w_qkv_ref, w_qkv), (w_out_ref, w_out), (w_up_ref, w_up), (w_down_ref, w_down))
    loads = [pltpu.make_async_copy(src, dst, w_sem.at[i]) for i, (src, dst) in enumerate(big)]
    for load in loads:
        load.start()
    patch_load = pltpu.make_async_copy(patches_ref, rows_buf.at[0], in_sem)
    target_load = pltpu.make_async_copy(targets_ref, rows_buf.at[1], in_sem)

    @pl.when(section == 0)
    def _():
        patch_load.start()

    @pl.when(section == 1)
    def _():
        target_load.start()

    rows_here = codebook_ref.shape[0]
    for p in range(SLICES):
        shards[dp, p] = jnp.zeros((SHARD, SLICE), BF)
        shards[dp, p, :rows_here] = codebook_ref[:, p * SLICE : (p + 1) * SLICE]

    barrier = pltpu.get_barrier_semaphore()
    for target in [across, along_y, beside] + along_z:
        pl.semaphore_signal(barrier, inc=1, device_id=target, device_id_type=MESH)
    pl.semaphore_wait(barrier, 6)

    home = section == core
    corner = (z == 0) | (z == 3)
    near_1 = jnp.where(z == 0, 3, 1)
    near_2 = jnp.where(corner, 2, 3)
    near_3 = jnp.where(z == 0, 1, jnp.where(z == 3, 3, 2))
    def place_of(number):
        return (z - number % 4 + 4) % 4 * 4 + (y + number // 4) % 2 * 2 + core

    def move(place, p, send, recv, target):
        part = shards.at[place, p]
        return pltpu.make_async_remote_copy(part, part, send.at[p], recv.at[p], device_id=target, device_id_type=MESH)

    def send_z(order, place, up, p):
        towards = jnp.where(up, z + 1, z - 1)
        number = (towards - place // 4 + 4) % 4
        return move(place, p, s_z.at[order], r_in.at[number], (section, towards * 4 + y * 2 + core))

    def pass_on(e, p):
        up = (e == 1) | ((e == 5) & (z == 2))
        return send_z((e + 3) // 2, place_of(number_at(e)), up, p)

    def send_y(order, number, p):
        return move(place_of(number), p, s_y.at[order], r_in.at[4 + number], along_y)

    def send_x(order, number, p):
        return move(place_of(number), p, s_x.at[order], r_in.at[number], beside)

    def send_core(order, number, p):
        return move(place_of(number), p, s_c.at[order], r_c.at[order], across)

    pieces = range(SLICES)

    def number_at(e):
        pairs = ((1, near_1), (2, 4), (3, near_2), (4, 4 + near_1), (5, near_3), (6, 4 + near_2), (7, 4 + near_3))
        number = 0
        for at, value in pairs:
            number = jnp.where(e == at, value, number)
        return number

    for p in pieces:

        @pl.when(z < 3)
        def _():
            send_z(0, dp, True, p).start()

        @pl.when(z > 0)
        def _():
            send_z(1, dp, False, p).start()

        send_y(0, 0, p).start()
        send_core(0, 0, p).start()

    vec_ref[...] = jnp.zeros_like(vec_ref)
    loss_buf[...] = jnp.zeros_like(loss_buf)
    ids_col[...] = jnp.broadcast_to(ids_ref[...], (128, IMAGES * SEQ)).T
    lane = lax.broadcasted_iota(jnp.int32, (IMAGES * SEQ, 128), 1)
    dest = 1 - section

    def pick(place, first=False):
        rel = ids_col[...] - place * rows_here
        low = (rel == lane).astype(F32)
        high = ((rel - 128 == lane) & (lane < rows_here - 128)).astype(F32)
        one_hot = jnp.concatenate([low, high], axis=1)
        vec_ref[pl.ds(place, 1), D:] = column_sum(one_hot)
        one_hot = one_hot[:, :SHARD].astype(BF)
        for i in range(IMAGES):
            for p in pieces:
                rows = matmul_nn(one_hot[i * SEQ : (i + 1) * SEQ], shards[place, p]).astype(BF)
                cols = slice(p * SLICE, (p + 1) * SLICE)
                rows_buf[dest, i, :, cols] = rows if first else rows_buf[dest, i, :, cols] + rows

    def pick_core(e):
        for p in pieces:
            send_core(e, number_at(e), p).wait_recv()
        pick(place_of(number_at(e)) + 1 - 2 * core)

    def event(e, carry):
        number = number_at(e)
        near = (e == 1) | (e == 3) | (e == 5)
        for p in pieces:
            move(place_of(number), p, s_c.at[e], r_in.at[number], across).wait_recv()

            @pl.when(home & near & jnp.logical_not(corner))
            def _():
                pass_on(e, p).start()

            @pl.when(home & near)
            def _():
                send_y((e + 1) // 2, number, p).start()

            @pl.when(home & ((e >= 4) | ((e == 3) & corner)))
            def _():
                send_x(e - 3, number, p).start()

            send_core(e, number, p).start()
        pick(place_of(number))
        pick_core(e - 1)
        return carry

    pick(dp, True)
    lax.fori_loop(1, 8, event, 0)
    pick_core(7)

    for p in pieces:

        @pl.when(z < 3)
        def _():
            send_z(0, dp, True, p).wait_send()

        @pl.when(z > 0)
        def _():
            send_z(1, dp, False, p).wait_send()

        send_y(0, 0, p).wait_send()

        @pl.when(home)
        def _():
            for order in (1, 2, 3):
                send_y(order, number_at(2 * order - 1), p).wait_send()
            for e in (4, 5, 6, 7):
                send_x(e - 3, number_at(e), p).wait_send()

        @pl.when(home & jnp.logical_not(corner))
        def _():
            for e in (1, 3, 5):
                pass_on(e, p).wait_send()

        @pl.when(home & corner)
        def _():
            send_x(0, number_at(3), p).wait_send()

        for e in range(8):
            send_core(e, number_at(e), p).wait_send()
    for load in loads:
        load.wait()

    @pl.when(section == 0)
    def _():
        patch_load.wait()

    @pl.when(section == 1)
    def _():
        target_load.wait()

    weights = (gains, shifts, w_qkv, w_out, out_bias, w_up, up_bias, w_down, down_bias)
    scale = jnp.where(section == 0, COMMIT_WEIGHT, 1.0)

    def rows_of(ref, image):
        return ref.at[pl.ds(pl.multiple_of(image * SEQ, SEQ), SEQ)]

    def stores(image, forward):
        pairs = ((l_buf, l_ref), (result_buf, result_ref)) if forward else ((d_buf, d_ref), (dh_buf, dh_ref))
        first = 0 if forward else 2
        return [
            pltpu.make_async_copy(src, rows_of(dst, image), out_sem.at[first + i]) for i, (src, dst) in enumerate(pairs)
        ]

    def cross(image):
        return pltpu.make_async_remote_copy(
            crossing.at[image], crossing.at[image], sx.at[image], rx.at[image], device_id=beside, device_id_type=MESH
        )

    trade = pltpu.make_async_remote_copy(loss_buf, loss_side, s_loss, r_loss, device_id=beside, device_id_type=MESH)

    def step(i, carry):
        even = i % 2 == 0
        ahead = jnp.where(section == 1, even, (i == 0) | ((i % 2 == 1) & (i < 7)))

        @pl.when(ahead)
        def _():
            image = (i + 1) // 2
            slot = image % 2

            @pl.when(image > 0)
            def _():
                for copy in stores(image - 1, True):
                    copy.wait()

            forward_image(
                rows_buf.at[0, image], weights, l_buf, qkv.at[slot], pt.at[slot], slope.at[slot], h1.at[slot],
                result.at[slot], result_buf, vt, ot,
            )
            diff = result[slot] - rows_buf[1, image].astype(F32)
            loss_buf[0:1, :] += column_sum(diff * diff * scale)
            for copy in stores(image, True):
                copy.start()

            @pl.when(image == IMAGES - 1)
            def _():
                trade.start()

        @pl.when(jnp.logical_not(ahead))
        def _():
            image = (i - 1) // 2
            slot = image % 2

            @pl.when(image > 0)
            def _():
                for copy in stores(image - 1, False):
                    copy.wait()

            @pl.when(section == 0)
            def _():
                cross(image).wait_recv()

            backward_image(
                scale, section == 0, result.at[slot], rows_buf.at[1, image], crossing.at[image], rows_buf.at[0, image], weights,
                qkv.at[slot], pt.at[slot], slope.at[slot], h1.at[slot], d_buf, vec_ref, dh_buf, crossing.at[image],
                vt, ot,
            )

            @pl.when(section == 1)
            def _():
                cross(image).start()

            for copy in stores(image, False):
                copy.start()

        return carry

    lax.fori_loop(0, 2 * IMAGES, step, 0)
    for forward in (True, False):
        for copy in stores(IMAGES - 1, forward):
            copy.wait()

    @pl.when(section == 1)
    def _():
        for image in range(IMAGES):
            cross(image).wait_send()

    trade.wait()
    vec_ref[V_LOSS : V_LOSS + 1, :D] = loss_buf[0:1, :]
    vec_ref[V_SIDE : V_SIDE + 1, :D] = loss_side[0:1, :]


def run_blocks(patches, targets, ids, codebook, weights):
    dma = pltpu.SemaphoreType.DMA
    vm = pltpu.VMEM
    rows = IMAGES * SEQ
    inside, outside = pl.BlockSpec(memory_space=pltpu.VMEM), pl.BlockSpec(memory_space=pl.ANY)
    weight_places = [inside, inside, outside, outside, inside, outside, inside, outside, inside]
    return pl.pallas_call(
        blocks_kernel,
        out_shape=[
            jax.ShapeDtypeStruct((rows, D), BF),
            jax.ShapeDtypeStruct((rows, D), F32),
            jax.ShapeDtypeStruct((rows, L_ALL), BF),
            jax.ShapeDtypeStruct((rows, D_ALL), BF),
            jax.ShapeDtypeStruct((V_ROWS, V_COLS), F32),
        ],
        in_specs=[outside, outside, inside, inside] + weight_places,
        out_specs=[outside] * 4 + [inside],
        scratch_shapes=[
            vm((D, QKV), BF), vm((D, D), BF), vm((D, FF), BF), vm((FF, D), BF),
            vm((16, SLICES, SHARD, SLICE), BF), vm((rows, 128), jnp.int32),
            vm((2, IMAGES, SEQ, D), BF), vm((IMAGES, SEQ, D), BF), vm((8, D), F32), vm((8, D), F32),
            vm((2, SEQ, QKV), BF), vm((2, HEADS, SEQ, SEQ), BF), vm((2, SEQ, FF), BF), vm((2, SEQ, D), F32),
            vm((2, SEQ, D), F32), vm((SEQ, L_ALL), BF), vm((SEQ, D_ALL), BF), vm((SEQ, D), BF), vm((SEQ, D), F32),
            vm((D, SEQ), BF), vm((D, SEQ), BF),
            dma((4,)), dma(()), dma((4,)), dma((8, SLICES)), dma((5, SLICES)),
            dma((4, SLICES)), dma((5, SLICES)), dma((8, SLICES)), dma((8, SLICES)), dma(()), dma(()),
            dma((IMAGES,)), dma((IMAGES,)),
        ],
        compiler_params=pltpu.CompilerParams(collective_id=2, has_side_effects=True, vmem_limit_bytes=VMEM_BYTES),
        name="blocks",
    )(patches.reshape(IMAGES, SEQ, D), targets.reshape(IMAGES, SEQ, D), ids.reshape(1, rows), codebook, *weights)


UNITS = 36
PART = D // 16
COLS = 256
LAG_Y, LAG_Z, HOP = 1, 4, 3
LAG_OUT = LAG_Z + 3 * HOP
BLOCKS = D_ALL // COLS
FIRST_DOWN = 24
EVERY, EARLY = 6, UNITS // 6
LAG_LAST = 3
RING = 16


def reduce_kernel(
    vocab, l_ref, d_ref, vec_ref, qkv_out, out_out, up_out, down_out, vec_out, hist_out, stats_out,
    left, right, product, acc_y, acc_z, tx_c, rx_c, tx_y, rx_y, tx_up, rx_up, tx_dn, rx_dn,
    acc_e, tx_eu, rx_eu, tx_ed, rx_ed, acc_l, tx_l, rx_l, vec_tx, vec_c, vec_y, vec_z,
    lsem, dsem, sc, rc, sy, ry, s_up, r_up, s_dn, r_dn,
    s_eu, r_eu, s_ed, r_ed, s_l, r_l, sv, rv,
):
    sec, dp = lax.axis_index("section"), lax.axis_index("dp")
    core, y, z = dp % 2, (dp // 2) % 2, dp // 4
    across = (sec, dp + 1 - 2 * core)
    along_y = (sec, dp + 2 - 4 * y)
    along_z = [(sec, (z + k) % 4 * 4 + y * 2 + core) for k in (1, 2, 3)]
    above, below = (sec, jnp.minimum(dp + 4, 12 + dp % 4)), (sec, jnp.maximum(dp - 4, dp % 4))

    lefts = [pltpu.make_async_copy(l_ref.at[:, i * D : (i + 1) * D], left.at[i], lsem.at[i]) for i in range(7)]

    def load_right(n):
        cols = pl.ds(pl.multiple_of(n * COLS, COLS), COLS)
        return pltpu.make_async_copy(d_ref.at[:, cols], right.at[n % 2], dsem.at[n % 2])

    lefts[0].start()
    load_right(0).start()

    barrier = pltpu.get_barrier_semaphore()
    for target in [across, along_y] + along_z:
        pl.semaphore_signal(barrier, inc=1, device_id=target, device_id_type=MESH)
    pl.semaphore_wait(barrier, 5)

    def remote(src, dst, send, recv, target):
        return pltpu.make_async_remote_copy(src, dst, send, recv, device_id=target, device_id_type=MESH)

    def send_core(u):
        return remote(tx_c.at[u % 2], rx_c.at[u], sc.at[u % 2], rc.at[u], across)

    def send_y(u):
        return remote(tx_y.at[u % RING], rx_y.at[u], sy.at[u % RING], ry.at[u], along_y)

    def send_up(u, d):
        return remote(tx_up.at[u % RING, d], rx_up.at[u, d], s_up.at[u % RING, d], r_up.at[u, d], above)

    def send_dn(u, d):
        return remote(tx_dn.at[u % RING, d], rx_dn.at[u, d], s_dn.at[u % RING, d], r_dn.at[u, d], below)

    def early_up(u, h, d):
        return remote(tx_eu.at[u, h, d], rx_eu.at[u, h, d], s_eu.at[u, h, d], r_eu.at[u, h, d], above)

    def early_dn(u, h, d):
        return remote(tx_ed.at[u, h, d], rx_ed.at[u, h, d], s_ed.at[u, h, d], r_ed.at[u, h, d], below)

    def send_last(u):
        return remote(tx_l.at[u], rx_l.at[u], s_l.at[u], r_l.at[u], along_y)

    def is_early(u):
        return u % EVERY == 2

    def valid(u):
        return (u >= 0) & (u < UNITS)

    def climb(quarter, tx, rx, send):
        for d in range(3):

            @pl.when((z > 0) & (d + 1 >= z))
            def _():
                send(d).wait_recv()

            @pl.when(d + 1 > z)
            def _():
                got = jnp.where(z > 0, rx[d].astype(F32), 0.0)
                tx[d] = (quarter(d + 1) + got).astype(BF)
                send(d).start()

    def sink(quarter, tx, rx, send):
        for d in range(3):

            @pl.when((z < 3) & (d <= z))
            def _():
                send(d).wait_recv()

            @pl.when(d < z)
            def _():
                got = jnp.where(z < 3, rx[d].astype(F32), 0.0)
                tx[d] = (quarter(d) + got).astype(BF)
                send(d).start()

    def settle(quarter_own, rx_above, rx_below, up, dn):
        for d in range(3):

            @pl.when(d + 1 > z)
            def _():
                up(d).wait_send()

            @pl.when(d < z)
            def _():
                dn(d).wait_send()

        from_below = jnp.where(z > 0, rx_above[jnp.maximum(z - 1, 0)].astype(F32), 0.0)
        from_above = jnp.where(z < 3, rx_below[jnp.minimum(z, 2)].astype(F32), 0.0)
        return quarter_own + from_below + from_above

    vec_core = remote(vec_ref, vec_c, sv.at[0], rv.at[0], across)
    vec_along_y = remote(vec_tx, vec_y, sv.at[1], rv.at[1], along_y)
    vec_along_z = [remote(vec_z.at[z], vec_z.at[z], sv.at[2 + k], rv.at[2 + k], along_z[k]) for k in range(3)]
    vec_core.start()

    def multiply(u):
        down = u >= FIRST_DOWN
        n = jnp.where(down, FIRST_DOWN + (u - FIRST_DOWN) // 4, u)
        fresh = jnp.logical_not(down) | (u % 4 == 0)

        @pl.when(fresh & (n + 1 < BLOCKS))
        def _():
            load_right(n + 1).start()

        @pl.when(fresh)
        def _():
            load_right(n).wait()

        @pl.when(u == 1)
        def _():
            for load in lefts[1:]:
                load.start()

        for i, first in enumerate((0, 12, 15, FIRST_DOWN)):

            @pl.when(u == first)
            def _():
                for load in lefts[i : i + 1] if i < 3 else lefts[3:]:
                    load.wait()

        @pl.when(jnp.logical_not(down))
        def _():
            which = jnp.where(u < 12, 0, jnp.where(u < 15, 1, 2))
            product[:D] = matmul_tn(left[which], right[n % 2])

        @pl.when(down & fresh)
        def _():
            for i in range(4):
                product[i * D : (i + 1) * D] = matmul_tn(left[3 + i], right[n % 2])

        def rows_for(place):
            owner = place % 4 * 4 + (y + place // 4 % 2) % 2 * 2 + (core + place // 8) % 2
            row = jnp.where(down, owner * (4 * PART) + u % 4 * PART, owner * PART)
            return product[pl.ds(pl.multiple_of(row, PART), PART), :]

        for place in range(8):
            tx_c[u % 2, place * PART : (place + 1) * PART] = rows_for(8 + place).astype(BF)
        send_core(u).start()
        for place in range(8):
            acc_y[u % 2, place * PART : (place + 1) * PART] = rows_for(place)

    def step(i, carry):
        @pl.when(i < UNITS)
        def _():
            multiply(i)

        @pl.when((i >= LAG_Y) & (i < UNITS + LAG_Y))
        def _():
            u = i - LAG_Y
            send_core(u).wait()

            @pl.when(is_early(u))
            def _():
                acc_e[u // EVERY] = acc_y[u % 2] + rx_c[u].astype(F32)

            @pl.when(jnp.logical_not(is_early(u)))
            def _():
                tx_y[u % RING] = (acc_y[u % 2, 4 * PART :] + rx_c[u, 4 * PART :].astype(F32)).astype(BF)
                send_y(u).start()
                acc_z[u % RING] = acc_y[u % 2, : 4 * PART] + rx_c[u, : 4 * PART].astype(F32)

        @pl.when(valid(i - LAG_Z) & jnp.logical_not(is_early(i - LAG_Z)))
        def _():
            u = i - LAG_Z
            send_y(u).wait()
            acc_z[u % RING] = acc_z[u % RING] + rx_y[u].astype(F32)

        def quarter(u):
            return lambda d: acc_z[u % RING, d * PART : (d + 1) * PART]

        def early_quarter(u, h):
            return lambda d: acc_e[u, (4 * h + d) * PART : (4 * h + d + 1) * PART]

        u_up = i - LAG_Z - z * HOP

        @pl.when(valid(u_up) & jnp.logical_not(is_early(u_up)))
        def _():
            climb(quarter(u_up), tx_up.at[u_up % RING], rx_up.at[u_up], functools.partial(send_up, u_up))

        @pl.when(valid(u_up) & is_early(u_up))
        def _():
            e = u_up // EVERY
            for h in range(2):
                climb(early_quarter(e, h), tx_eu.at[e, h], rx_eu.at[e, h], functools.partial(early_up, e, h))

        u_dn = i - LAG_Z - (3 - z) * HOP

        @pl.when(valid(u_dn) & jnp.logical_not(is_early(u_dn)))
        def _():
            sink(quarter(u_dn), tx_dn.at[u_dn % RING], rx_dn.at[u_dn], functools.partial(send_dn, u_dn))

        @pl.when(valid(u_dn) & is_early(u_dn))
        def _():
            e = u_dn // EVERY
            for h in range(2):
                sink(early_quarter(e, h), tx_ed.at[e, h], rx_ed.at[e, h], functools.partial(early_dn, e, h))

        own = pl.ds(pl.multiple_of(z * PART, PART), PART)

        def put(u, t):
            def lanes(n):
                return pl.ds(pl.multiple_of(n * COLS, COLS), COLS)

            @pl.when(u < 12)
            def _():
                up_out[:, lanes(u)] = t

            @pl.when((u >= 12) & (u < 15))
            def _():
                out_out[:, lanes(u - 12)] = t

            @pl.when((u >= 15) & (u < FIRST_DOWN))
            def _():
                qkv_out[:, lanes(u - 15)] = t

            @pl.when(u >= FIRST_DOWN)
            def _():
                rows = pl.ds(pl.multiple_of(u % 4 * PART, PART), PART)
                down_out[rows, lanes((u - FIRST_DOWN) // 4)] = t

        @pl.when(valid(i - LAG_OUT) & is_early(i - LAG_OUT))
        def _():
            e = (i - LAG_OUT) // EVERY
            for h in range(2):
                rows = pl.ds(pl.multiple_of((4 * h + z) * PART, PART), PART)
                t = settle(
                    acc_e[e, rows, :], rx_eu.at[e, h], rx_ed.at[e, h],
                    functools.partial(early_up, e, h), functools.partial(early_dn, e, h),
                )
                if h == 0:
                    acc_l[e] = t
                else:
                    tx_l[e] = t.astype(BF)
                    send_last(e).start()

        @pl.when(valid(i - LAG_OUT - LAG_LAST) & is_early(i - LAG_OUT - LAG_LAST))
        def _():
            u = i - LAG_OUT - LAG_LAST
            e = u // EVERY
            send_last(e).wait()
            put(u, acc_l[e] + rx_l[e].astype(F32))

        @pl.when(valid(i - LAG_OUT) & jnp.logical_not(is_early(i - LAG_OUT)))
        def _():
            u = i - LAG_OUT
            put(u, settle(
                acc_z[u % RING, own, :], rx_up.at[u], rx_dn.at[u],
                functools.partial(send_up, u), functools.partial(send_dn, u),
            ))

        @pl.when(i == 3)
        def _():
            vec_core.wait()
            vec_tx[...] = vec_ref[...] + vec_c[...]
            vec_along_y.start()

        @pl.when(i == 8)
        def _():
            vec_along_y.wait()
            vec_z[z] = vec_tx[...] + vec_y[...]
            for copy in vec_along_z:
                copy.start()

        @pl.when(i == 14)
        def _():
            for copy in vec_along_z:
                copy.wait()
            vec_out[...] = (vec_z[0] + vec_z[1]) + (vec_z[2] + vec_z[3])

        return carry

    lax.fori_loop(0, UNITS + LAG_OUT, step, 0)

    def total(value):
        return jnp.sum(jnp.sum(value, axis=1, keepdims=True), axis=0, keepdims=True)

    tokens = 16 * l_ref.shape[0]
    counts = vec_out[:, D:]
    shares = counts * (1.0 / tokens)
    entropy = -total(shares * jnp.log(jnp.where(counts > 0, shares, 1.0)))
    used = total((counts > 0).astype(F32))
    loss = total(vec_out[V_LOSS : V_LOSS + 1, :D]) + total(vec_out[V_SIDE : V_SIDE + 1, :D])
    lane = lax.broadcasted_iota(jnp.int32, (8, 128), 1)
    last = jnp.where(lane == 1, used / vocab, jnp.exp(entropy) / vocab)
    stats_out[...] = jnp.where(lane == 0, loss / (tokens * D), last)
    hist_out[...] = vec_out[pl.ds(dp, 1), D:].astype(jnp.int32)


def reduce_weights(l, d, vec, vocab):
    dma = pltpu.SemaphoreType.DMA
    vm = pltpu.VMEM
    rows = l.shape[0]
    sums = (V_ROWS, V_COLS)
    return pl.pallas_call(
        functools.partial(reduce_kernel, vocab),
        out_shape=[
            jax.ShapeDtypeStruct((PART, QKV), F32),
            jax.ShapeDtypeStruct((PART, D), F32),
            jax.ShapeDtypeStruct((PART, FF), F32),
            jax.ShapeDtypeStruct((4 * PART, D), F32),
            jax.ShapeDtypeStruct(sums, F32),
            jax.ShapeDtypeStruct((1, V_COLS - D), jnp.int32),
            jax.ShapeDtypeStruct((8, 128), F32),
        ],
        in_specs=[pl.BlockSpec(memory_space=pl.ANY)] * 2 + [pl.BlockSpec(memory_space=pltpu.VMEM)],
        out_specs=[pl.BlockSpec(memory_space=pltpu.VMEM)] * 7,
        scratch_shapes=[
            vm((7, rows, D), BF), vm((2, rows, COLS), BF), vm((4 * D, COLS), F32),
            vm((2, 8 * PART, COLS), F32), vm((RING, 4 * PART, COLS), F32),
            vm((2, 8 * PART, COLS), BF), vm((UNITS, 8 * PART, COLS), BF),
            vm((RING, 4 * PART, COLS), BF), vm((UNITS, 4 * PART, COLS), BF),
            vm((RING, 3, PART, COLS), BF), vm((UNITS, 3, PART, COLS), BF),
            vm((RING, 3, PART, COLS), BF), vm((UNITS, 3, PART, COLS), BF),
            vm((EARLY, 8 * PART, COLS), F32), vm((EARLY, 2, 3, PART, COLS), BF), vm((EARLY, 2, 3, PART, COLS), BF),
            vm((EARLY, 2, 3, PART, COLS), BF), vm((EARLY, 2, 3, PART, COLS), BF),
            vm((EARLY, PART, COLS), F32), vm((EARLY, PART, COLS), BF), vm((EARLY, PART, COLS), BF),
            vm(sums, F32), vm(sums, F32), vm(sums, F32), vm((4,) + sums, F32),
            dma((7,)), dma((2,)), dma((2,)), dma((UNITS,)), dma((RING,)), dma((UNITS,)),
            dma((RING, 3)), dma((UNITS, 3)), dma((RING, 3)), dma((UNITS, 3)),
            dma((EARLY, 2, 3)), dma((EARLY, 2, 3)), dma((EARLY, 2, 3)), dma((EARLY, 2, 3)), dma((EARLY,)), dma((EARLY,)),
            dma((5,)), dma((5,)),
        ],
        compiler_params=pltpu.CompilerParams(collective_id=1, has_side_effects=True, vmem_limit_bytes=VMEM_BYTES),
        name="weight_grad_reduce",
    )(l, d, vec)


def finish(result, dh, g_qkv, g_out, g_up, g_down, vec):
    rows = result.shape[0]
    pieces = 4

    def body(result_ref, dh_ref, qkv_ref, out_ref, up_ref, down_ref, vec_ref,
             result_to, dh_to, gains_to, shifts_to, qkv_to, out_to, out_bias_to, up_to, up_bias_to, down_to, down_bias_to, *scratch):
        *bufs, into, outof = scratch
        copies = []
        for src, dst in ((dh_ref, dh_to), (result_ref, result_to)):
            for i in range(pieces):
                part = pl.ds(i * rows // pieces, rows // pieces)
                copies.append((src.at[part], dst.at[0, part]))
        copies += [(qkv_ref, qkv_to.at[0]), (out_ref, out_to.at[0]), (up_ref, up_to.at[0]), (down_ref, down_to.at[0])]
        loads, saves = [], []
        for i, (src, dst) in enumerate(copies):
            buf = bufs[i // pieces].at[i % pieces] if i < 2 * pieces else bufs[i - 2 * pieces + 2]
            loads.append(pltpu.make_async_copy(src, buf, into.at[i]))
            saves.append(pltpu.make_async_copy(buf, dst, outof.at[i]))
        for load in loads:
            load.start()
        for load, save in zip(loads, saves):
            load.wait()
            save.start()
        gains_to[0] = vec_ref[0:2, :D]
        shifts_to[0] = vec_ref[2:4, :D]
        out_bias_to[...] = vec_ref[4:5, :D]
        for j in range(FF // D):
            up_bias_to[:, j * D : (j + 1) * D] = vec_ref[5 + j : 6 + j, :D]
        down_bias_to[...] = vec_ref[9:10, :D]
        for save in saves:
            save.wait()

    inside, outside = pl.BlockSpec(memory_space=pltpu.VMEM), pl.BlockSpec(memory_space=pl.ANY)

    def shape(*dims, dtype=F32):
        return jax.ShapeDtypeStruct((1,) + dims, dtype)

    out = pl.pallas_call(
        body,
        out_shape=[
            shape(rows, D, dtype=BF), shape(rows, D), shape(2, D), shape(2, D), shape(PART, QKV), shape(PART, D),
            shape(D), shape(PART, FF), shape(FF), shape(4 * PART, D), shape(D),
        ],
        in_specs=[outside] * 6 + [inside],
        out_specs=[outside, outside, inside, inside, outside, outside, inside, outside, inside, outside, inside],
        scratch_shapes=[
            pltpu.VMEM((pieces, rows // pieces, D), F32), pltpu.VMEM((pieces, rows // pieces, D), BF),
            pltpu.VMEM((PART, QKV), F32), pltpu.VMEM((PART, D), F32), pltpu.VMEM((PART, FF), F32),
            pltpu.VMEM((4 * PART, D), F32),
            pltpu.SemaphoreType.DMA((2 * pieces + 4,)), pltpu.SemaphoreType.DMA((2 * pieces + 4,)),
        ],
        compiler_params=pltpu.CompilerParams(vmem_limit_bytes=VMEM_BYTES),
        name="place_outputs",
    )(result, dh, g_qkv, g_out, g_up, g_down, vec)
    return tuple(out)


def count_shares(counts, total_count):
    shares = counts / total_count
    nonzero_share = jnp.where(counts > 0, shares, 1.0)
    return -jnp.sum(shares * jnp.log(nonzero_share)), jnp.sum((counts > 0).astype(F32))


def on_device(
    patches, targets, code_ids, codebook, norm_gains, norm_shifts, w_qkv, w_out, out_bias, w_up, up_bias, w_down, down_bias
):
    section = lax.axis_index("section")
    leading = section == 0
    dp_size = lax.axis_size("dp")
    dp = lax.axis_index("dp")
    weights = (
        norm_gains[0], norm_shifts[0], w_qkv[0], w_out[0], out_bias, w_up[0], up_bias, w_down[0], down_bias
    )
    rows, width = patches.shape
    images = rows // SEQ
    vocab_local = codebook.shape[0]
    vocab_all = vocab_local * dp_size
    total_tokens = rows * dp_size

    small = dp_size == 16 and vocab_local <= SHARD and rows == IMAGES * SEQ
    if small:
        result_bf, dh, l, d, vec = run_blocks(patches, targets, code_ids, codebook, weights)
        g_qkv, g_out, g_up, g_down, vec, hist, stats = reduce_weights(l, d, vec, vocab_all)
        return finish(result_bf, dh, g_qkv, g_out, g_up, g_down, vec) + (hist[0, :vocab_local], stats[0, :3])
    else:
        shard_rows = lax.all_gather(codebook, "dp", axis=0, tiled=True)
        chosen = jnp.take(shard_rows, jnp.clip(code_ids, 0, vocab_all - 1), axis=0)
        x = jnp.where(leading, patches, chosen)
        l, qkv, pt, slope, h1, result, result_bf = block_forward(x, weights)
        other = jnp.where(leading, chosen, targets)
        d = dh = None
        vec = jnp.zeros((V_ROWS, V_COLS), F32)
        arrived = jnp.zeros((SEQ, D), BF)
        for moment in range(images + 1):
            which = jnp.clip(moment - 1 + section, 0, images - 1).astype(jnp.int32)[None]
            active = jnp.where(leading, moment >= 1, moment < images).astype(F32)
            flags = jnp.stack(
                [jnp.where(leading, COMMIT_WEIGHT, 1.0).astype(F32), active, jnp.where(leading, 1.0, 0.0).astype(F32)]
            )
            d, dh, vec, outgoing = block_backward(
                which, flags, result, other, arrived, x, weights, qkv, pt, slope, h1, vec, d, dh
            )
            if moment < images:
                arrived = lax.ppermute(outgoing, "section", [(1, 0)])
        pairs = (
            (l[:, L_A:L_M], d[:, D_QKV:D_GB]),
            (l[:, L_O:L_A], d[:, D_GH:D_QKV]),
            (l[:, :L_O], d[:, :D_GH]),
            (l[:, L_M:], d[:, D_GB:]),
        )
        g_qkv, g_out, g_up, g_down = (
            lax.psum_scatter(matmul_tn(left, right), "dp", scatter_dimension=0, tiled=True) for left, right in pairs
        )
        vocab_iota = lax.broadcasted_iota(jnp.int32, (1, vocab_all), 1)
        counts = jnp.sum((code_ids[:, None] == vocab_iota).astype(F32), axis=0)
        hist_local = lax.psum_scatter(counts, "dp", scatter_dimension=0, tiled=True)
        entropy_part, used_part = count_shares(hist_local, total_tokens)
        hist_local = hist_local.astype(jnp.int32)
        vec = lax.psum(vec, "dp")
        entropy_all, used_all = lax.psum((entropy_part, used_part), "dp")
        loss_all = lax.psum(jnp.sum(vec[V_LOSS, :D]), "section")
        stats = jnp.stack(
            [loss_all / (total_tokens * width), used_all / vocab_all, jnp.exp(entropy_all) / vocab_all]
        )
    return (
        result_bf[None],
        dh[None],
        vec[None, 0:2, :D],
        vec[None, 2:4, :D],
        g_qkv[None],
        g_out[None],
        vec[None, 4, :D],
        g_up[None],
        vec[5:9, :D].reshape(1, FF),
        g_down[None],
        vec[None, 9, :D],
        hist_local,
        stats,
    )


def solution(mesh):
    return jax.shard_map(
        on_device,
        mesh=mesh,
        in_specs=(
            P("dp", None),
            P("dp", None),
            P("dp"),
            P("dp", None),
            P("section", None, None),
            P("section", None, None),
            P("section", None, None),
            P("section", None, None),
            P("section", None),
            P("section", None, None),
            P("section", None),
            P("section", None, None),
            P("section", None),
        ),
        out_specs=(
            P("section", "dp", None),
            P("section", "dp", None),
            P("section", None, None),
            P("section", None, None),
            P("section", "dp", None),
            P("section", "dp", None),
            P("section", None),
            P("section", "dp", None),
            P("section", None),
            P("section", "dp", None),
            P("section", None),
            P("dp"),
            P(),
        ),
        check_vma=False,
    )
```

```python
import functools

import jax
import jax.numpy as jnp
from jax import lax
from jax.experimental import pallas as pl
from jax.experimental.pallas import tpu as pltpu
from jax.sharding import PartitionSpec as P

SEQ = 256
D = 768
HD = 64
HEADS = 12
FF = 3072
FF_PIECE = 768
QKV = 3 * D
L_O, L_A, L_M, L_ALL = D, 2 * D, 3 * D, 3 * D + FF
D_GH, D_QKV, D_GB, D_ALL = FF, FF + D, FF + D + QKV, FF + D + QKV + D
V_SIDE, V_LOSS, V_ROWS, V_COLS = 14, 15, 16, D + 256

COMMIT_WEIGHT = 0.25
EPSILON = 1e-06
SQRT_HALF = 0.5**0.5
INV_ROOT_TAU = 0.3989422804014327
LOG2_E = 1.4426950408889634
HEAD_SCALE = HD**-0.5
MESH = pl.DeviceIdType.MESH
BF, F32 = jnp.bfloat16, jnp.float32
VMEM_BYTES = 60 << 20


def matmul_nn(left, right):
    return jnp.dot(left, right, preferred_element_type=F32)


def matmul_nt(left, right):
    return lax.dot_general(left, right, (((1,), (1,)), ((), ())), preferred_element_type=F32)


def matmul_tn(left, right):
    return lax.dot_general(left, right, (((0,), (0,)), ((), ())), preferred_element_type=F32)


def layer_norm(rows_in):
    centered = rows_in - jnp.mean(rows_in, axis=-1, keepdims=True)
    inv_std = lax.rsqrt(jnp.mean(centered * centered, axis=-1, keepdims=True) + EPSILON)
    return centered * inv_std, inv_std


def norm_back(incoming, scaled, inv_std, gain_row):
    x = incoming * gain_row
    return inv_std * (
        x
        - jnp.mean(x, axis=-1, keepdims=True)
        - scaled * jnp.mean(x * scaled, axis=-1, keepdims=True)
    )


def column_sum(x):
    return jnp.sum(x, axis=0, keepdims=True)


def head_masks():
    low = lax.broadcasted_iota(jnp.int32, (1, 2 * HD), 1) < HD
    ones = low.astype(F32)
    return ones.astype(BF), (1.0 - ones).astype(BF)


def head_pair(ref, base, head):
    return ref[:, base + head // 2 * 128 : base + (head // 2 + 1) * 128]


def forward_image(x_ref, weights, l_ref, qkv_ref, pt_ref, slope_ref, h1_ref, out_ref, outb_ref, vt_ref, ot_ref):
    gains, shifts, w_qkv, w_out, out_bias, w_up, up_bias, w_down, down_bias = weights
    h = x_ref[...].astype(F32)
    s1, _ = layer_norm(h)
    a = (s1 * gains[0:1, :] + shifts[0:1, :]).astype(BF)
    l_ref[:, L_A:L_M] = a
    for j in range(3):
        qkv_ref[:, j * D : (j + 1) * D] = matmul_nn(a, w_qkv[:, j * D : (j + 1) * D]).astype(BF)
    vt_ref[...] = qkv_ref[:, 2 * D : 3 * D].T
    masks = head_masks()
    scores = [
        matmul_nt(head_pair(qkv_ref, D, head) * masks[head % 2], head_pair(qkv_ref, 0, head)) for head in range(HEADS)
    ]
    for head in range(HEADS):
        st = scores[head]
        e = jnp.exp2((st - jnp.max(st, axis=0, keepdims=True)) * (HEAD_SCALE * LOG2_E))
        pt_ref[head] = e * (1.0 / column_sum(e))
    for head in range(HEADS):
        span = slice(head * HD, (head + 1) * HD)
        ot_ref[span, :] = matmul_nn(vt_ref[span, :], pt_ref[head].astype(BF)).astype(BF)
    o = ot_ref[...].T
    l_ref[:, L_O:L_A] = o
    h1 = h + matmul_nn(o, w_out[...]) + out_bias[...]
    h1_ref[...] = h1
    s2, _ = layer_norm(h1)
    b = (s2 * gains[1:2, :] + shifts[1:2, :]).astype(BF)
    l_ref[:, 0:L_O] = b
    result = h1 + down_bias[...]
    for j in range(FF // FF_PIECE):
        span = slice(j * FF_PIECE, (j + 1) * FF_PIECE)
        u = matmul_nn(b, w_up[:, span]) + up_bias[:, span]
        half_curve = 0.5 + 0.5 * lax.erf(u * SQRT_HALF)
        m = (u * half_curve).astype(BF)
        l_ref[:, L_M + j * FF_PIECE : L_M + (j + 1) * FF_PIECE] = m
        slope = half_curve + u * jnp.exp(-0.5 * u * u) * INV_ROOT_TAU
        slope_ref[:, span] = slope
        result = result + matmul_nn(m, w_down[span, :])
    out_ref[...] = result
    outb_ref[...] = result.astype(BF)


def backward_image(
    scale, receives, out_ref, other_ref, arrived_ref, x_ref, weights, qkv_ref, pt_ref, slope_ref, h1_ref,
    d_ref, vec_ref, dh_ref, dhb_ref, kt_ref, qt_ref,
):
    gains, shifts, w_qkv, w_out, out_bias, w_up, up_bias, w_down, down_bias = weights
    diff = out_ref[...] - other_ref[...].astype(F32)

    def add(row, value):
        vec_ref[row : row + 1, :D] += column_sum(value)

    g = diff * scale + jnp.where(receives, arrived_ref[...].astype(F32), 0.0)
    gb = g.astype(BF)
    d_ref[:, D_GB:D_ALL] = gb
    add(9, g)
    db = jnp.zeros((SEQ, D), F32)
    for j in range(FF // FF_PIECE):
        span = slice(j * FF_PIECE, (j + 1) * FF_PIECE)
        du = (matmul_nt(gb, w_down[span, :]) * slope_ref[:, span]).astype(BF)
        d_ref[:, span] = du
        add(5 + j, du.astype(F32))
        db = db + matmul_nt(du, w_up[:, span])
    s2, inv2 = layer_norm(h1_ref[...])
    add(1, db * s2)
    add(3, db)
    dh1 = g + norm_back(db, s2, inv2, gains[1:2, :])
    add(4, dh1)
    gh = dh1.astype(BF)
    d_ref[:, D_GH:D_QKV] = gh
    do = matmul_nt(gh, w_out[...]).astype(BF)
    kt_ref[...] = qkv_ref[:, D : 2 * D].T
    masks = head_masks()

    def do_pair(head):
        return do[:, head // 2 * 128 : (head // 2 + 1) * 128]

    dpts = [matmul_nt(head_pair(qkv_ref, 2 * D, head) * masks[head % 2], do_pair(head)) for head in range(HEADS)]

    def both(parts, pair, make):
        return matmul_nn(
            jnp.concatenate(parts[2 * pair : 2 * pair + 2], axis=1),
            jnp.concatenate([make(2 * pair) * masks[0], make(2 * pair) * masks[1]], axis=0),
        )

    base = D_QKV + D
    for pair in range(HEADS // 2):
        dv = both([pt_ref[head].astype(BF) for head in range(HEADS)], pair, do_pair)
        d_ref[:, base + D + pair * 128 : base + D + (pair + 1) * 128] = dv.astype(BF)
    dsts = []
    for head in range(HEADS):
        ptf = pt_ref[head]
        dsts.append((ptf * (dpts[head] - column_sum(dpts[head] * ptf))).astype(BF))
    for pair in range(HEADS // 2):
        dk = both(dsts, pair, lambda head: head_pair(qkv_ref, 0, head))
        d_ref[:, base + pair * 128 : base + (pair + 1) * 128] = (dk * HEAD_SCALE).astype(BF)
    for head in range(HEADS):
        span = slice(head * HD, (head + 1) * HD)
        qt_ref[span, :] = (matmul_nn(kt_ref[span, :], dsts[head]) * HEAD_SCALE).astype(BF)
    d_ref[:, D_QKV : D_QKV + D] = qt_ref[...].T
    da = matmul_nt(d_ref[:, D_QKV:D_GB], w_qkv[...])
    s1, inv1 = layer_norm(x_ref[...].astype(F32))
    add(0, da * s1)
    add(2, da)
    dh = dh1 + norm_back(da, s1, inv1, gains[0:1, :])
    dh_ref[...] = dh
    dhb_ref[...] = dh.astype(BF)


WEIGHT_SHAPES = ((2, D), (2, D), (D, QKV), (D, D), (1, D), (D, FF), (1, FF), (FF, D), (1, D))


def weight_specs():
    def whole(shape):
        return pl.BlockSpec(shape, lambda *_: (0, 0), pipeline_mode=pl.Buffered(1))

    return [whole(shape) for shape in WEIGHT_SHAPES]


def block_forward(x, weights):
    rows = x.shape[0]
    images = rows // SEQ

    def row_block(width):
        return pl.BlockSpec((SEQ, width), lambda i: (i, 0))

    def body(x_ref, *refs):
        forward_image(x_ref, refs[:9], *refs[9:])

    def shape(width, dtype):
        return jax.ShapeDtypeStruct((rows, width), dtype)

    return pl.pallas_call(
        body,
        grid=(images,),
        in_specs=[row_block(D)] + weight_specs(),
        out_specs=[
            row_block(L_ALL),
            row_block(QKV),
            pl.BlockSpec((HEADS, SEQ, SEQ), lambda i: (i, 0, 0)),
            row_block(FF),
            row_block(D),
            row_block(D),
            row_block(D),
        ],
        out_shape=[
            shape(L_ALL, BF),
            shape(QKV, BF),
            jax.ShapeDtypeStruct((images * HEADS, SEQ, SEQ), F32),
            shape(FF, F32),
            shape(D, F32),
            shape(D, F32),
            shape(D, BF),
        ],
        scratch_shapes=[pltpu.VMEM((D, SEQ), BF), pltpu.VMEM((D, SEQ), BF)],
        compiler_params=pltpu.CompilerParams(vmem_limit_bytes=VMEM_BYTES),
        name="block_forward",
    )(x, *weights)


def block_backward(which, flags, result, other, arrived, x, weights, qkv, pt, slope, h1, vec, d, dh):
    rows = x.shape[0]

    def row_block(width):
        return pl.BlockSpec((SEQ, width), lambda i, which_ref: (which_ref[0], 0))

    def whole(height, width):
        return pl.BlockSpec((height, width), lambda i, which_ref: (0, 0))

    def body(which_ref, flags_ref, out_ref, other_ref, arrived_ref, x_ref, *refs):
        weight_refs = refs[:9]
        qkv_ref, pt_ref, slope_ref, h1_ref, vec_in = refs[9:14]
        d_ref, dh_ref, vec_out, dhb_ref, kt_ref, qt_ref = refs[-6:]
        vec_out[...] = jnp.zeros_like(vec_out)
        backward_image(
            flags_ref[0], flags_ref[2] > 0, out_ref, other_ref, arrived_ref, x_ref, weight_refs, qkv_ref, pt_ref,
            slope_ref, h1_ref, d_ref, vec_out, dh_ref, dhb_ref, kt_ref, qt_ref,
        )
        diff = out_ref[...] - other_ref[...].astype(F32)
        vec_out[V_LOSS : V_LOSS + 1, :D] = column_sum(diff * diff * flags_ref[0])
        vec_out[...] = vec_in[...] + vec_out[...] * flags_ref[1]

    keep = [] if d is None else [d, dh]
    first_kept = 2 + 4 + 9 + 5
    return pl.pallas_call(
        body,
        grid_spec=pltpu.PrefetchScalarGridSpec(
            num_scalar_prefetch=1,
            grid=(1,),
            in_specs=[pl.BlockSpec(memory_space=pltpu.SMEM), row_block(D), row_block(D), whole(SEQ, D), row_block(D)]
            + weight_specs()
            + [
                row_block(QKV),
                pl.BlockSpec((HEADS, SEQ, SEQ), lambda i, which_ref: (which_ref[0], 0, 0)),
                row_block(FF),
                row_block(D),
                whole(V_ROWS, V_COLS),
            ]
            + [pl.BlockSpec(memory_space=pl.ANY)] * len(keep),
            out_specs=[row_block(D_ALL), row_block(D), whole(V_ROWS, V_COLS), whole(SEQ, D)],
            scratch_shapes=[pltpu.VMEM((D, SEQ), BF), pltpu.VMEM((D, SEQ), BF)],
        ),
        out_shape=[
            jax.ShapeDtypeStruct((rows, D_ALL), BF),
            jax.ShapeDtypeStruct((rows, D), F32),
            jax.ShapeDtypeStruct((V_ROWS, V_COLS), F32),
            jax.ShapeDtypeStruct((SEQ, D), BF),
        ],
        input_output_aliases={first_kept: 0, first_kept + 1: 1} if keep else {},
        compiler_params=pltpu.CompilerParams(vmem_limit_bytes=VMEM_BYTES),
        name="block_backward",
    )(which, flags, result, other, arrived, x, *weights, qkv, pt, slope, h1, vec, *keep)


IMAGES = 4
SHARD = 208
SLICES = 3
SLICE = D // SLICES


def blocks_kernel(
    patches_ref, targets_ref, ids_ref, codebook_ref, gains, shifts, w_qkv_ref, w_out_ref, out_bias, w_up_ref, up_bias,
    w_down_ref, down_bias, result_ref, dh_ref, l_ref, d_ref, vec_ref,
    w_qkv, w_out, w_up, w_down, shards, ids_col, rows_buf, crossing, loss_buf, loss_side,
    qkv, pt, slope, h1, result, l_buf, d_buf, result_buf, dh_buf, vt, ot,
    w_sem, in_sem, out_sem, r_in, s_z, s_y, s_x, s_c, r_c, s_loss, r_loss, sx, rx,
):
    section, dp = lax.axis_index("section"), lax.axis_index("dp")
    core, y, z = dp % 2, (dp // 2) % 2, dp // 4
    across = (section, dp + 1 - 2 * core)
    along_y = (section, dp + 2 - 4 * y)
    along_z = [(section, (z + k) % 4 * 4 + y * 2 + core) for k in (1, 2, 3)]
    beside = (1 - section, dp)

    big = ((w_qkv_ref, w_qkv), (w_out_ref, w_out), (w_up_ref, w_up), (w_down_ref, w_down))
    loads = [pltpu.make_async_copy(src, dst, w_sem.at[i]) for i, (src, dst) in enumerate(big)]
    for load in loads:
        load.start()
    patch_load = pltpu.make_async_copy(patches_ref, rows_buf.at[0], in_sem)
    target_load = pltpu.make_async_copy(targets_ref, rows_buf.at[1], in_sem)

    @pl.when(section == 0)
    def _():
        patch_load.start()

    @pl.when(section == 1)
    def _():
        target_load.start()

    rows_here = codebook_ref.shape[0]
    for p in range(SLICES):
        shards[dp, p] = jnp.zeros((SHARD, SLICE), BF)
        shards[dp, p, :rows_here] = codebook_ref[:, p * SLICE : (p + 1) * SLICE]

    barrier = pltpu.get_barrier_semaphore()
    for target in [across, along_y, beside] + along_z:
        pl.semaphore_signal(barrier, inc=1, device_id=target, device_id_type=MESH)
    pl.semaphore_wait(barrier, 6)

    home = section == core
    corner = (z == 0) | (z == 3)
    near_1 = jnp.where(z == 0, 3, 1)
    near_2 = jnp.where(corner, 2, 3)
    near_3 = jnp.where(z == 0, 1, jnp.where(z == 3, 3, 2))
    def place_of(number):
        return (z - number % 4 + 4) % 4 * 4 + (y + number // 4) % 2 * 2 + core

    def move(place, p, send, recv, target):
        part = shards.at[place, p]
        return pltpu.make_async_remote_copy(part, part, send.at[p], recv.at[p], device_id=target, device_id_type=MESH)

    def send_z(order, place, up, p):
        towards = jnp.where(up, z + 1, z - 1)
        number = (towards - place // 4 + 4) % 4
        return move(place, p, s_z.at[order], r_in.at[number], (section, towards * 4 + y * 2 + core))

    def pass_on(e, p):
        up = (e == 1) | ((e == 5) & (z == 2))
        return send_z((e + 3) // 2, place_of(number_at(e)), up, p)

    def send_y(order, number, p):
        return move(place_of(number), p, s_y.at[order], r_in.at[4 + number], along_y)

    def send_x(order, number, p):
        return move(place_of(number), p, s_x.at[order], r_in.at[number], beside)

    def send_core(order, number, p):
        return move(place_of(number), p, s_c.at[order], r_c.at[order], across)

    pieces = range(SLICES)

    def number_at(e):
        pairs = ((1, near_1), (2, 4), (3, near_2), (4, 4 + near_1), (5, near_3), (6, 4 + near_2), (7, 4 + near_3))
        number = 0
        for at, value in pairs:
            number = jnp.where(e == at, value, number)
        return number

    for p in pieces:

        @pl.when(z < 3)
        def _():
            send_z(0, dp, True, p).start()

        @pl.when(z > 0)
        def _():
            send_z(1, dp, False, p).start()

        send_y(0, 0, p).start()
        send_core(0, 0, p).start()

    vec_ref[...] = jnp.zeros_like(vec_ref)
    loss_buf[...] = jnp.zeros_like(loss_buf)
    ids_col[...] = jnp.broadcast_to(ids_ref[...], (128, IMAGES * SEQ)).T
    lane = lax.broadcasted_iota(jnp.int32, (IMAGES * SEQ, 128), 1)
    dest = 1 - section

    def pick(place, first=False):
        rel = ids_col[...] - place * rows_here
        low = (rel == lane).astype(F32)
        high = ((rel - 128 == lane) & (lane < rows_here - 128)).astype(F32)
        one_hot = jnp.concatenate([low, high], axis=1)
        vec_ref[pl.ds(place, 1), D:] = column_sum(one_hot)
        one_hot = one_hot[:, :SHARD].astype(BF)
        for i in range(IMAGES):
            for p in pieces:
                rows = matmul_nn(one_hot[i * SEQ : (i + 1) * SEQ], shards[place, p]).astype(BF)
                cols = slice(p * SLICE, (p + 1) * SLICE)
                rows_buf[dest, i, :, cols] = rows if first else rows_buf[dest, i, :, cols] + rows

    def pick_core(e):
        for p in pieces:
            send_core(e, number_at(e), p).wait_recv()
        pick(place_of(number_at(e)) + 1 - 2 * core)

    def event(e, carry):
        number = number_at(e)
        near = (e == 1) | (e == 3) | (e == 5)
        for p in pieces:
            move(place_of(number), p, s_c.at[e], r_in.at[number], across).wait_recv()

            @pl.when(home & near & jnp.logical_not(corner))
            def _():
                pass_on(e, p).start()

            @pl.when(home & near)
            def _():
                send_y((e + 1) // 2, number, p).start()

            @pl.when(home & ((e >= 4) | ((e == 3) & corner)))
            def _():
                send_x(e - 3, number, p).start()

            send_core(e, number, p).start()
        pick(place_of(number))
        pick_core(e - 1)
        return carry

    pick(dp, True)
    lax.fori_loop(1, 8, event, 0)
    pick_core(7)

    for p in pieces:

        @pl.when(z < 3)
        def _():
            send_z(0, dp, True, p).wait_send()

        @pl.when(z > 0)
        def _():
            send_z(1, dp, False, p).wait_send()

        send_y(0, 0, p).wait_send()

        @pl.when(home)
        def _():
            for order in (1, 2, 3):
                send_y(order, number_at(2 * order - 1), p).wait_send()
            for e in (4, 5, 6, 7):
                send_x(e - 3, number_at(e), p).wait_send()

        @pl.when(home & jnp.logical_not(corner))
        def _():
            for e in (1, 3, 5):
                pass_on(e, p).wait_send()

        @pl.when(home & corner)
        def _():
            send_x(0, number_at(3), p).wait_send()

        for e in range(8):
            send_core(e, number_at(e), p).wait_send()
    for load in loads:
        load.wait()

    @pl.when(section == 0)
    def _():
        patch_load.wait()

    @pl.when(section == 1)
    def _():
        target_load.wait()

    weights = (gains, shifts, w_qkv, w_out, out_bias, w_up, up_bias, w_down, down_bias)
    scale = jnp.where(section == 0, COMMIT_WEIGHT, 1.0)

    def rows_of(ref, image):
        return ref.at[pl.ds(pl.multiple_of(image * SEQ, SEQ), SEQ)]

    def stores(image, forward):
        pairs = ((l_buf, l_ref), (result_buf, result_ref)) if forward else ((d_buf, d_ref), (dh_buf, dh_ref))
        first = 0 if forward else 2
        return [
            pltpu.make_async_copy(src, rows_of(dst, image), out_sem.at[first + i]) for i, (src, dst) in enumerate(pairs)
        ]

    def cross(image):
        return pltpu.make_async_remote_copy(
            crossing.at[image], crossing.at[image], sx.at[image], rx.at[image], device_id=beside, device_id_type=MESH
        )

    trade = pltpu.make_async_remote_copy(loss_buf, loss_side, s_loss, r_loss, device_id=beside, device_id_type=MESH)

    def step(i, carry):
        even = i % 2 == 0
        ahead = jnp.where(section == 1, even, (i == 0) | ((i % 2 == 1) & (i < 7)))

        @pl.when(ahead)
        def _():
            image = (i + 1) // 2
            slot = image % 2

            @pl.when(image > 0)
            def _():
                for copy in stores(image - 1, True):
                    copy.wait()

            forward_image(
                rows_buf.at[0, image], weights, l_buf, qkv.at[slot], pt.at[slot], slope.at[slot], h1.at[slot],
                result.at[slot], result_buf, vt, ot,
            )
            diff = result[slot] - rows_buf[1, image].astype(F32)
            loss_buf[0:1, :] += column_sum(diff * diff * scale)
            for copy in stores(image, True):
                copy.start()

            @pl.when(image == IMAGES - 1)
            def _():
                trade.start()

        @pl.when(jnp.logical_not(ahead))
        def _():
            image = (i - 1) // 2
            slot = image % 2

            @pl.when(image > 0)
            def _():
                for copy in stores(image - 1, False):
                    copy.wait()

            @pl.when(section == 0)
            def _():
                cross(image).wait_recv()

            backward_image(
                scale, section == 0, result.at[slot], rows_buf.at[1, image], crossing.at[image], rows_buf.at[0, image], weights,
                qkv.at[slot], pt.at[slot], slope.at[slot], h1.at[slot], d_buf, vec_ref, dh_buf, crossing.at[image],
                vt, ot,
            )

            @pl.when(section == 1)
            def _():
                cross(image).start()

            for copy in stores(image, False):
                copy.start()

        return carry

    lax.fori_loop(0, 2 * IMAGES, step, 0)
    for forward in (True, False):
        for copy in stores(IMAGES - 1, forward):
            copy.wait()

    @pl.when(section == 1)
    def _():
        for image in range(IMAGES):
            cross(image).wait_send()

    trade.wait()
    vec_ref[V_LOSS : V_LOSS + 1, :D] = loss_buf[0:1, :]
    vec_ref[V_SIDE : V_SIDE + 1, :D] = loss_side[0:1, :]


def run_blocks(patches, targets, ids, codebook, weights):
    dma = pltpu.SemaphoreType.DMA
    vm = pltpu.VMEM
    rows = IMAGES * SEQ
    inside, outside = pl.BlockSpec(memory_space=pltpu.VMEM), pl.BlockSpec(memory_space=pl.ANY)
    weight_places = [inside, inside, outside, outside, inside, outside, inside, outside, inside]
    return pl.pallas_call(
        blocks_kernel,
        out_shape=[
            jax.ShapeDtypeStruct((rows, D), BF),
            jax.ShapeDtypeStruct((rows, D), F32),
            jax.ShapeDtypeStruct((rows, L_ALL), BF),
            jax.ShapeDtypeStruct((rows, D_ALL), BF),
            jax.ShapeDtypeStruct((V_ROWS, V_COLS), F32),
        ],
        in_specs=[outside, outside, inside, inside] + weight_places,
        out_specs=[outside] * 4 + [inside],
        scratch_shapes=[
            vm((D, QKV), BF), vm((D, D), BF), vm((D, FF), BF), vm((FF, D), BF),
            vm((16, SLICES, SHARD, SLICE), BF), vm((rows, 128), jnp.int32),
            vm((2, IMAGES, SEQ, D), BF), vm((IMAGES, SEQ, D), BF), vm((8, D), F32), vm((8, D), F32),
            vm((2, SEQ, QKV), BF), vm((2, HEADS, SEQ, SEQ), F32), vm((2, SEQ, FF), F32), vm((2, SEQ, D), F32),
            vm((2, SEQ, D), F32), vm((SEQ, L_ALL), BF), vm((SEQ, D_ALL), BF), vm((SEQ, D), BF), vm((SEQ, D), F32),
            vm((D, SEQ), BF), vm((D, SEQ), BF),
            dma((4,)), dma(()), dma((4,)), dma((8, SLICES)), dma((5, SLICES)),
            dma((4, SLICES)), dma((5, SLICES)), dma((8, SLICES)), dma((8, SLICES)), dma(()), dma(()),
            dma((IMAGES,)), dma((IMAGES,)),
        ],
        compiler_params=pltpu.CompilerParams(collective_id=2, has_side_effects=True, vmem_limit_bytes=VMEM_BYTES),
        name="blocks",
    )(patches.reshape(IMAGES, SEQ, D), targets.reshape(IMAGES, SEQ, D), ids.reshape(1, rows), codebook, *weights)


UNITS = 36
PART = D // 16
COLS = 256
LAG_Y, LAG_Z, HOP = 1, 4, 4
LAG_OUT = LAG_Z + 3 * HOP
BLOCKS = D_ALL // COLS
FIRST_DOWN = 24
EVERY, EARLY = 9, UNITS // 9
LAG_LAST = 3
RING = 20


def reduce_kernel(
    vocab, l_ref, d_ref, vec_ref, qkv_out, out_out, up_out, down_out, vec_out, hist_out, stats_out,
    left, right, product, acc_y, acc_z, tx_c, rx_c, tx_y, rx_y, tx_up, rx_up, tx_dn, rx_dn,
    acc_e, tx_eu, rx_eu, tx_ed, rx_ed, tx_l, rx_l, vec_tx, vec_c, vec_y, vec_z,
    lsem, dsem, sc, rc, sy, ry, s_up, r_up, s_dn, r_dn,
    s_eu, r_eu, s_ed, r_ed, s_l, r_l, sv, rv,
):
    sec, dp = lax.axis_index("section"), lax.axis_index("dp")
    core, y, z = dp % 2, (dp // 2) % 2, dp // 4
    across = (sec, dp + 1 - 2 * core)
    along_y = (sec, dp + 2 - 4 * y)
    along_z = [(sec, (z + k) % 4 * 4 + y * 2 + core) for k in (1, 2, 3)]
    above, below = (sec, jnp.minimum(dp + 4, 12 + dp % 4)), (sec, jnp.maximum(dp - 4, dp % 4))

    lefts = [pltpu.make_async_copy(l_ref.at[:, i * D : (i + 1) * D], left.at[i], lsem.at[i]) for i in range(7)]

    def load_right(n):
        cols = pl.ds(pl.multiple_of(n * COLS, COLS), COLS)
        return pltpu.make_async_copy(d_ref.at[:, cols], right.at[n % 2], dsem.at[n % 2])

    lefts[0].start()
    load_right(0).start()

    barrier = pltpu.get_barrier_semaphore()
    for target in [across, along_y] + along_z:
        pl.semaphore_signal(barrier, inc=1, device_id=target, device_id_type=MESH)
    pl.semaphore_wait(barrier, 5)

    def remote(src, dst, send, recv, target):
        return pltpu.make_async_remote_copy(src, dst, send, recv, device_id=target, device_id_type=MESH)

    def send_core(u):
        return remote(tx_c.at[u % 2], rx_c.at[u], sc.at[u % 2], rc.at[u], across)

    def send_y(u):
        return remote(tx_y.at[u % RING], rx_y.at[u], sy.at[u % RING], ry.at[u], along_y)

    def up_link(at, high, tx, rx, send, recv):
        rows = slice(at * high, 3 * high)
        return remote(tx.at[rows], rx.at[rows], send, recv, above)

    def dn_link(at, high, tx, rx, send, recv):
        rows = slice(0, at * high)
        return remote(tx.at[rows], rx.at[rows], send, recv, below)

    def send_last(u):
        return remote(tx_l.at[u], rx_l.at[u], s_l.at[u], r_l.at[u], along_y)

    def is_early(u):
        return u % EVERY == 2

    def valid(u):
        return (u >= 0) & (u < UNITS)

    def climb(high, acc, tx, rx, send, recv):
        for at in range(4):

            @pl.when(z == at)
            def _():
                if at > 0:
                    up_link(at - 1, high, tx, rx, send, recv).wait_recv()
                if at < 3:
                    t = acc[(at + 1) * high : 4 * high]
                    if at > 0:
                        t = t + rx[at * high : 3 * high].astype(F32)
                    tx[at * high : 3 * high] = t.astype(BF)
                    up_link(at, high, tx, rx, send, recv).start()

    def sink(high, acc, tx, rx, send, recv):
        for at in range(4):

            @pl.when(z == at)
            def _():
                if at < 3:
                    dn_link(at + 1, high, tx, rx, send, recv).wait_recv()
                if at > 0:
                    t = acc[: at * high]
                    if at < 3:
                        t = t + rx[: at * high].astype(F32)
                    tx[: at * high] = t.astype(BF)
                    dn_link(at, high, tx, rx, send, recv).start()

    def settle(high, acc, up, dn):
        for at in range(4):

            @pl.when(z == at)
            def _():
                t = acc[at * high : (at + 1) * high]
                if at < 3:
                    up_link(at, high, *up).wait_send()
                    t = t + dn[1][at * high : (at + 1) * high].astype(F32)
                if at > 0:
                    dn_link(at, high, *dn).wait_send()
                    t = t + up[1][(at - 1) * high : at * high].astype(F32)
                acc[at * high : (at + 1) * high] = t

    def up_args(u):
        return tx_up.at[u % RING], rx_up.at[u], s_up.at[u % RING], r_up.at[u]

    def dn_args(u):
        return tx_dn.at[u % RING], rx_dn.at[u], s_dn.at[u % RING], r_dn.at[u]

    def early_up(e):
        return tx_eu.at[e], rx_eu.at[e], s_eu.at[e], r_eu.at[e]

    def early_dn(e):
        return tx_ed.at[e], rx_ed.at[e], s_ed.at[e], r_ed.at[e]

    vec_core = remote(vec_ref, vec_c, sv.at[0], rv.at[0], across)
    vec_along_y = remote(vec_tx, vec_y, sv.at[1], rv.at[1], along_y)
    vec_along_z = [remote(vec_z.at[z], vec_z.at[z], sv.at[2 + k], rv.at[2 + k], along_z[k]) for k in range(3)]
    vec_core.start()

    def multiply(u):
        down = u >= FIRST_DOWN
        n = jnp.where(down, FIRST_DOWN + (u - FIRST_DOWN) // 4, u)
        fresh = jnp.logical_not(down) | (u % 4 == 0)

        @pl.when(fresh & (n + 1 < BLOCKS))
        def _():
            load_right(n + 1).start()

        @pl.when(fresh)
        def _():
            load_right(n).wait()

        @pl.when(u == 1)
        def _():
            for load in lefts[1:]:
                load.start()

        for i, first in enumerate((0, 12, 15, FIRST_DOWN)):

            @pl.when(u == first)
            def _():
                for load in lefts[i : i + 1] if i < 3 else lefts[3:]:
                    load.wait()

        @pl.when(jnp.logical_not(down))
        def _():
            which = jnp.where(u < 12, 0, jnp.where(u < 15, 1, 2))
            product[:D] = matmul_tn(left[which], right[n % 2])

        @pl.when(down & fresh)
        def _():
            for i in range(4):
                product[i * D : (i + 1) * D] = matmul_tn(left[3 + i], right[n % 2])

        def rows_for(place):
            owner = place % 4 * 4 + (y + place // 4 % 2) % 2 * 2 + (core + place // 8) % 2
            row = jnp.where(down, owner * (4 * PART) + u % 4 * PART, owner * PART)
            return product[pl.ds(pl.multiple_of(row, PART), PART), :]

        for place in range(8):
            tx_c[u % 2, place * PART : (place + 1) * PART] = rows_for(8 + place).astype(BF)
        send_core(u).start()
        for place in range(8):
            acc_y[u % 2, place * PART : (place + 1) * PART] = rows_for(place)

    def step(i, carry):
        @pl.when(i < UNITS)
        def _():
            multiply(i)

        @pl.when((i >= LAG_Y) & (i < UNITS + LAG_Y))
        def _():
            u = i - LAG_Y
            send_core(u).wait()

            @pl.when(is_early(u))
            def _():
                t = acc_y[u % 2] + rx_c[u].astype(F32)
                for place in range(8):
                    to = (2 * (place % 4) + place // 4) * PART
                    acc_e[u // EVERY, to : to + PART] = t[place * PART : (place + 1) * PART]

            @pl.when(jnp.logical_not(is_early(u)))
            def _():
                tx_y[u % RING] = (acc_y[u % 2, 4 * PART :] + rx_c[u, 4 * PART :].astype(F32)).astype(BF)
                send_y(u).start()
                acc_z[u % RING] = acc_y[u % 2, : 4 * PART] + rx_c[u, : 4 * PART].astype(F32)

        @pl.when(valid(i - LAG_Z) & jnp.logical_not(is_early(i - LAG_Z)))
        def _():
            u = i - LAG_Z
            send_y(u).wait()
            acc_z[u % RING] = acc_z[u % RING] + rx_y[u].astype(F32)

        u_up = i - LAG_Z - z * HOP

        @pl.when(valid(u_up) & jnp.logical_not(is_early(u_up)))
        def _():
            climb(PART, acc_z.at[u_up % RING], *up_args(u_up))

        @pl.when(valid(u_up) & is_early(u_up))
        def _():
            climb(2 * PART, acc_e.at[u_up // EVERY], *early_up(u_up // EVERY))

        u_dn = i - LAG_Z - (3 - z) * HOP

        @pl.when(valid(u_dn) & jnp.logical_not(is_early(u_dn)))
        def _():
            sink(PART, acc_z.at[u_dn % RING], *dn_args(u_dn))

        @pl.when(valid(u_dn) & is_early(u_dn))
        def _():
            sink(2 * PART, acc_e.at[u_dn // EVERY], *early_dn(u_dn // EVERY))

        def put(u, t):
            def lanes(n):
                return pl.ds(pl.multiple_of(n * COLS, COLS), COLS)

            @pl.when(u < 12)
            def _():
                up_out[:, lanes(u)] = t

            @pl.when((u >= 12) & (u < 15))
            def _():
                out_out[:, lanes(u - 12)] = t

            @pl.when((u >= 15) & (u < FIRST_DOWN))
            def _():
                qkv_out[:, lanes(u - 15)] = t

            @pl.when(u >= FIRST_DOWN)
            def _():
                rows = pl.ds(pl.multiple_of(u % 4 * PART, PART), PART)
                down_out[rows, lanes((u - FIRST_DOWN) // 4)] = t

        @pl.when(valid(i - LAG_OUT) & is_early(i - LAG_OUT))
        def _():
            e = (i - LAG_OUT) // EVERY
            settle(2 * PART, acc_e.at[e], early_up(e), early_dn(e))
            rows = pl.ds(pl.multiple_of((2 * z + 1) * PART, PART), PART)
            tx_l[e] = acc_e[e, rows, :].astype(BF)
            send_last(e).start()

        @pl.when(valid(i - LAG_OUT - LAG_LAST) & is_early(i - LAG_OUT - LAG_LAST))
        def _():
            u = i - LAG_OUT - LAG_LAST
            e = u // EVERY
            send_last(e).wait()
            rows = pl.ds(pl.multiple_of(2 * z * PART, PART), PART)
            put(u, acc_e[e, rows, :] + rx_l[e].astype(F32))

        @pl.when(valid(i - LAG_OUT) & jnp.logical_not(is_early(i - LAG_OUT)))
        def _():
            u = i - LAG_OUT
            settle(PART, acc_z.at[u % RING], up_args(u), dn_args(u))
            put(u, acc_z[u % RING, pl.ds(pl.multiple_of(z * PART, PART), PART), :])

        @pl.when(i == 3)
        def _():
            vec_core.wait()
            vec_tx[...] = vec_ref[...] + vec_c[...]
            vec_along_y.start()

        @pl.when(i == 8)
        def _():
            vec_along_y.wait()
            vec_z[z] = vec_tx[...] + vec_y[...]
            for copy in vec_along_z:
                copy.start()

        @pl.when(i == 14)
        def _():
            for copy in vec_along_z:
                copy.wait()
            vec_out[...] = (vec_z[0] + vec_z[1]) + (vec_z[2] + vec_z[3])

        return carry

    lax.fori_loop(0, UNITS + LAG_OUT, step, 0)

    def total(value):
        return jnp.sum(jnp.sum(value, axis=1, keepdims=True), axis=0, keepdims=True)

    tokens = 16 * l_ref.shape[0]
    counts = vec_out[:, D:]
    shares = counts * (1.0 / tokens)
    entropy = -total(shares * jnp.log(jnp.where(counts > 0, shares, 1.0)))
    used = total((counts > 0).astype(F32))
    loss = total(vec_out[V_LOSS : V_LOSS + 1, :D]) + total(vec_out[V_SIDE : V_SIDE + 1, :D])
    lane = lax.broadcasted_iota(jnp.int32, (8, 128), 1)
    last = jnp.where(lane == 1, used / vocab, jnp.exp(entropy) / vocab)
    stats_out[...] = jnp.where(lane == 0, loss / (tokens * D), last)
    hist_out[...] = vec_out[pl.ds(dp, 1), D:].astype(jnp.int32)


def reduce_weights(l, d, vec, vocab):
    dma = pltpu.SemaphoreType.DMA
    vm = pltpu.VMEM
    rows = l.shape[0]
    sums = (V_ROWS, V_COLS)
    return pl.pallas_call(
        functools.partial(reduce_kernel, vocab),
        out_shape=[
            jax.ShapeDtypeStruct((PART, QKV), F32),
            jax.ShapeDtypeStruct((PART, D), F32),
            jax.ShapeDtypeStruct((PART, FF), F32),
            jax.ShapeDtypeStruct((4 * PART, D), F32),
            jax.ShapeDtypeStruct(sums, F32),
            jax.ShapeDtypeStruct((1, V_COLS - D), jnp.int32),
            jax.ShapeDtypeStruct((8, 128), F32),
        ],
        in_specs=[pl.BlockSpec(memory_space=pl.ANY)] * 2 + [pl.BlockSpec(memory_space=pltpu.VMEM)],
        out_specs=[pl.BlockSpec(memory_space=pltpu.VMEM)] * 7,
        scratch_shapes=[
            vm((7, rows, D), BF), vm((2, rows, COLS), BF), vm((4 * D, COLS), F32),
            vm((2, 8 * PART, COLS), F32), vm((RING, 4 * PART, COLS), F32),
            vm((2, 8 * PART, COLS), BF), vm((UNITS, 8 * PART, COLS), BF),
            vm((RING, 4 * PART, COLS), BF), vm((UNITS, 4 * PART, COLS), BF),
            vm((RING, 3 * PART, COLS), BF), vm((UNITS, 3 * PART, COLS), BF),
            vm((RING, 3 * PART, COLS), BF), vm((UNITS, 3 * PART, COLS), BF),
            vm((EARLY, 8 * PART, COLS), F32), vm((EARLY, 6 * PART, COLS), BF), vm((EARLY, 6 * PART, COLS), BF),
            vm((EARLY, 6 * PART, COLS), BF), vm((EARLY, 6 * PART, COLS), BF),
            vm((EARLY, PART, COLS), BF), vm((EARLY, PART, COLS), BF),
            vm(sums, F32), vm(sums, F32), vm(sums, F32), vm((4,) + sums, F32),
            dma((7,)), dma((2,)), dma((2,)), dma((UNITS,)), dma((RING,)), dma((UNITS,)),
            dma((RING,)), dma((UNITS,)), dma((RING,)), dma((UNITS,)),
            dma((EARLY,)), dma((EARLY,)), dma((EARLY,)), dma((EARLY,)), dma((EARLY,)), dma((EARLY,)),
            dma((5,)), dma((5,)),
        ],
        compiler_params=pltpu.CompilerParams(collective_id=1, has_side_effects=True, vmem_limit_bytes=VMEM_BYTES),
        name="weight_grad_reduce",
    )(l, d, vec)


def finish(result, dh, g_qkv, g_out, g_up, g_down, vec, hist, stats, shard):
    rows = result.shape[0]
    pieces = 1

    def body(result_ref, dh_ref, qkv_ref, out_ref, up_ref, down_ref, vec_ref, hist_ref, stats_ref,
             result_to, dh_to, gains_to, shifts_to, qkv_to, out_to, out_bias_to, up_to, up_bias_to, down_to, down_bias_to, hist_to, stats_to, *scratch):
        *bufs, into, outof = scratch
        copies = []
        for src, dst in ((dh_ref, dh_to), (result_ref, result_to)):
            for i in range(pieces):
                part = pl.ds(i * rows // pieces, rows // pieces)
                copies.append((src.at[part], dst.at[0, part]))
        copies += [(qkv_ref, qkv_to.at[0]), (out_ref, out_to.at[0]), (up_ref, up_to.at[0]), (down_ref, down_to.at[0])]
        loads, saves = [], []
        for i, (src, dst) in enumerate(copies):
            buf = bufs[i // pieces].at[i % pieces] if i < 2 * pieces else bufs[i - 2 * pieces + 2]
            loads.append(pltpu.make_async_copy(src, buf, into.at[i]))
            saves.append(pltpu.make_async_copy(buf, dst, outof.at[i]))
        for load in loads:
            load.start()
        for load, save in zip(loads, saves):
            load.wait()
            save.start()
        gains_to[0] = vec_ref[0:2, :D]
        shifts_to[0] = vec_ref[2:4, :D]
        out_bias_to[...] = vec_ref[4:5, :D]
        for j in range(FF // D):
            up_bias_to[:, j * D : (j + 1) * D] = vec_ref[5 + j : 6 + j, :D]
        down_bias_to[...] = vec_ref[9:10, :D]
        hist_to[...] = hist_ref[0, :shard]
        stats_to[...] = stats_ref[0, :3]
        for save in saves:
            save.wait()

    inside, outside = pl.BlockSpec(memory_space=pltpu.VMEM), pl.BlockSpec(memory_space=pl.ANY)

    def shape(*dims, dtype=F32):
        return jax.ShapeDtypeStruct((1,) + dims, dtype)

    out = pl.pallas_call(
        body,
        out_shape=[
            shape(rows, D, dtype=BF), shape(rows, D), shape(2, D), shape(2, D), shape(PART, QKV), shape(PART, D),
            shape(D), shape(PART, FF), shape(FF), shape(4 * PART, D), shape(D),
            jax.ShapeDtypeStruct((shard,), jnp.int32), jax.ShapeDtypeStruct((3,), F32),
        ],
        in_specs=[outside] * 6 + [inside] * 3,
        out_specs=[outside, outside, inside, inside, outside, outside, inside, outside, inside, outside, inside, inside, inside],
        scratch_shapes=[
            pltpu.VMEM((pieces, rows // pieces, D), F32), pltpu.VMEM((pieces, rows // pieces, D), BF),
            pltpu.VMEM((PART, QKV), F32), pltpu.VMEM((PART, D), F32), pltpu.VMEM((PART, FF), F32),
            pltpu.VMEM((4 * PART, D), F32),
            pltpu.SemaphoreType.DMA((2 * pieces + 4,)), pltpu.SemaphoreType.DMA((2 * pieces + 4,)),
        ],
        compiler_params=pltpu.CompilerParams(vmem_limit_bytes=VMEM_BYTES),
        name="place_outputs",
    )(result, dh, g_qkv, g_out, g_up, g_down, vec, hist, stats)
    return tuple(out)


def count_shares(counts, total_count):
    shares = counts / total_count
    nonzero_share = jnp.where(counts > 0, shares, 1.0)
    return -jnp.sum(shares * jnp.log(nonzero_share)), jnp.sum((counts > 0).astype(F32))


def on_device(
    patches, targets, code_ids, codebook, norm_gains, norm_shifts, w_qkv, w_out, out_bias, w_up, up_bias, w_down, down_bias
):
    section = lax.axis_index("section")
    leading = section == 0
    dp_size = lax.axis_size("dp")
    dp = lax.axis_index("dp")
    weights = (
        norm_gains[0], norm_shifts[0], w_qkv[0], w_out[0], out_bias, w_up[0], up_bias, w_down[0], down_bias
    )
    rows, width = patches.shape
    images = rows // SEQ
    vocab_local = codebook.shape[0]
    vocab_all = vocab_local * dp_size
    total_tokens = rows * dp_size

    small = dp_size == 16 and vocab_local <= SHARD and rows == IMAGES * SEQ
    if small:
        result_bf, dh, l, d, vec = run_blocks(patches, targets, code_ids, codebook, weights)
        g_qkv, g_out, g_up, g_down, vec, hist, stats = reduce_weights(l, d, vec, vocab_all)
        return finish(result_bf, dh, g_qkv, g_out, g_up, g_down, vec, hist, stats, vocab_local)
    else:
        shard_rows = lax.all_gather(codebook, "dp", axis=0, tiled=True)
        chosen = jnp.take(shard_rows, jnp.clip(code_ids, 0, vocab_all - 1), axis=0)
        x = jnp.where(leading, patches, chosen)
        l, qkv, pt, slope, h1, result, result_bf = block_forward(x, weights)
        other = jnp.where(leading, chosen, targets)
        d = dh = None
        vec = jnp.zeros((V_ROWS, V_COLS), F32)
        arrived = jnp.zeros((SEQ, D), BF)
        for moment in range(images + 1):
            which = jnp.clip(moment - 1 + section, 0, images - 1).astype(jnp.int32)[None]
            active = jnp.where(leading, moment >= 1, moment < images).astype(F32)
            flags = jnp.stack(
                [jnp.where(leading, COMMIT_WEIGHT, 1.0).astype(F32), active, jnp.where(leading, 1.0, 0.0).astype(F32)]
            )
            d, dh, vec, outgoing = block_backward(
                which, flags, result, other, arrived, x, weights, qkv, pt, slope, h1, vec, d, dh
            )
            if moment < images:
                arrived = lax.ppermute(outgoing, "section", [(1, 0)])
        pairs = (
            (l[:, L_A:L_M], d[:, D_QKV:D_GB]),
            (l[:, L_O:L_A], d[:, D_GH:D_QKV]),
            (l[:, :L_O], d[:, :D_GH]),
            (l[:, L_M:], d[:, D_GB:]),
        )
        g_qkv, g_out, g_up, g_down = (
            lax.psum_scatter(matmul_tn(left, right), "dp", scatter_dimension=0, tiled=True) for left, right in pairs
        )
        vocab_iota = lax.broadcasted_iota(jnp.int32, (1, vocab_all), 1)
        counts = jnp.sum((code_ids[:, None] == vocab_iota).astype(F32), axis=0)
        hist_local = lax.psum_scatter(counts, "dp", scatter_dimension=0, tiled=True)
        entropy_part, used_part = count_shares(hist_local, total_tokens)
        hist_local = hist_local.astype(jnp.int32)
        vec = lax.psum(vec, "dp")
        entropy_all, used_all = lax.psum((entropy_part, used_part), "dp")
        loss_all = lax.psum(jnp.sum(vec[V_LOSS, :D]), "section")
        stats = jnp.stack(
            [loss_all / (total_tokens * width), used_all / vocab_all, jnp.exp(entropy_all) / vocab_all]
        )
    return (
        result_bf[None],
        dh[None],
        vec[None, 0:2, :D],
        vec[None, 2:4, :D],
        g_qkv[None],
        g_out[None],
        vec[None, 4, :D],
        g_up[None],
        vec[5:9, :D].reshape(1, FF),
        g_down[None],
        vec[None, 9, :D],
        hist_local,
        stats,
    )


def solution(mesh):
    return jax.shard_map(
        on_device,
        mesh=mesh,
        in_specs=(
            P("dp", None),
            P("dp", None),
            P("dp"),
            P("dp", None),
            P("section", None, None),
            P("section", None, None),
            P("section", None, None),
            P("section", None, None),
            P("section", None),
            P("section", None, None),
            P("section", None),
            P("section", None, None),
            P("section", None),
        ),
        out_specs=(
            P("section", "dp", None),
            P("section", "dp", None),
            P("section", None, None),
            P("section", None, None),
            P("section", "dp", None),
            P("section", "dp", None),
            P("section", None),
            P("section", "dp", None),
            P("section", None),
            P("section", "dp", None),
            P("section", None),
            P("dp"),
            P(),
        ),
        check_vma=False,
    )
```

```python
import functools

import jax
import jax.numpy as jnp
from jax import lax
from jax.experimental import pallas as pl
from jax.experimental.pallas import tpu as pltpu
from jax.sharding import PartitionSpec as P

SEQ = 256
D = 768
HD = 64
HEADS = 12
FF = 3072
FF_PIECE = 768
QKV = 3 * D
L_O, L_A, L_M, L_ALL = D, 2 * D, 3 * D, 3 * D + FF
D_GH, D_QKV, D_GB, D_ALL = FF, FF + D, FF + D + QKV, FF + D + QKV + D
V_SIDE, V_LOSS, V_ROWS, V_COLS = 14, 15, 16, D + 256

COMMIT_WEIGHT = 0.25
EPSILON = 1e-06
SQRT_HALF = 0.5**0.5
INV_ROOT_TAU = 0.3989422804014327
LOG2_E = 1.4426950408889634
HEAD_SCALE = HD**-0.5
MESH = pl.DeviceIdType.MESH
BF, F32 = jnp.bfloat16, jnp.float32
VMEM_BYTES, REDUCE_BYTES, PLACE_BYTES = 60 << 20, 48 << 20, 14 << 20


def matmul_nn(left, right):
    return jnp.dot(left, right, preferred_element_type=F32)


def matmul_nt(left, right):
    return lax.dot_general(left, right, (((1,), (1,)), ((), ())), preferred_element_type=F32)


def matmul_tn(left, right):
    return lax.dot_general(left, right, (((0,), (0,)), ((), ())), preferred_element_type=F32)


def layer_norm(rows_in):
    centered = rows_in - jnp.mean(rows_in, axis=-1, keepdims=True)
    inv_std = lax.rsqrt(jnp.mean(centered * centered, axis=-1, keepdims=True) + EPSILON)
    return centered * inv_std, inv_std


def norm_back(incoming, scaled, inv_std, gain_row):
    x = incoming * gain_row
    return inv_std * (
        x
        - jnp.mean(x, axis=-1, keepdims=True)
        - scaled * jnp.mean(x * scaled, axis=-1, keepdims=True)
    )


def column_sum(x):
    return jnp.sum(x, axis=0, keepdims=True)


def head_masks():
    low = lax.broadcasted_iota(jnp.int32, (1, 2 * HD), 1) < HD
    ones = low.astype(F32)
    return ones.astype(BF), (1.0 - ones).astype(BF)


def head_pair(ref, base, head):
    return ref[:, base + head // 2 * 128 : base + (head // 2 + 1) * 128]


def forward_image(x_ref, weights, l_ref, qkv_ref, pt_ref, slope_ref, h1_ref, out_ref, outb_ref, vt_ref, ot_ref):
    gains, shifts, w_qkv, w_out, out_bias, w_up, up_bias, w_down, down_bias = weights
    h = x_ref[...].astype(F32)
    s1, _ = layer_norm(h)
    a = (s1 * gains[0:1, :] + shifts[0:1, :]).astype(BF)
    l_ref[:, L_A:L_M] = a
    for j in range(3):
        qkv_ref[:, j * D : (j + 1) * D] = matmul_nn(a, w_qkv[:, j * D : (j + 1) * D]).astype(BF)
    vt_ref[...] = qkv_ref[:, 2 * D : 3 * D].T
    masks = head_masks()
    scores = [
        matmul_nt(head_pair(qkv_ref, D, head) * masks[head % 2], head_pair(qkv_ref, 0, head)) for head in range(HEADS)
    ]
    for head in range(HEADS):
        st = scores[head]
        e = jnp.exp2((st - jnp.max(st, axis=0, keepdims=True)) * (HEAD_SCALE * LOG2_E))
        pt_ref[head] = e * (1.0 / column_sum(e))
    for head in range(HEADS):
        span = slice(head * HD, (head + 1) * HD)
        ot_ref[span, :] = matmul_nn(vt_ref[span, :], pt_ref[head].astype(BF)).astype(BF)
    o = ot_ref[...].T
    l_ref[:, L_O:L_A] = o
    h1 = h + matmul_nn(o, w_out[...]) + out_bias[...]
    h1_ref[...] = h1
    s2, _ = layer_norm(h1)
    b = (s2 * gains[1:2, :] + shifts[1:2, :]).astype(BF)
    l_ref[:, 0:L_O] = b
    result = h1 + down_bias[...]
    for j in range(FF // FF_PIECE):
        span = slice(j * FF_PIECE, (j + 1) * FF_PIECE)
        u = matmul_nn(b, w_up[:, span]) + up_bias[:, span]
        half_curve = 0.5 + 0.5 * lax.erf(u * SQRT_HALF)
        m = (u * half_curve).astype(BF)
        l_ref[:, L_M + j * FF_PIECE : L_M + (j + 1) * FF_PIECE] = m
        slope = half_curve + u * jnp.exp(-0.5 * u * u) * INV_ROOT_TAU
        slope_ref[:, span] = slope
        result = result + matmul_nn(m, w_down[span, :])
    out_ref[...] = result
    outb_ref[...] = result.astype(BF)


def backward_image(
    scale, receives, out_ref, other_ref, arrived_ref, x_ref, weights, qkv_ref, pt_ref, slope_ref, h1_ref,
    d_ref, vec_ref, dh_ref, dhb_ref, kt_ref, qt_ref,
):
    gains, shifts, w_qkv, w_out, out_bias, w_up, up_bias, w_down, down_bias = weights
    diff = out_ref[...] - other_ref[...].astype(F32)

    def add(row, value):
        vec_ref[row : row + 1, :D] += column_sum(value)

    g = diff * scale + jnp.where(receives, arrived_ref[...].astype(F32), 0.0)
    gb = g.astype(BF)
    d_ref[:, D_GB:D_ALL] = gb
    add(9, g)
    db = jnp.zeros((SEQ, D), F32)
    for j in range(FF // FF_PIECE):
        span = slice(j * FF_PIECE, (j + 1) * FF_PIECE)
        du = (matmul_nt(gb, w_down[span, :]) * slope_ref[:, span]).astype(BF)
        d_ref[:, span] = du
        add(5 + j, du.astype(F32))
        db = db + matmul_nt(du, w_up[:, span])
    s2, inv2 = layer_norm(h1_ref[...])
    add(1, db * s2)
    add(3, db)
    dh1 = g + norm_back(db, s2, inv2, gains[1:2, :])
    add(4, dh1)
    gh = dh1.astype(BF)
    d_ref[:, D_GH:D_QKV] = gh
    do = matmul_nt(gh, w_out[...]).astype(BF)
    kt_ref[...] = qkv_ref[:, D : 2 * D].T
    masks = head_masks()

    def do_pair(head):
        return do[:, head // 2 * 128 : (head // 2 + 1) * 128]

    dpts = [matmul_nt(head_pair(qkv_ref, 2 * D, head) * masks[head % 2], do_pair(head)) for head in range(HEADS)]

    def both(parts, pair, make):
        return matmul_nn(
            jnp.concatenate(parts[2 * pair : 2 * pair + 2], axis=1),
            jnp.concatenate([make(2 * pair) * masks[0], make(2 * pair) * masks[1]], axis=0),
        )

    base = D_QKV + D
    for pair in range(HEADS // 2):
        dv = both([pt_ref[head].astype(BF) for head in range(HEADS)], pair, do_pair)
        d_ref[:, base + D + pair * 128 : base + D + (pair + 1) * 128] = dv.astype(BF)
    dsts = []
    for head in range(HEADS):
        ptf = pt_ref[head]
        dsts.append((ptf * (dpts[head] - column_sum(dpts[head] * ptf))).astype(BF))
    for pair in range(HEADS // 2):
        dk = both(dsts, pair, lambda head: head_pair(qkv_ref, 0, head))
        d_ref[:, base + pair * 128 : base + (pair + 1) * 128] = (dk * HEAD_SCALE).astype(BF)
    for head in range(HEADS):
        span = slice(head * HD, (head + 1) * HD)
        qt_ref[span, :] = (matmul_nn(kt_ref[span, :], dsts[head]) * HEAD_SCALE).astype(BF)
    d_ref[:, D_QKV : D_QKV + D] = qt_ref[...].T
    da = matmul_nt(d_ref[:, D_QKV:D_GB], w_qkv[...])
    s1, inv1 = layer_norm(x_ref[...].astype(F32))
    add(0, da * s1)
    add(2, da)
    dh = dh1 + norm_back(da, s1, inv1, gains[0:1, :])
    dh_ref[...] = dh
    dhb_ref[...] = dh.astype(BF)


WEIGHT_SHAPES = ((2, D), (2, D), (D, QKV), (D, D), (1, D), (D, FF), (1, FF), (FF, D), (1, D))


def weight_specs():
    def whole(shape):
        return pl.BlockSpec(shape, lambda *_: (0, 0), pipeline_mode=pl.Buffered(1))

    return [whole(shape) for shape in WEIGHT_SHAPES]


def block_forward(x, weights):
    rows = x.shape[0]
    images = rows // SEQ

    def row_block(width):
        return pl.BlockSpec((SEQ, width), lambda i: (i, 0))

    def body(x_ref, *refs):
        forward_image(x_ref, refs[:9], *refs[9:])

    def shape(width, dtype):
        return jax.ShapeDtypeStruct((rows, width), dtype)

    return pl.pallas_call(
        body,
        grid=(images,),
        in_specs=[row_block(D)] + weight_specs(),
        out_specs=[
            row_block(L_ALL),
            row_block(QKV),
            pl.BlockSpec((HEADS, SEQ, SEQ), lambda i: (i, 0, 0)),
            row_block(FF),
            row_block(D),
            row_block(D),
            row_block(D),
        ],
        out_shape=[
            shape(L_ALL, BF),
            shape(QKV, BF),
            jax.ShapeDtypeStruct((images * HEADS, SEQ, SEQ), F32),
            shape(FF, F32),
            shape(D, F32),
            shape(D, F32),
            shape(D, BF),
        ],
        scratch_shapes=[pltpu.VMEM((D, SEQ), BF), pltpu.VMEM((D, SEQ), BF)],
        compiler_params=pltpu.CompilerParams(vmem_limit_bytes=VMEM_BYTES),
        name="block_forward",
    )(x, *weights)


def block_backward(which, flags, result, other, arrived, x, weights, qkv, pt, slope, h1, vec, d, dh):
    rows = x.shape[0]

    def row_block(width):
        return pl.BlockSpec((SEQ, width), lambda i, which_ref: (which_ref[0], 0))

    def whole(height, width):
        return pl.BlockSpec((height, width), lambda i, which_ref: (0, 0))

    def body(which_ref, flags_ref, out_ref, other_ref, arrived_ref, x_ref, *refs):
        weight_refs = refs[:9]
        qkv_ref, pt_ref, slope_ref, h1_ref, vec_in = refs[9:14]
        d_ref, dh_ref, vec_out, dhb_ref, kt_ref, qt_ref = refs[-6:]
        vec_out[...] = jnp.zeros_like(vec_out)
        backward_image(
            flags_ref[0], flags_ref[2] > 0, out_ref, other_ref, arrived_ref, x_ref, weight_refs, qkv_ref, pt_ref,
            slope_ref, h1_ref, d_ref, vec_out, dh_ref, dhb_ref, kt_ref, qt_ref,
        )
        diff = out_ref[...] - other_ref[...].astype(F32)
        vec_out[V_LOSS : V_LOSS + 1, :D] = column_sum(diff * diff * flags_ref[0])
        vec_out[...] = vec_in[...] + vec_out[...] * flags_ref[1]

    keep = [] if d is None else [d, dh]
    first_kept = 2 + 4 + 9 + 5
    return pl.pallas_call(
        body,
        grid_spec=pltpu.PrefetchScalarGridSpec(
            num_scalar_prefetch=1,
            grid=(1,),
            in_specs=[pl.BlockSpec(memory_space=pltpu.SMEM), row_block(D), row_block(D), whole(SEQ, D), row_block(D)]
            + weight_specs()
            + [
                row_block(QKV),
                pl.BlockSpec((HEADS, SEQ, SEQ), lambda i, which_ref: (which_ref[0], 0, 0)),
                row_block(FF),
                row_block(D),
                whole(V_ROWS, V_COLS),
            ]
            + [pl.BlockSpec(memory_space=pl.ANY)] * len(keep),
            out_specs=[row_block(D_ALL), row_block(D), whole(V_ROWS, V_COLS), whole(SEQ, D)],
            scratch_shapes=[pltpu.VMEM((D, SEQ), BF), pltpu.VMEM((D, SEQ), BF)],
        ),
        out_shape=[
            jax.ShapeDtypeStruct((rows, D_ALL), BF),
            jax.ShapeDtypeStruct((rows, D), F32),
            jax.ShapeDtypeStruct((V_ROWS, V_COLS), F32),
            jax.ShapeDtypeStruct((SEQ, D), BF),
        ],
        input_output_aliases={first_kept: 0, first_kept + 1: 1} if keep else {},
        compiler_params=pltpu.CompilerParams(vmem_limit_bytes=VMEM_BYTES),
        name="block_backward",
    )(which, flags, result, other, arrived, x, *weights, qkv, pt, slope, h1, vec, *keep)


IMAGES = 4
SHARD = 208
SLICES = 3
SLICE = D // SLICES


def blocks_kernel(
    patches_ref, targets_ref, ids_ref, codebook_ref, gains, shifts, w_qkv_ref, w_out_ref, out_bias, w_up_ref, up_bias,
    w_down_ref, down_bias, result_ref, dh_ref, l_ref, d_ref, vec_ref,
    w_qkv, w_out, w_up, w_down, shards, ids_col, rows_buf, crossing, loss_buf, loss_side,
    qkv, pt, slope, h1, result, l_buf, d_buf, result_buf, dh_buf, vt, ot,
    w_sem, in_sem, out_sem, r_in, s_z, s_y, s_x, s_c, r_c, s_loss, r_loss, sx, rx,
):
    section, dp = lax.axis_index("section"), lax.axis_index("dp")
    core, y, z = dp % 2, (dp // 2) % 2, dp // 4
    across = (section, dp + 1 - 2 * core)
    along_y = (section, dp + 2 - 4 * y)
    along_z = [(section, (z + k) % 4 * 4 + y * 2 + core) for k in (1, 2, 3)]
    beside = (1 - section, dp)

    big = ((w_qkv_ref, w_qkv), (w_out_ref, w_out), (w_up_ref, w_up), (w_down_ref, w_down))
    loads = [pltpu.make_async_copy(src, dst, w_sem.at[i]) for i, (src, dst) in enumerate(big)]
    for load in loads:
        load.start()
    patch_load = pltpu.make_async_copy(patches_ref, rows_buf.at[0], in_sem)
    target_load = pltpu.make_async_copy(targets_ref, rows_buf.at[1], in_sem)

    @pl.when(section == 0)
    def _():
        patch_load.start()

    @pl.when(section == 1)
    def _():
        target_load.start()

    rows_here = codebook_ref.shape[0]
    for p in range(SLICES):
        shards[dp, p] = jnp.zeros((SHARD, SLICE), BF)
        shards[dp, p, :rows_here] = codebook_ref[:, p * SLICE : (p + 1) * SLICE]

    barrier = pltpu.get_barrier_semaphore()
    for target in [across, along_y, beside] + along_z:
        pl.semaphore_signal(barrier, inc=1, device_id=target, device_id_type=MESH)
    pl.semaphore_wait(barrier, 6)

    home = section == core
    corner = (z == 0) | (z == 3)
    near_1 = jnp.where(z == 0, 3, 1)
    near_2 = jnp.where(corner, 2, 3)
    near_3 = jnp.where(z == 0, 1, jnp.where(z == 3, 3, 2))
    def place_of(number):
        return (z - number % 4 + 4) % 4 * 4 + (y + number // 4) % 2 * 2 + core

    def move(place, p, send, recv, target):
        part = shards.at[place, p]
        return pltpu.make_async_remote_copy(part, part, send.at[p], recv.at[p], device_id=target, device_id_type=MESH)

    def send_z(order, place, up, p):
        towards = jnp.where(up, z + 1, z - 1)
        number = (towards - place // 4 + 4) % 4
        return move(place, p, s_z.at[order], r_in.at[number], (section, towards * 4 + y * 2 + core))

    def pass_on(e, p):
        up = (e == 1) | ((e == 5) & (z == 2))
        return send_z((e + 3) // 2, place_of(number_at(e)), up, p)

    def send_y(order, number, p):
        return move(place_of(number), p, s_y.at[order], r_in.at[4 + number], along_y)

    def send_x(order, number, p):
        return move(place_of(number), p, s_x.at[order], r_in.at[number], beside)

    def send_core(order, number, p):
        return move(place_of(number), p, s_c.at[order], r_c.at[order], across)

    pieces = range(SLICES)

    def number_at(e):
        pairs = ((1, near_1), (2, 4), (3, near_2), (4, 4 + near_1), (5, near_3), (6, 4 + near_2), (7, 4 + near_3))
        number = 0
        for at, value in pairs:
            number = jnp.where(e == at, value, number)
        return number

    for p in pieces:

        @pl.when(z < 3)
        def _():
            send_z(0, dp, True, p).start()

        @pl.when(z > 0)
        def _():
            send_z(1, dp, False, p).start()

        send_y(0, 0, p).start()
        send_core(0, 0, p).start()

    vec_ref[...] = jnp.zeros_like(vec_ref)
    loss_buf[...] = jnp.zeros_like(loss_buf)
    ids_col[...] = jnp.broadcast_to(ids_ref[...], (128, IMAGES * SEQ)).T
    lane = lax.broadcasted_iota(jnp.int32, (IMAGES * SEQ, 128), 1)
    dest = 1 - section

    def pick(place, first=False):
        rel = ids_col[...] - place * rows_here
        low = (rel == lane).astype(F32)
        high = ((rel - 128 == lane) & (lane < rows_here - 128)).astype(F32)
        one_hot = jnp.concatenate([low, high], axis=1)
        vec_ref[pl.ds(place, 1), D:] = column_sum(one_hot)
        one_hot = one_hot[:, :SHARD].astype(BF)
        for i in range(IMAGES):
            for p in pieces:
                rows = matmul_nn(one_hot[i * SEQ : (i + 1) * SEQ], shards[place, p]).astype(BF)
                cols = slice(p * SLICE, (p + 1) * SLICE)
                rows_buf[dest, i, :, cols] = rows if first else rows_buf[dest, i, :, cols] + rows

    def pick_core(e):
        for p in pieces:
            send_core(e, number_at(e), p).wait_recv()
        pick(place_of(number_at(e)) + 1 - 2 * core)

    def event(e, carry):
        number = number_at(e)
        near = (e == 1) | (e == 3) | (e == 5)
        for p in pieces:
            move(place_of(number), p, s_c.at[e], r_in.at[number], across).wait_recv()

            @pl.when(home & near & jnp.logical_not(corner))
            def _():
                pass_on(e, p).start()

            @pl.when(home & near)
            def _():
                send_y((e + 1) // 2, number, p).start()

            @pl.when(home & ((e >= 4) | ((e == 3) & corner)))
            def _():
                send_x(e - 3, number, p).start()

            send_core(e, number, p).start()
        pick(place_of(number))
        pick_core(e - 1)
        return carry

    pick(dp, True)
    lax.fori_loop(1, 8, event, 0)
    pick_core(7)

    for p in pieces:

        @pl.when(z < 3)
        def _():
            send_z(0, dp, True, p).wait_send()

        @pl.when(z > 0)
        def _():
            send_z(1, dp, False, p).wait_send()

        send_y(0, 0, p).wait_send()

        @pl.when(home)
        def _():
            for order in (1, 2, 3):
                send_y(order, number_at(2 * order - 1), p).wait_send()
            for e in (4, 5, 6, 7):
                send_x(e - 3, number_at(e), p).wait_send()

        @pl.when(home & jnp.logical_not(corner))
        def _():
            for e in (1, 3, 5):
                pass_on(e, p).wait_send()

        @pl.when(home & corner)
        def _():
            send_x(0, number_at(3), p).wait_send()

        for e in range(8):
            send_core(e, number_at(e), p).wait_send()
    for load in loads:
        load.wait()

    @pl.when(section == 0)
    def _():
        patch_load.wait()

    @pl.when(section == 1)
    def _():
        target_load.wait()

    weights = (gains, shifts, w_qkv, w_out, out_bias, w_up, up_bias, w_down, down_bias)
    scale = jnp.where(section == 0, COMMIT_WEIGHT, 1.0)

    def rows_of(ref, image):
        return ref.at[pl.ds(pl.multiple_of(image * SEQ, SEQ), SEQ)]

    def stores(image, forward):
        pairs = ((l_buf, l_ref), (result_buf, result_ref)) if forward else ((d_buf, d_ref), (dh_buf, dh_ref))
        first = 0 if forward else 2
        return [
            pltpu.make_async_copy(src, rows_of(dst, image), out_sem.at[first + i]) for i, (src, dst) in enumerate(pairs)
        ]

    def cross(image):
        return pltpu.make_async_remote_copy(
            crossing.at[image], crossing.at[image], sx.at[image], rx.at[image], device_id=beside, device_id_type=MESH
        )

    trade = pltpu.make_async_remote_copy(loss_buf, loss_side, s_loss, r_loss, device_id=beside, device_id_type=MESH)

    def step(i, carry):
        even = i % 2 == 0
        ahead = jnp.where(section == 1, even, (i == 0) | ((i % 2 == 1) & (i < 7)))

        @pl.when(ahead)
        def _():
            image = (i + 1) // 2
            slot = image % 2

            @pl.when(image > 0)
            def _():
                for copy in stores(image - 1, True):
                    copy.wait()

            forward_image(
                rows_buf.at[0, image], weights, l_buf, qkv.at[slot], pt.at[slot], slope.at[slot], h1.at[slot],
                result.at[slot], result_buf, vt, ot,
            )
            diff = result[slot] - rows_buf[1, image].astype(F32)
            loss_buf[0:1, :] += column_sum(diff * diff * scale)
            for copy in stores(image, True):
                copy.start()

            @pl.when(image == IMAGES - 1)
            def _():
                trade.start()

        @pl.when(jnp.logical_not(ahead))
        def _():
            image = (i - 1) // 2
            slot = image % 2

            @pl.when(image > 0)
            def _():
                for copy in stores(image - 1, False):
                    copy.wait()

            @pl.when(section == 0)
            def _():
                cross(image).wait_recv()

            backward_image(
                scale, section == 0, result.at[slot], rows_buf.at[1, image], crossing.at[image], rows_buf.at[0, image], weights,
                qkv.at[slot], pt.at[slot], slope.at[slot], h1.at[slot], d_buf, vec_ref, dh_buf, crossing.at[image],
                vt, ot,
            )

            @pl.when(section == 1)
            def _():
                cross(image).start()

            for copy in stores(image, False):
                copy.start()

        return carry

    lax.fori_loop(0, 2 * IMAGES, step, 0)
    for forward in (True, False):
        for copy in stores(IMAGES - 1, forward):
            copy.wait()

    @pl.when(section == 1)
    def _():
        for image in range(IMAGES):
            cross(image).wait_send()

    trade.wait()
    vec_ref[V_LOSS : V_LOSS + 1, :D] = loss_buf[0:1, :]
    vec_ref[V_SIDE : V_SIDE + 1, :D] = loss_side[0:1, :]


def run_blocks(patches, targets, ids, codebook, weights):
    dma = pltpu.SemaphoreType.DMA
    vm = pltpu.VMEM
    rows = IMAGES * SEQ
    inside, outside = pl.BlockSpec(memory_space=pltpu.VMEM), pl.BlockSpec(memory_space=pl.ANY)
    weight_places = [inside, inside, outside, outside, inside, outside, inside, outside, inside]
    return pl.pallas_call(
        blocks_kernel,
        out_shape=[
            jax.ShapeDtypeStruct((rows, D), BF),
            jax.ShapeDtypeStruct((rows, D), F32),
            jax.ShapeDtypeStruct((rows, L_ALL), BF),
            jax.ShapeDtypeStruct((rows, D_ALL), BF),
            jax.ShapeDtypeStruct((V_ROWS, V_COLS), F32),
        ],
        in_specs=[outside, outside, inside, inside] + weight_places,
        out_specs=[outside] * 4 + [inside],
        scratch_shapes=[
            vm((D, QKV), BF), vm((D, D), BF), vm((D, FF), BF), vm((FF, D), BF),
            vm((16, SLICES, SHARD, SLICE), BF), vm((rows, 128), jnp.int32),
            vm((2, IMAGES, SEQ, D), BF), vm((IMAGES, SEQ, D), BF), vm((8, D), F32), vm((8, D), F32),
            vm((2, SEQ, QKV), BF), vm((2, HEADS, SEQ, SEQ), F32), vm((2, SEQ, FF), F32), vm((2, SEQ, D), F32),
            vm((2, SEQ, D), F32), vm((SEQ, L_ALL), BF), vm((SEQ, D_ALL), BF), vm((SEQ, D), BF), vm((SEQ, D), F32),
            vm((D, SEQ), BF), vm((D, SEQ), BF),
            dma((4,)), dma(()), dma((4,)), dma((8, SLICES)), dma((5, SLICES)),
            dma((4, SLICES)), dma((5, SLICES)), dma((8, SLICES)), dma((8, SLICES)), dma(()), dma(()),
            dma((IMAGES,)), dma((IMAGES,)),
        ],
        compiler_params=pltpu.CompilerParams(collective_id=2, has_side_effects=True, vmem_limit_bytes=VMEM_BYTES),
        name="blocks",
    )(patches.reshape(IMAGES, SEQ, D), targets.reshape(IMAGES, SEQ, D), ids.reshape(1, rows), codebook, *weights)


UNITS = 36
PART = D // 16
COLS = 256
LAG_Y, LAG_Z, HOP = 1, 4, 4
LAG_OUT = LAG_Z + 3 * HOP
BLOCKS = D_ALL // COLS
FIRST_DOWN = 24
EVERY, EARLY = 9, UNITS // 9
LAG_LAST = 3
RING = 20


def reduce_kernel(
    vocab, l_ref, d_ref, vec_ref, qkv_out, out_out, up_out, down_out, vec_out, hist_out, stats_out,
    left, right, product, acc_y, acc_z, tx_c, rx_c, tx_y, rx_y, tx_up, rx_up, tx_dn, rx_dn,
    acc_e, tx_eu, rx_eu, tx_ed, rx_ed, tx_l, rx_l, vec_tx, vec_c, vec_y, vec_z,
    lsem, dsem, sc, rc, sy, ry, s_up, r_up, s_dn, r_dn,
    s_eu, r_eu, s_ed, r_ed, s_l, r_l, sv, rv,
):
    sec, dp = lax.axis_index("section"), lax.axis_index("dp")
    core, y, z = dp % 2, (dp // 2) % 2, dp // 4
    across = (sec, dp + 1 - 2 * core)
    along_y = (sec, dp + 2 - 4 * y)
    along_z = [(sec, (z + k) % 4 * 4 + y * 2 + core) for k in (1, 2, 3)]
    above, below = (sec, jnp.minimum(dp + 4, 12 + dp % 4)), (sec, jnp.maximum(dp - 4, dp % 4))

    lefts = [pltpu.make_async_copy(l_ref.at[:, i * D : (i + 1) * D], left.at[i], lsem.at[i]) for i in range(7)]

    def load_right(n):
        cols = pl.ds(pl.multiple_of(n * COLS, COLS), COLS)
        return pltpu.make_async_copy(d_ref.at[:, cols], right.at[n % 2], dsem.at[n % 2])

    lefts[0].start()
    load_right(0).start()

    barrier = pltpu.get_barrier_semaphore()
    for target in [across, along_y] + along_z:
        pl.semaphore_signal(barrier, inc=1, device_id=target, device_id_type=MESH)
    pl.semaphore_wait(barrier, 5)

    def remote(src, dst, send, recv, target):
        return pltpu.make_async_remote_copy(src, dst, send, recv, device_id=target, device_id_type=MESH)

    def send_core(u):
        return remote(tx_c.at[u % 2], rx_c.at[u], sc.at[u % 2], rc.at[u], across)

    def send_y(u):
        return remote(tx_y.at[u % RING], rx_y.at[u], sy.at[u % RING], ry.at[u], along_y)

    def up_link(at, high, tx, rx, send, recv):
        rows = slice(at * high, 3 * high)
        return remote(tx.at[rows], rx.at[rows], send, recv, above)

    def dn_link(at, high, tx, rx, send, recv):
        rows = slice(0, at * high)
        return remote(tx.at[rows], rx.at[rows], send, recv, below)

    def send_last(u):
        return remote(tx_l.at[u], rx_l.at[u], s_l.at[u], r_l.at[u], along_y)

    def is_early(u):
        return u % EVERY == 2

    def valid(u):
        return (u >= 0) & (u < UNITS)

    def climb(high, acc, tx, rx, send, recv):
        for at in range(4):

            @pl.when(z == at)
            def _():
                if at > 0:
                    up_link(at - 1, high, tx, rx, send, recv).wait_recv()
                if at < 3:
                    t = acc[(at + 1) * high : 4 * high]
                    if at > 0:
                        t = t + rx[at * high : 3 * high].astype(F32)
                    tx[at * high : 3 * high] = t.astype(BF)
                    up_link(at, high, tx, rx, send, recv).start()

    def sink(high, acc, tx, rx, send, recv):
        for at in range(4):

            @pl.when(z == at)
            def _():
                if at < 3:
                    dn_link(at + 1, high, tx, rx, send, recv).wait_recv()
                if at > 0:
                    t = acc[: at * high]
                    if at < 3:
                        t = t + rx[: at * high].astype(F32)
                    tx[: at * high] = t.astype(BF)
                    dn_link(at, high, tx, rx, send, recv).start()

    def settle(high, acc, up, dn):
        for at in range(4):

            @pl.when(z == at)
            def _():
                t = acc[at * high : (at + 1) * high]
                if at < 3:
                    up_link(at, high, *up).wait_send()
                    t = t + dn[1][at * high : (at + 1) * high].astype(F32)
                if at > 0:
                    dn_link(at, high, *dn).wait_send()
                    t = t + up[1][(at - 1) * high : at * high].astype(F32)
                acc[at * high : (at + 1) * high] = t

    def up_args(u):
        return tx_up.at[u % RING], rx_up.at[u], s_up.at[u % RING], r_up.at[u]

    def dn_args(u):
        return tx_dn.at[u % RING], rx_dn.at[u], s_dn.at[u % RING], r_dn.at[u]

    def early_up(e):
        return tx_eu.at[e], rx_eu.at[e], s_eu.at[e], r_eu.at[e]

    def early_dn(e):
        return tx_ed.at[e], rx_ed.at[e], s_ed.at[e], r_ed.at[e]

    vec_core = remote(vec_ref, vec_c, sv.at[0], rv.at[0], across)
    vec_along_y = remote(vec_tx, vec_y, sv.at[1], rv.at[1], along_y)
    vec_along_z = [remote(vec_z.at[z], vec_z.at[z], sv.at[2 + k], rv.at[2 + k], along_z[k]) for k in range(3)]
    vec_core.start()

    def multiply(u):
        down = u >= FIRST_DOWN
        n = jnp.where(down, FIRST_DOWN + (u - FIRST_DOWN) // 4, u)
        fresh = jnp.logical_not(down) | (u % 4 == 0)

        @pl.when(fresh & (n + 1 < BLOCKS))
        def _():
            load_right(n + 1).start()

        @pl.when(fresh)
        def _():
            load_right(n).wait()

        @pl.when(u == 1)
        def _():
            for load in lefts[1:]:
                load.start()

        for i, first in enumerate((0, 12, 15, FIRST_DOWN)):

            @pl.when(u == first)
            def _():
                for load in lefts[i : i + 1] if i < 3 else lefts[3:]:
                    load.wait()

        @pl.when(jnp.logical_not(down))
        def _():
            which = jnp.where(u < 12, 0, jnp.where(u < 15, 1, 2))
            product[:D] = matmul_tn(left[which], right[n % 2])

        @pl.when(down & fresh)
        def _():
            for i in range(4):
                product[i * D : (i + 1) * D] = matmul_tn(left[3 + i], right[n % 2])

        def rows_for(place):
            owner = place % 4 * 4 + (y + place // 4 % 2) % 2 * 2 + (core + place // 8) % 2
            row = jnp.where(down, owner * (4 * PART) + u % 4 * PART, owner * PART)
            return product[pl.ds(pl.multiple_of(row, PART), PART), :]

        for place in range(8):
            tx_c[u % 2, place * PART : (place + 1) * PART] = rows_for(8 + place).astype(BF)
        send_core(u).start()
        for place in range(8):
            acc_y[u % 2, place * PART : (place + 1) * PART] = rows_for(place)

    def step(i, carry):
        @pl.when(i < UNITS)
        def _():
            multiply(i)

        @pl.when((i >= LAG_Y) & (i < UNITS + LAG_Y))
        def _():
            u = i - LAG_Y
            send_core(u).wait()

            @pl.when(is_early(u))
            def _():
                t = acc_y[u % 2] + rx_c[u].astype(F32)
                for place in range(8):
                    to = (2 * (place % 4) + place // 4) * PART
                    acc_e[u // EVERY, to : to + PART] = t[place * PART : (place + 1) * PART]

            @pl.when(jnp.logical_not(is_early(u)))
            def _():
                tx_y[u % RING] = (acc_y[u % 2, 4 * PART :] + rx_c[u, 4 * PART :].astype(F32)).astype(BF)
                send_y(u).start()
                acc_z[u % RING] = acc_y[u % 2, : 4 * PART] + rx_c[u, : 4 * PART].astype(F32)

        @pl.when(valid(i - LAG_Z) & jnp.logical_not(is_early(i - LAG_Z)))
        def _():
            u = i - LAG_Z
            send_y(u).wait()
            acc_z[u % RING] = acc_z[u % RING] + rx_y[u].astype(F32)

        u_up = i - LAG_Z - z * HOP

        @pl.when(valid(u_up) & jnp.logical_not(is_early(u_up)))
        def _():
            climb(PART, acc_z.at[u_up % RING], *up_args(u_up))

        @pl.when(valid(u_up) & is_early(u_up))
        def _():
            climb(2 * PART, acc_e.at[u_up // EVERY], *early_up(u_up // EVERY))

        u_dn = i - LAG_Z - (3 - z) * HOP

        @pl.when(valid(u_dn) & jnp.logical_not(is_early(u_dn)))
        def _():
            sink(PART, acc_z.at[u_dn % RING], *dn_args(u_dn))

        @pl.when(valid(u_dn) & is_early(u_dn))
        def _():
            sink(2 * PART, acc_e.at[u_dn // EVERY], *early_dn(u_dn // EVERY))

        def put(u, t):
            def lanes(n):
                return pl.ds(pl.multiple_of(n * COLS, COLS), COLS)

            @pl.when(u < 12)
            def _():
                up_out[:, lanes(u)] = t

            @pl.when((u >= 12) & (u < 15))
            def _():
                out_out[:, lanes(u - 12)] = t

            @pl.when((u >= 15) & (u < FIRST_DOWN))
            def _():
                qkv_out[:, lanes(u - 15)] = t

            @pl.when(u >= FIRST_DOWN)
            def _():
                rows = pl.ds(pl.multiple_of(u % 4 * PART, PART), PART)
                down_out[rows, lanes((u - FIRST_DOWN) // 4)] = t

        @pl.when(valid(i - LAG_OUT) & is_early(i - LAG_OUT))
        def _():
            e = (i - LAG_OUT) // EVERY
            settle(2 * PART, acc_e.at[e], early_up(e), early_dn(e))
            rows = pl.ds(pl.multiple_of((2 * z + 1) * PART, PART), PART)
            tx_l[e] = acc_e[e, rows, :].astype(BF)
            send_last(e).start()

        @pl.when(valid(i - LAG_OUT - LAG_LAST) & is_early(i - LAG_OUT - LAG_LAST))
        def _():
            u = i - LAG_OUT - LAG_LAST
            e = u // EVERY
            send_last(e).wait()
            rows = pl.ds(pl.multiple_of(2 * z * PART, PART), PART)
            put(u, acc_e[e, rows, :] + rx_l[e].astype(F32))

        @pl.when(valid(i - LAG_OUT) & jnp.logical_not(is_early(i - LAG_OUT)))
        def _():
            u = i - LAG_OUT
            settle(PART, acc_z.at[u % RING], up_args(u), dn_args(u))
            put(u, acc_z[u % RING, pl.ds(pl.multiple_of(z * PART, PART), PART), :])

        @pl.when(i == 3)
        def _():
            vec_core.wait()
            vec_tx[...] = vec_ref[...] + vec_c[...]
            vec_along_y.start()

        @pl.when(i == 8)
        def _():
            vec_along_y.wait()
            vec_z[z] = vec_tx[...] + vec_y[...]
            for copy in vec_along_z:
                copy.start()

        @pl.when(i == 14)
        def _():
            for copy in vec_along_z:
                copy.wait()
            vec_out[...] = (vec_z[0] + vec_z[1]) + (vec_z[2] + vec_z[3])

        return carry

    lax.fori_loop(0, UNITS + LAG_OUT, step, 0)

    def total(value):
        return jnp.sum(jnp.sum(value, axis=1, keepdims=True), axis=0, keepdims=True)

    tokens = 16 * l_ref.shape[0]
    counts = vec_out[:, D:]
    shares = counts * (1.0 / tokens)
    entropy = -total(shares * jnp.log(jnp.where(counts > 0, shares, 1.0)))
    used = total((counts > 0).astype(F32))
    loss = total(vec_out[V_LOSS : V_LOSS + 1, :D]) + total(vec_out[V_SIDE : V_SIDE + 1, :D])
    lane = lax.broadcasted_iota(jnp.int32, (8, 128), 1)
    last = jnp.where(lane == 1, used / vocab, jnp.exp(entropy) / vocab)
    stats_out[...] = jnp.where(lane == 0, loss / (tokens * D), last)
    hist_out[...] = vec_out[pl.ds(dp, 1), D:].astype(jnp.int32)


def reduce_weights(l, d, vec, vocab):
    dma = pltpu.SemaphoreType.DMA
    vm = pltpu.VMEM
    rows = l.shape[0]
    sums = (V_ROWS, V_COLS)
    return pl.pallas_call(
        functools.partial(reduce_kernel, vocab),
        out_shape=[
            jax.ShapeDtypeStruct((PART, QKV), F32),
            jax.ShapeDtypeStruct((PART, D), F32),
            jax.ShapeDtypeStruct((PART, FF), F32),
            jax.ShapeDtypeStruct((4 * PART, D), F32),
            jax.ShapeDtypeStruct(sums, F32),
            jax.ShapeDtypeStruct((1, V_COLS - D), jnp.int32),
            jax.ShapeDtypeStruct((8, 128), F32),
        ],
        in_specs=[pl.BlockSpec(memory_space=pl.ANY)] * 2 + [pl.BlockSpec(memory_space=pltpu.VMEM)],
        out_specs=[pl.BlockSpec(memory_space=pltpu.VMEM)] * 7,
        scratch_shapes=[
            vm((7, rows, D), BF), vm((2, rows, COLS), BF), vm((4 * D, COLS), F32),
            vm((2, 8 * PART, COLS), F32), vm((RING, 4 * PART, COLS), F32),
            vm((2, 8 * PART, COLS), BF), vm((UNITS, 8 * PART, COLS), BF),
            vm((RING, 4 * PART, COLS), BF), vm((UNITS, 4 * PART, COLS), BF),
            vm((RING, 3 * PART, COLS), BF), vm((UNITS, 3 * PART, COLS), BF),
            vm((RING, 3 * PART, COLS), BF), vm((UNITS, 3 * PART, COLS), BF),
            vm((EARLY, 8 * PART, COLS), F32), vm((EARLY, 6 * PART, COLS), BF), vm((EARLY, 6 * PART, COLS), BF),
            vm((EARLY, 6 * PART, COLS), BF), vm((EARLY, 6 * PART, COLS), BF),
            vm((EARLY, PART, COLS), BF), vm((EARLY, PART, COLS), BF),
            vm(sums, F32), vm(sums, F32), vm(sums, F32), vm((4,) + sums, F32),
            dma((7,)), dma((2,)), dma((2,)), dma((UNITS,)), dma((RING,)), dma((UNITS,)),
            dma((RING,)), dma((UNITS,)), dma((RING,)), dma((UNITS,)),
            dma((EARLY,)), dma((EARLY,)), dma((EARLY,)), dma((EARLY,)), dma((EARLY,)), dma((EARLY,)),
            dma((5,)), dma((5,)),
        ],
        compiler_params=pltpu.CompilerParams(collective_id=1, has_side_effects=True, vmem_limit_bytes=REDUCE_BYTES),
        name="weight_grad_reduce",
    )(l, d, vec)


def finish(result, dh, g_qkv, g_out, g_up, g_down, vec, hist, stats, shard):
    rows = result.shape[0]
    pieces = 1

    def body(result_ref, dh_ref, qkv_ref, out_ref, up_ref, down_ref, vec_ref, hist_ref, stats_ref,
             result_to, dh_to, gains_to, shifts_to, qkv_to, out_to, out_bias_to, up_to, up_bias_to, down_to, down_bias_to, hist_to, stats_to, *scratch):
        (outof,) = scratch
        copies = []
        for src, dst in ((dh_ref, dh_to), (result_ref, result_to)):
            for i in range(pieces):
                part = pl.ds(i * rows // pieces, rows // pieces)
                copies.append((src.at[part], dst.at[0, part]))
        copies += [(qkv_ref, qkv_to.at[0]), (out_ref, out_to.at[0]), (up_ref, up_to.at[0]), (down_ref, down_to.at[0])]
        saves = [pltpu.make_async_copy(src, dst, outof.at[i]) for i, (src, dst) in enumerate(copies)]
        for save in saves:
            save.start()
        gains_to[0] = vec_ref[0:2, :D]
        shifts_to[0] = vec_ref[2:4, :D]
        out_bias_to[...] = vec_ref[4:5, :D]
        for j in range(FF // D):
            up_bias_to[:, j * D : (j + 1) * D] = vec_ref[5 + j : 6 + j, :D]
        down_bias_to[...] = vec_ref[9:10, :D]
        hist_to[...] = hist_ref[0, :shard]
        stats_to[...] = stats_ref[0, :3]
        for save in saves:
            save.wait()

    inside, outside = pl.BlockSpec(memory_space=pltpu.VMEM), pl.BlockSpec(memory_space=pl.ANY)

    def shape(*dims, dtype=F32):
        return jax.ShapeDtypeStruct((1,) + dims, dtype)

    out = pl.pallas_call(
        body,
        out_shape=[
            shape(rows, D, dtype=BF), shape(rows, D), shape(2, D), shape(2, D), shape(PART, QKV), shape(PART, D),
            shape(D), shape(PART, FF), shape(FF), shape(4 * PART, D), shape(D),
            jax.ShapeDtypeStruct((shard,), jnp.int32), jax.ShapeDtypeStruct((3,), F32),
        ],
        in_specs=[outside] * 6 + [inside] * 3,
        out_specs=[outside, outside, inside, inside, outside, outside, inside, outside, inside, outside, inside, inside, inside],
        scratch_shapes=[
            pltpu.SemaphoreType.DMA((2 * pieces + 4,)),
        ],
        compiler_params=pltpu.CompilerParams(vmem_limit_bytes=PLACE_BYTES),
        name="place_outputs",
    )(result, dh, g_qkv, g_out, g_up, g_down, vec, hist, stats)
    return tuple(out)


def count_shares(counts, total_count):
    shares = counts / total_count
    nonzero_share = jnp.where(counts > 0, shares, 1.0)
    return -jnp.sum(shares * jnp.log(nonzero_share)), jnp.sum((counts > 0).astype(F32))


def on_device(
    patches, targets, code_ids, codebook, norm_gains, norm_shifts, w_qkv, w_out, out_bias, w_up, up_bias, w_down, down_bias
):
    section = lax.axis_index("section")
    leading = section == 0
    dp_size = lax.axis_size("dp")
    dp = lax.axis_index("dp")
    weights = (
        norm_gains[0], norm_shifts[0], w_qkv[0], w_out[0], out_bias, w_up[0], up_bias, w_down[0], down_bias
    )
    rows, width = patches.shape
    images = rows // SEQ
    vocab_local = codebook.shape[0]
    vocab_all = vocab_local * dp_size
    total_tokens = rows * dp_size

    small = dp_size == 16 and vocab_local <= SHARD and rows == IMAGES * SEQ
    if small:
        result_bf, dh, l, d, vec = run_blocks(patches, targets, code_ids, codebook, weights)
        g_qkv, g_out, g_up, g_down, vec, hist, stats = reduce_weights(l, d, vec, vocab_all)
        return finish(result_bf, dh, g_qkv, g_out, g_up, g_down, vec, hist, stats, vocab_local)
    else:
        shard_rows = lax.all_gather(codebook, "dp", axis=0, tiled=True)
        chosen = jnp.take(shard_rows, jnp.clip(code_ids, 0, vocab_all - 1), axis=0)
        x = jnp.where(leading, patches, chosen)
        l, qkv, pt, slope, h1, result, result_bf = block_forward(x, weights)
        other = jnp.where(leading, chosen, targets)
        d = dh = None
        vec = jnp.zeros((V_ROWS, V_COLS), F32)
        arrived = jnp.zeros((SEQ, D), BF)
        for moment in range(images + 1):
            which = jnp.clip(moment - 1 + section, 0, images - 1).astype(jnp.int32)[None]
            active = jnp.where(leading, moment >= 1, moment < images).astype(F32)
            flags = jnp.stack(
                [jnp.where(leading, COMMIT_WEIGHT, 1.0).astype(F32), active, jnp.where(leading, 1.0, 0.0).astype(F32)]
            )
            d, dh, vec, outgoing = block_backward(
                which, flags, result, other, arrived, x, weights, qkv, pt, slope, h1, vec, d, dh
            )
            if moment < images:
                arrived = lax.ppermute(outgoing, "section", [(1, 0)])
        pairs = (
            (l[:, L_A:L_M], d[:, D_QKV:D_GB]),
            (l[:, L_O:L_A], d[:, D_GH:D_QKV]),
            (l[:, :L_O], d[:, :D_GH]),
            (l[:, L_M:], d[:, D_GB:]),
        )
        g_qkv, g_out, g_up, g_down = (
            lax.psum_scatter(matmul_tn(left, right), "dp", scatter_dimension=0, tiled=True) for left, right in pairs
        )
        vocab_iota = lax.broadcasted_iota(jnp.int32, (1, vocab_all), 1)
        counts = jnp.sum((code_ids[:, None] == vocab_iota).astype(F32), axis=0)
        hist_local = lax.psum_scatter(counts, "dp", scatter_dimension=0, tiled=True)
        entropy_part, used_part = count_shares(hist_local, total_tokens)
        hist_local = hist_local.astype(jnp.int32)
        vec = lax.psum(vec, "dp")
        entropy_all, used_all = lax.psum((entropy_part, used_part), "dp")
        loss_all = lax.psum(jnp.sum(vec[V_LOSS, :D]), "section")
        stats = jnp.stack(
            [loss_all / (total_tokens * width), used_all / vocab_all, jnp.exp(entropy_all) / vocab_all]
        )
    return (
        result_bf[None],
        dh[None],
        vec[None, 0:2, :D],
        vec[None, 2:4, :D],
        g_qkv[None],
        g_out[None],
        vec[None, 4, :D],
        g_up[None],
        vec[5:9, :D].reshape(1, FF),
        g_down[None],
        vec[None, 9, :D],
        hist_local,
        stats,
    )


def solution(mesh):
    return jax.shard_map(
        on_device,
        mesh=mesh,
        in_specs=(
            P("dp", None),
            P("dp", None),
            P("dp"),
            P("dp", None),
            P("section", None, None),
            P("section", None, None),
            P("section", None, None),
            P("section", None, None),
            P("section", None),
            P("section", None, None),
            P("section", None),
            P("section", None, None),
            P("section", None),
        ),
        out_specs=(
            P("section", "dp", None),
            P("section", "dp", None),
            P("section", None, None),
            P("section", None, None),
            P("section", "dp", None),
            P("section", "dp", None),
            P("section", None),
            P("section", "dp", None),
            P("section", None),
            P("section", "dp", None),
            P("section", None),
            P("dp"),
            P(),
        ),
        check_vma=False,
    )
```

```python
import functools

import jax
import jax.numpy as jnp
from jax import lax
from jax.experimental import pallas as pl
from jax.experimental.pallas import tpu as pltpu
from jax.sharding import PartitionSpec as P

SEQ = 256
D = 768
HD = 64
HEADS = 12
FF = 3072
FF_PIECE = 768
QKV = 3 * D
L_O, L_A, L_M, L_ALL = D, 2 * D, 3 * D, 3 * D + FF
D_GH, D_QKV, D_GB, D_ALL = FF, FF + D, FF + D + QKV, FF + D + QKV + D
V_SIDE, V_LOSS, V_ROWS, V_COLS = 14, 15, 16, D + 256

COMMIT_WEIGHT = 0.25
EPSILON = 1e-06
SQRT_HALF = 0.5**0.5
INV_ROOT_TAU = 0.3989422804014327
LOG2_E = 1.4426950408889634
HEAD_SCALE = HD**-0.5
MESH = pl.DeviceIdType.MESH
BF, F32 = jnp.bfloat16, jnp.float32
VMEM_BYTES, REDUCE_BYTES, PLACE_BYTES = 60 << 20, 48 << 20, 14 << 20


def matmul_nn(left, right):
    return jnp.dot(left, right, preferred_element_type=F32)


def matmul_nt(left, right):
    return lax.dot_general(left, right, (((1,), (1,)), ((), ())), preferred_element_type=F32)


def matmul_tn(left, right):
    return lax.dot_general(left, right, (((0,), (0,)), ((), ())), preferred_element_type=F32)


def layer_norm(rows_in):
    centered = rows_in - jnp.mean(rows_in, axis=-1, keepdims=True)
    inv_std = lax.rsqrt(jnp.mean(centered * centered, axis=-1, keepdims=True) + EPSILON)
    return centered * inv_std, inv_std


def norm_back(incoming, scaled, inv_std, gain_row):
    x = incoming * gain_row
    return inv_std * (
        x
        - jnp.mean(x, axis=-1, keepdims=True)
        - scaled * jnp.mean(x * scaled, axis=-1, keepdims=True)
    )


def column_sum(x):
    return jnp.sum(x, axis=0, keepdims=True)


def head_masks():
    low = lax.broadcasted_iota(jnp.int32, (1, 2 * HD), 1) < HD
    ones = low.astype(F32)
    return ones.astype(BF), (1.0 - ones).astype(BF)


def head_pair(ref, base, head):
    return ref[:, base + head // 2 * 128 : base + (head // 2 + 1) * 128]


def forward_image(x_ref, weights, l_ref, qkv_ref, pt_ref, slope_ref, h1_ref, out_ref, outb_ref, vt_ref, ot_ref):
    gains, shifts, w_qkv, w_out, out_bias, w_up, up_bias, w_down, down_bias = weights
    h = x_ref[...].astype(F32)
    s1, _ = layer_norm(h)
    a = (s1 * gains[0:1, :] + shifts[0:1, :]).astype(BF)
    l_ref[:, L_A:L_M] = a
    for j in range(3):
        qkv_ref[:, j * D : (j + 1) * D] = matmul_nn(a, w_qkv[:, j * D : (j + 1) * D]).astype(BF)
    vt_ref[...] = qkv_ref[:, 2 * D : 3 * D].T
    masks = head_masks()
    scores = [
        matmul_nt(head_pair(qkv_ref, D, head) * masks[head % 2], head_pair(qkv_ref, 0, head)) for head in range(HEADS)
    ]
    for head in range(HEADS):
        st = scores[head]
        e = jnp.exp2((st - jnp.max(st, axis=0, keepdims=True)) * (HEAD_SCALE * LOG2_E))
        pt_ref[head] = e * (1.0 / column_sum(e))
    for head in range(HEADS):
        span = slice(head * HD, (head + 1) * HD)
        ot_ref[span, :] = matmul_nn(vt_ref[span, :], pt_ref[head].astype(BF)).astype(BF)
    o = ot_ref[...].T
    l_ref[:, L_O:L_A] = o
    h1 = h + matmul_nn(o, w_out[...]) + out_bias[...]
    h1_ref[...] = h1
    s2, _ = layer_norm(h1)
    b = (s2 * gains[1:2, :] + shifts[1:2, :]).astype(BF)
    l_ref[:, 0:L_O] = b
    result = h1 + down_bias[...]
    for j in range(FF // FF_PIECE):
        span = slice(j * FF_PIECE, (j + 1) * FF_PIECE)
        u = matmul_nn(b, w_up[:, span]) + up_bias[:, span]
        half_curve = 0.5 + 0.5 * lax.erf(u * SQRT_HALF)
        m = (u * half_curve).astype(BF)
        l_ref[:, L_M + j * FF_PIECE : L_M + (j + 1) * FF_PIECE] = m
        slope = half_curve + u * jnp.exp(-0.5 * u * u) * INV_ROOT_TAU
        slope_ref[:, span] = slope
        result = result + matmul_nn(m, w_down[span, :])
    out_ref[...] = result
    outb_ref[...] = result.astype(BF)


def backward_image(
    scale, receives, out_ref, other_ref, arrived_ref, x_ref, weights, qkv_ref, pt_ref, slope_ref, h1_ref,
    d_ref, vec_ref, dh_ref, dhb_ref, kt_ref, qt_ref,
):
    gains, shifts, w_qkv, w_out, out_bias, w_up, up_bias, w_down, down_bias = weights
    diff = out_ref[...] - other_ref[...].astype(F32)

    def add(row, value):
        vec_ref[row : row + 1, :D] += column_sum(value)

    g = diff * scale + jnp.where(receives, arrived_ref[...].astype(F32), 0.0)
    gb = g.astype(BF)
    d_ref[:, D_GB:D_ALL] = gb
    add(9, g)
    db = jnp.zeros((SEQ, D), F32)
    for j in range(FF // FF_PIECE):
        span = slice(j * FF_PIECE, (j + 1) * FF_PIECE)
        du = (matmul_nt(gb, w_down[span, :]) * slope_ref[:, span]).astype(BF)
        d_ref[:, span] = du
        add(5 + j, du.astype(F32))
        db = db + matmul_nt(du, w_up[:, span])
    s2, inv2 = layer_norm(h1_ref[...])
    add(1, db * s2)
    add(3, db)
    dh1 = g + norm_back(db, s2, inv2, gains[1:2, :])
    add(4, dh1)
    gh = dh1.astype(BF)
    d_ref[:, D_GH:D_QKV] = gh
    do = matmul_nt(gh, w_out[...]).astype(BF)
    kt_ref[...] = qkv_ref[:, D : 2 * D].T
    masks = head_masks()

    def do_pair(head):
        return do[:, head // 2 * 128 : (head // 2 + 1) * 128]

    dpts = [matmul_nt(head_pair(qkv_ref, 2 * D, head) * masks[head % 2], do_pair(head)) for head in range(HEADS)]

    def both(parts, pair, make):
        return matmul_nn(
            jnp.concatenate(parts[2 * pair : 2 * pair + 2], axis=1),
            jnp.concatenate([make(2 * pair) * masks[0], make(2 * pair) * masks[1]], axis=0),
        )

    base = D_QKV + D
    for pair in range(HEADS // 2):
        dv = both([pt_ref[head].astype(BF) for head in range(HEADS)], pair, do_pair)
        d_ref[:, base + D + pair * 128 : base + D + (pair + 1) * 128] = dv.astype(BF)
    dsts = []
    for head in range(HEADS):
        ptf = pt_ref[head]
        dsts.append((ptf * (dpts[head] - column_sum(dpts[head] * ptf))).astype(BF))
    for pair in range(HEADS // 2):
        dk = both(dsts, pair, lambda head: head_pair(qkv_ref, 0, head))
        d_ref[:, base + pair * 128 : base + (pair + 1) * 128] = (dk * HEAD_SCALE).astype(BF)
    for head in range(HEADS):
        span = slice(head * HD, (head + 1) * HD)
        qt_ref[span, :] = (matmul_nn(kt_ref[span, :], dsts[head]) * HEAD_SCALE).astype(BF)
    d_ref[:, D_QKV : D_QKV + D] = qt_ref[...].T
    da = matmul_nt(d_ref[:, D_QKV:D_GB], w_qkv[...])
    s1, inv1 = layer_norm(x_ref[...].astype(F32))
    add(0, da * s1)
    add(2, da)
    dh = dh1 + norm_back(da, s1, inv1, gains[0:1, :])
    dh_ref[...] = dh
    dhb_ref[...] = dh.astype(BF)


WEIGHT_SHAPES = ((2, D), (2, D), (D, QKV), (D, D), (1, D), (D, FF), (1, FF), (FF, D), (1, D))


def weight_specs():
    def whole(shape):
        return pl.BlockSpec(shape, lambda *_: (0, 0), pipeline_mode=pl.Buffered(1))

    return [whole(shape) for shape in WEIGHT_SHAPES]


def block_forward(x, weights):
    rows = x.shape[0]
    images = rows // SEQ

    def row_block(width):
        return pl.BlockSpec((SEQ, width), lambda i: (i, 0))

    def body(x_ref, *refs):
        forward_image(x_ref, refs[:9], *refs[9:])

    def shape(width, dtype):
        return jax.ShapeDtypeStruct((rows, width), dtype)

    return pl.pallas_call(
        body,
        grid=(images,),
        in_specs=[row_block(D)] + weight_specs(),
        out_specs=[
            row_block(L_ALL),
            row_block(QKV),
            pl.BlockSpec((HEADS, SEQ, SEQ), lambda i: (i, 0, 0)),
            row_block(FF),
            row_block(D),
            row_block(D),
            row_block(D),
        ],
        out_shape=[
            shape(L_ALL, BF),
            shape(QKV, BF),
            jax.ShapeDtypeStruct((images * HEADS, SEQ, SEQ), F32),
            shape(FF, F32),
            shape(D, F32),
            shape(D, F32),
            shape(D, BF),
        ],
        scratch_shapes=[pltpu.VMEM((D, SEQ), BF), pltpu.VMEM((D, SEQ), BF)],
        compiler_params=pltpu.CompilerParams(vmem_limit_bytes=VMEM_BYTES),
        name="block_forward",
    )(x, *weights)


def block_backward(which, flags, result, other, arrived, x, weights, qkv, pt, slope, h1, vec, d, dh):
    rows = x.shape[0]

    def row_block(width):
        return pl.BlockSpec((SEQ, width), lambda i, which_ref: (which_ref[0], 0))

    def whole(height, width):
        return pl.BlockSpec((height, width), lambda i, which_ref: (0, 0))

    def body(which_ref, flags_ref, out_ref, other_ref, arrived_ref, x_ref, *refs):
        weight_refs = refs[:9]
        qkv_ref, pt_ref, slope_ref, h1_ref, vec_in = refs[9:14]
        d_ref, dh_ref, vec_out, dhb_ref, kt_ref, qt_ref = refs[-6:]
        vec_out[...] = jnp.zeros_like(vec_out)
        backward_image(
            flags_ref[0], flags_ref[2] > 0, out_ref, other_ref, arrived_ref, x_ref, weight_refs, qkv_ref, pt_ref,
            slope_ref, h1_ref, d_ref, vec_out, dh_ref, dhb_ref, kt_ref, qt_ref,
        )
        diff = out_ref[...] - other_ref[...].astype(F32)
        vec_out[V_LOSS : V_LOSS + 1, :D] = column_sum(diff * diff * flags_ref[0])
        vec_out[...] = vec_in[...] + vec_out[...] * flags_ref[1]

    keep = [] if d is None else [d, dh]
    first_kept = 2 + 4 + 9 + 5
    return pl.pallas_call(
        body,
        grid_spec=pltpu.PrefetchScalarGridSpec(
            num_scalar_prefetch=1,
            grid=(1,),
            in_specs=[pl.BlockSpec(memory_space=pltpu.SMEM), row_block(D), row_block(D), whole(SEQ, D), row_block(D)]
            + weight_specs()
            + [
                row_block(QKV),
                pl.BlockSpec((HEADS, SEQ, SEQ), lambda i, which_ref: (which_ref[0], 0, 0)),
                row_block(FF),
                row_block(D),
                whole(V_ROWS, V_COLS),
            ]
            + [pl.BlockSpec(memory_space=pl.ANY)] * len(keep),
            out_specs=[row_block(D_ALL), row_block(D), whole(V_ROWS, V_COLS), whole(SEQ, D)],
            scratch_shapes=[pltpu.VMEM((D, SEQ), BF), pltpu.VMEM((D, SEQ), BF)],
        ),
        out_shape=[
            jax.ShapeDtypeStruct((rows, D_ALL), BF),
            jax.ShapeDtypeStruct((rows, D), F32),
            jax.ShapeDtypeStruct((V_ROWS, V_COLS), F32),
            jax.ShapeDtypeStruct((SEQ, D), BF),
        ],
        input_output_aliases={first_kept: 0, first_kept + 1: 1} if keep else {},
        compiler_params=pltpu.CompilerParams(vmem_limit_bytes=VMEM_BYTES),
        name="block_backward",
    )(which, flags, result, other, arrived, x, *weights, qkv, pt, slope, h1, vec, *keep)


IMAGES = 4
SHARD = 208
SLICES = 3
SLICE = D // SLICES


def blocks_kernel(
    patches_ref, targets_ref, ids_ref, codebook_ref, gains, shifts, w_qkv_ref, w_out_ref, out_bias, w_up_ref, up_bias,
    w_down_ref, down_bias, result_ref, dh_ref, l_ref, d_ref, vec_ref,
    w_qkv, w_out, w_up, w_down, shards, ids_col, rows_buf, crossing, loss_buf, loss_side,
    qkv, pt, slope, h1, result, l_buf, d_buf, result_buf, dh_buf, vt, ot,
    w_sem, in_sem, out_sem, r_in, s_z, s_y, s_x, s_c, r_c, s_loss, r_loss, sx, rx,
):
    section, dp = lax.axis_index("section"), lax.axis_index("dp")
    core, y, z = dp % 2, (dp // 2) % 2, dp // 4
    across = (section, dp + 1 - 2 * core)
    along_y = (section, dp + 2 - 4 * y)
    along_z = [(section, (z + k) % 4 * 4 + y * 2 + core) for k in (1, 2, 3)]
    beside = (1 - section, dp)

    big = ((w_qkv_ref, w_qkv), (w_out_ref, w_out), (w_up_ref, w_up), (w_down_ref, w_down))
    loads = [pltpu.make_async_copy(src, dst, w_sem.at[i]) for i, (src, dst) in enumerate(big)]
    for load in loads:
        load.start()
    patch_load = pltpu.make_async_copy(patches_ref, rows_buf.at[0], in_sem)
    target_load = pltpu.make_async_copy(targets_ref, rows_buf.at[1], in_sem)

    @pl.when(section == 0)
    def _():
        patch_load.start()

    @pl.when(section == 1)
    def _():
        target_load.start()

    rows_here = codebook_ref.shape[0]
    for p in range(SLICES):
        shards[dp, p] = jnp.zeros((SHARD, SLICE), BF)
        shards[dp, p, :rows_here] = codebook_ref[:, p * SLICE : (p + 1) * SLICE]

    barrier = pltpu.get_barrier_semaphore()
    for target in [across, along_y, beside] + along_z:
        pl.semaphore_signal(barrier, inc=1, device_id=target, device_id_type=MESH)
    pl.semaphore_wait(barrier, 6)

    home = section == core
    corner = (z == 0) | (z == 3)
    near_1 = jnp.where(z == 0, 3, 1)
    near_2 = jnp.where(corner, 2, 3)
    near_3 = jnp.where(z == 0, 1, jnp.where(z == 3, 3, 2))
    def place_of(number):
        return (z - number % 4 + 4) % 4 * 4 + (y + number // 4) % 2 * 2 + core

    def move(place, p, send, recv, target):
        part = shards.at[place, p]
        return pltpu.make_async_remote_copy(part, part, send.at[p], recv.at[p], device_id=target, device_id_type=MESH)

    def send_z(order, place, up, p):
        towards = jnp.where(up, z + 1, z - 1)
        number = (towards - place // 4 + 4) % 4
        return move(place, p, s_z.at[order], r_in.at[number], (section, towards * 4 + y * 2 + core))

    def pass_on(e, p):
        up = (e == 1) | ((e == 5) & (z == 2))
        return send_z((e + 3) // 2, place_of(number_at(e)), up, p)

    def send_y(order, number, p):
        return move(place_of(number), p, s_y.at[order], r_in.at[4 + number], along_y)

    def send_x(order, number, p):
        return move(place_of(number), p, s_x.at[order], r_in.at[number], beside)

    def send_core(order, number, p):
        return move(place_of(number), p, s_c.at[order], r_c.at[order], across)

    pieces = range(SLICES)

    def number_at(e):
        pairs = ((1, near_1), (2, 4), (3, near_2), (4, 4 + near_1), (5, near_3), (6, 4 + near_2), (7, 4 + near_3))
        number = 0
        for at, value in pairs:
            number = jnp.where(e == at, value, number)
        return number

    for p in pieces:

        @pl.when(z < 3)
        def _():
            send_z(0, dp, True, p).start()

        @pl.when(z > 0)
        def _():
            send_z(1, dp, False, p).start()

        send_y(0, 0, p).start()
        send_core(0, 0, p).start()

    vec_ref[...] = jnp.zeros_like(vec_ref)
    loss_buf[...] = jnp.zeros_like(loss_buf)
    ids_col[...] = jnp.broadcast_to(ids_ref[...], (128, IMAGES * SEQ)).T
    lane = lax.broadcasted_iota(jnp.int32, (IMAGES * SEQ, 128), 1)
    dest = 1 - section

    def pick(place, first=False):
        rel = ids_col[...] - place * rows_here
        low = (rel == lane).astype(F32)
        high = ((rel - 128 == lane) & (lane < rows_here - 128)).astype(F32)
        one_hot = jnp.concatenate([low, high], axis=1)
        vec_ref[pl.ds(place, 1), D:] = column_sum(one_hot)
        one_hot = one_hot[:, :SHARD].astype(BF)
        for i in range(IMAGES):
            for p in pieces:
                rows = matmul_nn(one_hot[i * SEQ : (i + 1) * SEQ], shards[place, p]).astype(BF)
                cols = slice(p * SLICE, (p + 1) * SLICE)
                rows_buf[dest, i, :, cols] = rows if first else rows_buf[dest, i, :, cols] + rows

    def pick_core(e):
        for p in pieces:
            send_core(e, number_at(e), p).wait_recv()
        pick(place_of(number_at(e)) + 1 - 2 * core)

    def event(e, carry):
        number = number_at(e)
        near = (e == 1) | (e == 3) | (e == 5)
        for p in pieces:
            move(place_of(number), p, s_c.at[e], r_in.at[number], across).wait_recv()

            @pl.when(home & near & jnp.logical_not(corner))
            def _():
                pass_on(e, p).start()

            @pl.when(home & near)
            def _():
                send_y((e + 1) // 2, number, p).start()

            @pl.when(home & ((e >= 4) | ((e == 3) & corner)))
            def _():
                send_x(e - 3, number, p).start()

            send_core(e, number, p).start()
        pick(place_of(number))
        pick_core(e - 1)
        return carry

    pick(dp, True)
    lax.fori_loop(1, 8, event, 0)
    pick_core(7)

    for load in loads:
        load.wait()

    @pl.when(section == 0)
    def _():
        patch_load.wait()

    @pl.when(section == 1)
    def _():
        target_load.wait()

    weights = (gains, shifts, w_qkv, w_out, out_bias, w_up, up_bias, w_down, down_bias)
    scale = jnp.where(section == 0, COMMIT_WEIGHT, 1.0)

    def rows_of(ref, image):
        return ref.at[pl.ds(pl.multiple_of(image * SEQ, SEQ), SEQ)]

    def stores(image, forward):
        pairs = ((l_buf, l_ref), (result_buf, result_ref)) if forward else ((d_buf, d_ref), (dh_buf, dh_ref))
        first = 0 if forward else 2
        return [
            pltpu.make_async_copy(src, rows_of(dst, image), out_sem.at[first + i]) for i, (src, dst) in enumerate(pairs)
        ]

    def cross(image):
        return pltpu.make_async_remote_copy(
            crossing.at[image], crossing.at[image], sx.at[image], rx.at[image], device_id=beside, device_id_type=MESH
        )

    trade = pltpu.make_async_remote_copy(loss_buf, loss_side, s_loss, r_loss, device_id=beside, device_id_type=MESH)

    def step(i, carry):
        even = i % 2 == 0
        ahead = jnp.where(section == 1, even, (i == 0) | ((i % 2 == 1) & (i < 7)))

        @pl.when(ahead)
        def _():
            image = (i + 1) // 2
            slot = image % 2

            @pl.when(image > 0)
            def _():
                for copy in stores(image - 1, True):
                    copy.wait()

            forward_image(
                rows_buf.at[0, image], weights, l_buf, qkv.at[slot], pt.at[slot], slope.at[slot], h1.at[slot],
                result.at[slot], result_buf, vt, ot,
            )
            diff = result[slot] - rows_buf[1, image].astype(F32)
            loss_buf[0:1, :] += column_sum(diff * diff * scale)
            for copy in stores(image, True):
                copy.start()

            @pl.when(image == IMAGES - 1)
            def _():
                trade.start()

        @pl.when(jnp.logical_not(ahead))
        def _():
            image = (i - 1) // 2
            slot = image % 2

            @pl.when(image > 0)
            def _():
                for copy in stores(image - 1, False):
                    copy.wait()

            @pl.when(section == 0)
            def _():
                cross(image).wait_recv()

            backward_image(
                scale, section == 0, result.at[slot], rows_buf.at[1, image], crossing.at[image], rows_buf.at[0, image], weights,
                qkv.at[slot], pt.at[slot], slope.at[slot], h1.at[slot], d_buf, vec_ref, dh_buf, crossing.at[image],
                vt, ot,
            )

            @pl.when(section == 1)
            def _():
                cross(image).start()

            for copy in stores(image, False):
                copy.start()

        return carry

    lax.fori_loop(0, 2 * IMAGES, step, 0)
    for forward in (True, False):
        for copy in stores(IMAGES - 1, forward):
            copy.wait()

    @pl.when(section == 1)
    def _():
        for image in range(IMAGES):
            cross(image).wait_send()

    for p in pieces:

        @pl.when(z < 3)
        def _():
            send_z(0, dp, True, p).wait_send()

        @pl.when(z > 0)
        def _():
            send_z(1, dp, False, p).wait_send()

        send_y(0, 0, p).wait_send()

        @pl.when(home)
        def _():
            for order in (1, 2, 3):
                send_y(order, number_at(2 * order - 1), p).wait_send()
            for e in (4, 5, 6, 7):
                send_x(e - 3, number_at(e), p).wait_send()

        @pl.when(home & jnp.logical_not(corner))
        def _():
            for e in (1, 3, 5):
                pass_on(e, p).wait_send()

        @pl.when(home & corner)
        def _():
            send_x(0, number_at(3), p).wait_send()

        for e in range(8):
            send_core(e, number_at(e), p).wait_send()

    trade.wait()
    vec_ref[V_LOSS : V_LOSS + 1, :D] = loss_buf[0:1, :]
    vec_ref[V_SIDE : V_SIDE + 1, :D] = loss_side[0:1, :]


def run_blocks(patches, targets, ids, codebook, weights):
    dma = pltpu.SemaphoreType.DMA
    vm = pltpu.VMEM
    rows = IMAGES * SEQ
    inside, outside = pl.BlockSpec(memory_space=pltpu.VMEM), pl.BlockSpec(memory_space=pl.ANY)
    weight_places = [inside, inside, outside, outside, inside, outside, inside, outside, inside]
    return pl.pallas_call(
        blocks_kernel,
        out_shape=[
            jax.ShapeDtypeStruct((rows, D), BF),
            jax.ShapeDtypeStruct((rows, D), F32),
            jax.ShapeDtypeStruct((rows, L_ALL), BF),
            jax.ShapeDtypeStruct((rows, D_ALL), BF),
            jax.ShapeDtypeStruct((V_ROWS, V_COLS), F32),
        ],
        in_specs=[outside, outside, inside, inside] + weight_places,
        out_specs=[outside] * 4 + [inside],
        scratch_shapes=[
            vm((D, QKV), BF), vm((D, D), BF), vm((D, FF), BF), vm((FF, D), BF),
            vm((16, SLICES, SHARD, SLICE), BF), vm((rows, 128), jnp.int32),
            vm((2, IMAGES, SEQ, D), BF), vm((IMAGES, SEQ, D), BF), vm((8, D), F32), vm((8, D), F32),
            vm((2, SEQ, QKV), BF), vm((2, HEADS, SEQ, SEQ), F32), vm((2, SEQ, FF), F32), vm((2, SEQ, D), F32),
            vm((2, SEQ, D), F32), vm((SEQ, L_ALL), BF), vm((SEQ, D_ALL), BF), vm((SEQ, D), BF), vm((SEQ, D), F32),
            vm((D, SEQ), BF), vm((D, SEQ), BF),
            dma((4,)), dma(()), dma((4,)), dma((8, SLICES)), dma((5, SLICES)),
            dma((4, SLICES)), dma((5, SLICES)), dma((8, SLICES)), dma((8, SLICES)), dma(()), dma(()),
            dma((IMAGES,)), dma((IMAGES,)),
        ],
        compiler_params=pltpu.CompilerParams(collective_id=2, has_side_effects=True, vmem_limit_bytes=VMEM_BYTES),
        name="blocks",
    )(patches.reshape(IMAGES, SEQ, D), targets.reshape(IMAGES, SEQ, D), ids.reshape(1, rows), codebook, *weights)


UNITS = 36
PART = D // 16
COLS = 256
LAG_Y, LAG_Z, HOP = 1, 4, 4
LAG_OUT = LAG_Z + 3 * HOP
BLOCKS = D_ALL // COLS
FIRST_DOWN = 24
EVERY, EARLY = 9, UNITS // 9
LAG_LAST = 3
RING = 20


def reduce_kernel(
    vocab, l_ref, d_ref, vec_from, qkv_out, out_out, up_out, down_out, vec_out, hist_out, stats_out,
    left, right, product, acc_y, acc_z, tx_c, rx_c, tx_y, rx_y, tx_up, rx_up, tx_dn, rx_dn,
    acc_e, tx_eu, rx_eu, tx_ed, rx_ed, tx_l, rx_l, vec_ref, vec_tx, vec_c, vec_y, vec_z,
    lsem, dsem, sc, rc, sy, ry, s_up, r_up, s_dn, r_dn,
    s_eu, r_eu, s_ed, r_ed, s_l, r_l, sv, rv, vec_sem,
):
    sec, dp = lax.axis_index("section"), lax.axis_index("dp")
    core, y, z = dp % 2, (dp // 2) % 2, dp // 4
    across = (sec, dp + 1 - 2 * core)
    along_y = (sec, dp + 2 - 4 * y)
    along_z = [(sec, (z + k) % 4 * 4 + y * 2 + core) for k in (1, 2, 3)]
    above, below = (sec, jnp.minimum(dp + 4, 12 + dp % 4)), (sec, jnp.maximum(dp - 4, dp % 4))

    lefts = [pltpu.make_async_copy(l_ref.at[:, i * D : (i + 1) * D], left.at[i], lsem.at[i]) for i in range(7)]

    def load_right(n):
        cols = pl.ds(pl.multiple_of(n * COLS, COLS), COLS)
        return pltpu.make_async_copy(d_ref.at[:, cols], right.at[n % 2], dsem.at[n % 2])

    vec_load = pltpu.make_async_copy(vec_from, vec_ref, vec_sem)
    lefts[0].start()
    load_right(0).start()
    vec_load.start()

    barrier = pltpu.get_barrier_semaphore()
    for target in [across, along_y] + along_z:
        pl.semaphore_signal(barrier, inc=1, device_id=target, device_id_type=MESH)
    pl.semaphore_wait(barrier, 5)

    def remote(src, dst, send, recv, target):
        return pltpu.make_async_remote_copy(src, dst, send, recv, device_id=target, device_id_type=MESH)

    def send_core(u):
        return remote(tx_c.at[u % 2], rx_c.at[u], sc.at[u % 2], rc.at[u], across)

    def send_y(u):
        return remote(tx_y.at[u % RING], rx_y.at[u], sy.at[u % RING], ry.at[u], along_y)

    def up_link(at, high, tx, rx, send, recv):
        rows = slice(at * high, 3 * high)
        return remote(tx.at[rows], rx.at[rows], send, recv, above)

    def dn_link(at, high, tx, rx, send, recv):
        rows = slice(0, at * high)
        return remote(tx.at[rows], rx.at[rows], send, recv, below)

    def send_last(u):
        return remote(tx_l.at[u], rx_l.at[u], s_l.at[u], r_l.at[u], along_y)

    def is_early(u):
        return u % EVERY == 2

    def valid(u):
        return (u >= 0) & (u < UNITS)

    def climb(high, acc, tx, rx, send, recv):
        for at in range(4):

            @pl.when(z == at)
            def _():
                if at > 0:
                    up_link(at - 1, high, tx, rx, send, recv).wait_recv()
                if at < 3:
                    t = acc[(at + 1) * high : 4 * high]
                    if at > 0:
                        t = t + rx[at * high : 3 * high].astype(F32)
                    tx[at * high : 3 * high] = t.astype(BF)
                    up_link(at, high, tx, rx, send, recv).start()

    def sink(high, acc, tx, rx, send, recv):
        for at in range(4):

            @pl.when(z == at)
            def _():
                if at < 3:
                    dn_link(at + 1, high, tx, rx, send, recv).wait_recv()
                if at > 0:
                    t = acc[: at * high]
                    if at < 3:
                        t = t + rx[: at * high].astype(F32)
                    tx[: at * high] = t.astype(BF)
                    dn_link(at, high, tx, rx, send, recv).start()

    def settle(high, acc, up, dn):
        for at in range(4):

            @pl.when(z == at)
            def _():
                t = acc[at * high : (at + 1) * high]
                if at < 3:
                    up_link(at, high, *up).wait_send()
                    t = t + dn[1][at * high : (at + 1) * high].astype(F32)
                if at > 0:
                    dn_link(at, high, *dn).wait_send()
                    t = t + up[1][(at - 1) * high : at * high].astype(F32)
                acc[at * high : (at + 1) * high] = t

    def up_args(u):
        return tx_up.at[u % RING], rx_up.at[u], s_up.at[u % RING], r_up.at[u]

    def dn_args(u):
        return tx_dn.at[u % RING], rx_dn.at[u], s_dn.at[u % RING], r_dn.at[u]

    def early_up(e):
        return tx_eu.at[e], rx_eu.at[e], s_eu.at[e], r_eu.at[e]

    def early_dn(e):
        return tx_ed.at[e], rx_ed.at[e], s_ed.at[e], r_ed.at[e]

    vec_core = remote(vec_ref, vec_c, sv.at[0], rv.at[0], across)
    vec_along_y = remote(vec_tx, vec_y, sv.at[1], rv.at[1], along_y)
    vec_along_z = [remote(vec_z.at[z], vec_z.at[z], sv.at[2 + k], rv.at[2 + k], along_z[k]) for k in range(3)]

    def multiply(u):
        down = u >= FIRST_DOWN
        n = jnp.where(down, FIRST_DOWN + (u - FIRST_DOWN) // 4, u)
        fresh = jnp.logical_not(down) | (u % 4 == 0)

        @pl.when(fresh & (n + 1 < BLOCKS))
        def _():
            load_right(n + 1).start()

        @pl.when(fresh)
        def _():
            load_right(n).wait()

        @pl.when(u == 1)
        def _():
            for load in lefts[1:]:
                load.start()

        for i, first in enumerate((0, 12, 15, FIRST_DOWN)):

            @pl.when(u == first)
            def _():
                for load in lefts[i : i + 1] if i < 3 else lefts[3:]:
                    load.wait()

        @pl.when(jnp.logical_not(down))
        def _():
            which = jnp.where(u < 12, 0, jnp.where(u < 15, 1, 2))
            product[:D] = matmul_tn(left[which], right[n % 2])

        @pl.when(down & fresh)
        def _():
            for i in range(4):
                product[i * D : (i + 1) * D] = matmul_tn(left[3 + i], right[n % 2])

        def rows_for(place):
            owner = place % 4 * 4 + (y + place // 4 % 2) % 2 * 2 + (core + place // 8) % 2
            row = jnp.where(down, owner * (4 * PART) + u % 4 * PART, owner * PART)
            return product[pl.ds(pl.multiple_of(row, PART), PART), :]

        for place in range(8):
            tx_c[u % 2, place * PART : (place + 1) * PART] = rows_for(8 + place).astype(BF)
        send_core(u).start()
        for place in range(8):
            acc_y[u % 2, place * PART : (place + 1) * PART] = rows_for(place)

    def step(i, carry):
        @pl.when(i < UNITS)
        def _():
            multiply(i)

        @pl.when((i >= LAG_Y) & (i < UNITS + LAG_Y))
        def _():
            u = i - LAG_Y
            send_core(u).wait()

            @pl.when(is_early(u))
            def _():
                t = acc_y[u % 2] + rx_c[u].astype(F32)
                for place in range(8):
                    to = (2 * (place % 4) + place // 4) * PART
                    acc_e[u // EVERY, to : to + PART] = t[place * PART : (place + 1) * PART]

            @pl.when(jnp.logical_not(is_early(u)))
            def _():
                tx_y[u % RING] = (acc_y[u % 2, 4 * PART :] + rx_c[u, 4 * PART :].astype(F32)).astype(BF)
                send_y(u).start()
                acc_z[u % RING] = acc_y[u % 2, : 4 * PART] + rx_c[u, : 4 * PART].astype(F32)

        @pl.when(valid(i - LAG_Z) & jnp.logical_not(is_early(i - LAG_Z)))
        def _():
            u = i - LAG_Z
            send_y(u).wait()
            acc_z[u % RING] = acc_z[u % RING] + rx_y[u].astype(F32)

        u_up = i - LAG_Z - z * HOP

        @pl.when(valid(u_up) & jnp.logical_not(is_early(u_up)))
        def _():
            climb(PART, acc_z.at[u_up % RING], *up_args(u_up))

        @pl.when(valid(u_up) & is_early(u_up))
        def _():
            climb(2 * PART, acc_e.at[u_up // EVERY], *early_up(u_up // EVERY))

        u_dn = i - LAG_Z - (3 - z) * HOP

        @pl.when(valid(u_dn) & jnp.logical_not(is_early(u_dn)))
        def _():
            sink(PART, acc_z.at[u_dn % RING], *dn_args(u_dn))

        @pl.when(valid(u_dn) & is_early(u_dn))
        def _():
            sink(2 * PART, acc_e.at[u_dn // EVERY], *early_dn(u_dn // EVERY))

        def put(u, t):
            def lanes(n):
                return pl.ds(pl.multiple_of(n * COLS, COLS), COLS)

            @pl.when(u < 12)
            def _():
                up_out[:, lanes(u)] = t

            @pl.when((u >= 12) & (u < 15))
            def _():
                out_out[:, lanes(u - 12)] = t

            @pl.when((u >= 15) & (u < FIRST_DOWN))
            def _():
                qkv_out[:, lanes(u - 15)] = t

            @pl.when(u >= FIRST_DOWN)
            def _():
                rows = pl.ds(pl.multiple_of(u % 4 * PART, PART), PART)
                down_out[rows, lanes((u - FIRST_DOWN) // 4)] = t

        @pl.when(valid(i - LAG_OUT) & is_early(i - LAG_OUT))
        def _():
            e = (i - LAG_OUT) // EVERY
            settle(2 * PART, acc_e.at[e], early_up(e), early_dn(e))
            rows = pl.ds(pl.multiple_of((2 * z + 1) * PART, PART), PART)
            tx_l[e] = acc_e[e, rows, :].astype(BF)
            send_last(e).start()

        @pl.when(valid(i - LAG_OUT - LAG_LAST) & is_early(i - LAG_OUT - LAG_LAST))
        def _():
            u = i - LAG_OUT - LAG_LAST
            e = u // EVERY
            send_last(e).wait()
            rows = pl.ds(pl.multiple_of(2 * z * PART, PART), PART)
            put(u, acc_e[e, rows, :] + rx_l[e].astype(F32))

        @pl.when(valid(i - LAG_OUT) & jnp.logical_not(is_early(i - LAG_OUT)))
        def _():
            u = i - LAG_OUT
            settle(PART, acc_z.at[u % RING], up_args(u), dn_args(u))
            put(u, acc_z[u % RING, pl.ds(pl.multiple_of(z * PART, PART), PART), :])

        @pl.when(i == 1)
        def _():
            vec_load.wait()
            vec_core.start()

        @pl.when(i == 4)
        def _():
            vec_core.wait()
            vec_tx[...] = vec_ref[...] + vec_c[...]
            vec_along_y.start()

        @pl.when(i == 8)
        def _():
            vec_along_y.wait()
            vec_z[z] = vec_tx[...] + vec_y[...]
            for copy in vec_along_z:
                copy.start()

        @pl.when(i == 14)
        def _():
            for copy in vec_along_z:
                copy.wait()
            vec_out[...] = (vec_z[0] + vec_z[1]) + (vec_z[2] + vec_z[3])

        return carry

    lax.fori_loop(0, UNITS + LAG_OUT, step, 0)

    def total(value):
        return jnp.sum(jnp.sum(value, axis=1, keepdims=True), axis=0, keepdims=True)

    tokens = 16 * l_ref.shape[0]
    counts = vec_out[:, D:]
    shares = counts * (1.0 / tokens)
    entropy = -total(shares * jnp.log(jnp.where(counts > 0, shares, 1.0)))
    used = total((counts > 0).astype(F32))
    loss = total(vec_out[V_LOSS : V_LOSS + 1, :D]) + total(vec_out[V_SIDE : V_SIDE + 1, :D])
    lane = lax.broadcasted_iota(jnp.int32, (8, 128), 1)
    last = jnp.where(lane == 1, used / vocab, jnp.exp(entropy) / vocab)
    stats_out[...] = jnp.where(lane == 0, loss / (tokens * D), last)
    hist_out[...] = vec_out[pl.ds(dp, 1), D:].astype(jnp.int32)


def reduce_weights(l, d, vec, vocab):
    dma = pltpu.SemaphoreType.DMA
    vm = pltpu.VMEM
    rows = l.shape[0]
    sums = (V_ROWS, V_COLS)
    return pl.pallas_call(
        functools.partial(reduce_kernel, vocab),
        out_shape=[
            jax.ShapeDtypeStruct((PART, QKV), F32),
            jax.ShapeDtypeStruct((PART, D), F32),
            jax.ShapeDtypeStruct((PART, FF), F32),
            jax.ShapeDtypeStruct((4 * PART, D), F32),
            jax.ShapeDtypeStruct(sums, F32),
            jax.ShapeDtypeStruct((1, V_COLS - D), jnp.int32),
            jax.ShapeDtypeStruct((8, 128), F32),
        ],
        in_specs=[pl.BlockSpec(memory_space=pl.ANY)] * 3,
        out_specs=[pl.BlockSpec(memory_space=pltpu.VMEM)] * 7,
        scratch_shapes=[
            vm((7, rows, D), BF), vm((2, rows, COLS), BF), vm((4 * D, COLS), F32),
            vm((2, 8 * PART, COLS), F32), vm((RING, 4 * PART, COLS), F32),
            vm((2, 8 * PART, COLS), BF), vm((UNITS, 8 * PART, COLS), BF),
            vm((RING, 4 * PART, COLS), BF), vm((UNITS, 4 * PART, COLS), BF),
            vm((RING, 3 * PART, COLS), BF), vm((UNITS, 3 * PART, COLS), BF),
            vm((RING, 3 * PART, COLS), BF), vm((UNITS, 3 * PART, COLS), BF),
            vm((EARLY, 8 * PART, COLS), F32), vm((EARLY, 6 * PART, COLS), BF), vm((EARLY, 6 * PART, COLS), BF),
            vm((EARLY, 6 * PART, COLS), BF), vm((EARLY, 6 * PART, COLS), BF),
            vm((EARLY, PART, COLS), BF), vm((EARLY, PART, COLS), BF),
            vm(sums, F32), vm(sums, F32), vm(sums, F32), vm(sums, F32), vm((4,) + sums, F32),
            dma((7,)), dma((2,)), dma((2,)), dma((UNITS,)), dma((RING,)), dma((UNITS,)),
            dma((RING,)), dma((UNITS,)), dma((RING,)), dma((UNITS,)),
            dma((EARLY,)), dma((EARLY,)), dma((EARLY,)), dma((EARLY,)), dma((EARLY,)), dma((EARLY,)),
            dma((5,)), dma((5,)), dma(()),
        ],
        compiler_params=pltpu.CompilerParams(collective_id=1, has_side_effects=True, vmem_limit_bytes=REDUCE_BYTES),
        name="weight_grad_reduce",
    )(l, d, vec)


def finish(result, dh, g_qkv, g_out, g_up, g_down, vec, hist, stats, shard):
    rows = result.shape[0]
    pieces = 1

    def body(result_ref, dh_ref, qkv_ref, out_ref, up_ref, down_ref, vec_ref, hist_ref, stats_ref,
             result_to, dh_to, gains_to, shifts_to, qkv_to, out_to, out_bias_to, up_to, up_bias_to, down_to, down_bias_to, hist_to, stats_to, *scratch):
        (outof,) = scratch
        copies = []
        for src, dst in ((dh_ref, dh_to), (result_ref, result_to)):
            for i in range(pieces):
                part = pl.ds(i * rows // pieces, rows // pieces)
                copies.append((src.at[part], dst.at[0, part]))
        copies += [(qkv_ref, qkv_to.at[0]), (out_ref, out_to.at[0]), (up_ref, up_to.at[0]), (down_ref, down_to.at[0])]
        saves = [pltpu.make_async_copy(src, dst, outof.at[i]) for i, (src, dst) in enumerate(copies)]
        for save in saves:
            save.start()
        gains_to[0] = vec_ref[0:2, :D]
        shifts_to[0] = vec_ref[2:4, :D]
        out_bias_to[...] = vec_ref[4:5, :D]
        for j in range(FF // D):
            up_bias_to[:, j * D : (j + 1) * D] = vec_ref[5 + j : 6 + j, :D]
        down_bias_to[...] = vec_ref[9:10, :D]
        hist_to[...] = hist_ref[0, :shard]
        stats_to[...] = stats_ref[0, :3]
        for save in saves:
            save.wait()

    inside, outside = pl.BlockSpec(memory_space=pltpu.VMEM), pl.BlockSpec(memory_space=pl.ANY)

    def shape(*dims, dtype=F32):
        return jax.ShapeDtypeStruct((1,) + dims, dtype)

    out = pl.pallas_call(
        body,
        out_shape=[
            shape(rows, D, dtype=BF), shape(rows, D), shape(2, D), shape(2, D), shape(PART, QKV), shape(PART, D),
            shape(D), shape(PART, FF), shape(FF), shape(4 * PART, D), shape(D),
            jax.ShapeDtypeStruct((shard,), jnp.int32), jax.ShapeDtypeStruct((3,), F32),
        ],
        in_specs=[outside] * 6 + [inside] * 3,
        out_specs=[outside, outside, inside, inside, outside, outside, inside, outside, inside, outside, inside, inside, inside],
        scratch_shapes=[
            pltpu.SemaphoreType.DMA((2 * pieces + 4,)),
        ],
        compiler_params=pltpu.CompilerParams(vmem_limit_bytes=PLACE_BYTES),
        name="place_outputs",
    )(result, dh, g_qkv, g_out, g_up, g_down, vec, hist, stats)
    return tuple(out)


def count_shares(counts, total_count):
    shares = counts / total_count
    nonzero_share = jnp.where(counts > 0, shares, 1.0)
    return -jnp.sum(shares * jnp.log(nonzero_share)), jnp.sum((counts > 0).astype(F32))


def on_device(
    patches, targets, code_ids, codebook, norm_gains, norm_shifts, w_qkv, w_out, out_bias, w_up, up_bias, w_down, down_bias
):
    section = lax.axis_index("section")
    leading = section == 0
    dp_size = lax.axis_size("dp")
    dp = lax.axis_index("dp")
    weights = (
        norm_gains[0], norm_shifts[0], w_qkv[0], w_out[0], out_bias, w_up[0], up_bias, w_down[0], down_bias
    )
    rows, width = patches.shape
    images = rows // SEQ
    vocab_local = codebook.shape[0]
    vocab_all = vocab_local * dp_size
    total_tokens = rows * dp_size

    small = dp_size == 16 and vocab_local <= SHARD and rows == IMAGES * SEQ
    if small:
        result_bf, dh, l, d, vec = run_blocks(patches, targets, code_ids, codebook, weights)
        g_qkv, g_out, g_up, g_down, vec, hist, stats = reduce_weights(l, d, vec, vocab_all)
        return finish(result_bf, dh, g_qkv, g_out, g_up, g_down, vec, hist, stats, vocab_local)
    else:
        shard_rows = lax.all_gather(codebook, "dp", axis=0, tiled=True)
        chosen = jnp.take(shard_rows, jnp.clip(code_ids, 0, vocab_all - 1), axis=0)
        x = jnp.where(leading, patches, chosen)
        l, qkv, pt, slope, h1, result, result_bf = block_forward(x, weights)
        other = jnp.where(leading, chosen, targets)
        d = dh = None
        vec = jnp.zeros((V_ROWS, V_COLS), F32)
        arrived = jnp.zeros((SEQ, D), BF)
        for moment in range(images + 1):
            which = jnp.clip(moment - 1 + section, 0, images - 1).astype(jnp.int32)[None]
            active = jnp.where(leading, moment >= 1, moment < images).astype(F32)
            flags = jnp.stack(
                [jnp.where(leading, COMMIT_WEIGHT, 1.0).astype(F32), active, jnp.where(leading, 1.0, 0.0).astype(F32)]
            )
            d, dh, vec, outgoing = block_backward(
                which, flags, result, other, arrived, x, weights, qkv, pt, slope, h1, vec, d, dh
            )
            if moment < images:
                arrived = lax.ppermute(outgoing, "section", [(1, 0)])
        pairs = (
            (l[:, L_A:L_M], d[:, D_QKV:D_GB]),
            (l[:, L_O:L_A], d[:, D_GH:D_QKV]),
            (l[:, :L_O], d[:, :D_GH]),
            (l[:, L_M:], d[:, D_GB:]),
        )
        g_qkv, g_out, g_up, g_down = (
            lax.psum_scatter(matmul_tn(left, right), "dp", scatter_dimension=0, tiled=True) for left, right in pairs
        )
        vocab_iota = lax.broadcasted_iota(jnp.int32, (1, vocab_all), 1)
        counts = jnp.sum((code_ids[:, None] == vocab_iota).astype(F32), axis=0)
        hist_local = lax.psum_scatter(counts, "dp", scatter_dimension=0, tiled=True)
        entropy_part, used_part = count_shares(hist_local, total_tokens)
        hist_local = hist_local.astype(jnp.int32)
        vec = lax.psum(vec, "dp")
        entropy_all, used_all = lax.psum((entropy_part, used_part), "dp")
        loss_all = lax.psum(jnp.sum(vec[V_LOSS, :D]), "section")
        stats = jnp.stack(
            [loss_all / (total_tokens * width), used_all / vocab_all, jnp.exp(entropy_all) / vocab_all]
        )
    return (
        result_bf[None],
        dh[None],
        vec[None, 0:2, :D],
        vec[None, 2:4, :D],
        g_qkv[None],
        g_out[None],
        vec[None, 4, :D],
        g_up[None],
        vec[5:9, :D].reshape(1, FF),
        g_down[None],
        vec[None, 9, :D],
        hist_local,
        stats,
    )


def solution(mesh):
    return jax.shard_map(
        on_device,
        mesh=mesh,
        in_specs=(
            P("dp", None),
            P("dp", None),
            P("dp"),
            P("dp", None),
            P("section", None, None),
            P("section", None, None),
            P("section", None, None),
            P("section", None, None),
            P("section", None),
            P("section", None, None),
            P("section", None),
            P("section", None, None),
            P("section", None),
        ),
        out_specs=(
            P("section", "dp", None),
            P("section", "dp", None),
            P("section", None, None),
            P("section", None, None),
            P("section", "dp", None),
            P("section", "dp", None),
            P("section", None),
            P("section", "dp", None),
            P("section", None),
            P("section", "dp", None),
            P("section", None),
            P("dp"),
            P(),
        ),
        check_vma=False,
    )
```
